512 devices in a mesh: batch: 8 (over x, y_hi), px: 4 (over y_lo), py: 16 (over z, core).
Axes of the slice: x: 4, y: 8 (y_hi: 2, y_lo: 4; y = y_hi * 4 + y_lo), z: 8, core: 2. Of those that a mesh axis runs over, the one named last changes fastest.
Arguments:
- field: bfloat16 [8, 16, 128, 128, 128], P('batch', None, 'px', 'py'), may hold values from -6 to 6
- cotangent: bfloat16 [8, 16, 128, 128, 128], P('batch', None, 'px', 'py'), may hold values from -6 to 6
- spec_weight: float32 [2, 16, 16, 16, 16, 16], P(None, None, None, 'py', 'px'), may hold values from -15 to 15
- skip_weight: bfloat16 [16, 16], replicated, may hold values from -1.5 to 1.5
- skip_bias: float32 [16], replicated, may hold values from -1 to 1
- mlp_in: bfloat16 [16, 16], replicated, may hold values from -1.5 to 1.5
- mlp_out: bfloat16 [16, 16], replicated, may hold values from -1.5 to 1.5
Outputs:
- grad_input: bfloat16 [8, 16, 128, 128, 128], P('batch', None, 'px', 'py')
- grad_spectral: float32 [2, 16, 16, 16, 16, 16], P(None, None, None, 'py', 'px', 'batch')
- grad_skip: float32 [16, 16], replicated
- grad_bias: float32 [16], replicated
- grad_mlp_in: float32 [16, 16], replicated
- grad_mlp_out: float32 [16, 16], replicated
The draws below stay inside these ranges and needn't reach their ends.
All inputs are finite; a program needn't handle non-finite values.
Results may differ from the reference program's by a relative error of at most 0.014.
Values sent between devices are 32-bit elements; how exact they have to be, the bound alone decides.
No kernel may reach another device: no remote copies, remote signals or barrier semaphores. Data moves between devices by JAX's collectives and lax.ppermute only.
A program may use at most 128 MiB of HBM per device.

```python
import math
import jax
import jax.numpy as jnp
from jax import lax

C = 16
HM = 16
NX = 128
NY = 128
NZ = 128
MX = 16
MY = 16
MZ = 16
BATCH = 8


def levels(rng, extent, pieces, least, high):
    factor_of = 1.0
    for dim, parts in pieces:
        steps = jax.random.uniform(jax.random.fold_in(jax.random.fold_in(rng, 6), dim), (parts,), jnp.float32, least / len(pieces), high / len(pieces))
        factor_of = factor_of * jnp.repeat(jnp.exp(steps), extent[dim] // parts).reshape((-1,) + (1,) * (len(extent) - 1 - dim))
    return factor_of


def scatter_about(key, shape, spread, reach, shards=(), held_as=jnp.bfloat16):
    drawn = jax.random.normal(key, shape, jnp.float32) * spread
    if len(shards) > 0:
        drawn = levels(key, shape, shards, -0.22, 0.18) * drawn
    return jnp.clip(drawn, min=-reach, max=reach).astype(held_as)


def setup_inputs(seed: int = 0) -> dict:
    seeds = jax.random.split(jax.random.key(seed), 8)
    field = scatter_about(seeds[0], (BATCH, C, NX, NY, NZ), 1.0, 6.0, ((0, 8), (2, 4), (3, 16)))
    cotangent = scatter_about(seeds[1], (BATCH, C, NX, NY, NZ), 1.0, 6.0, ((0, 8), (2, 4), (3, 16)))
    spec_weight = scatter_about(seeds[2], (2, C, C, MZ, MY, MX), 3.0, 15.0, ((3, 16), (4, 4)), jnp.float32)
    skip_weight = scatter_about(seeds[3], (C, C), C ** -0.5, 1.5)
    skip_bias = jnp.clip(jax.random.uniform(seeds[4], (C,), jnp.float32, -1.0, 1.0), -1.0, 1.0)
    mlp_in = scatter_about(seeds[5], (HM, C), C ** -0.5, 1.5)
    mlp_out = scatter_about(seeds[6], (C, HM), HM ** -0.5, 1.5)
    return dict(field=field, cotangent=cotangent, spec_weight=spec_weight, skip_weight=skip_weight, skip_bias=skip_bias, mlp_in=mlp_in, mlp_out=mlp_out)


precise = lax.Precision.HIGHEST

def signed(indices, total_modes):
    return jnp.where(indices < total_modes // 2, indices, indices - total_modes)

def phases(frequency, positions, length):
    residue = frequency[:, None] * positions[None, :] % length
    angles = residue.astype(jnp.float32) * (2.0 * math.pi / length)
    return (jnp.cos(angles), jnp.sin(angles))

def product(pattern, left_operand, right_operand):
    return jnp.einsum(pattern, left_operand.astype(jnp.float32), right_operand.astype(jnp.float32), precision=precise)

def reference(field, cotangent, spec_weight, skip_weight, skip_bias, mlp_in, mlp_out):
    norm_scale = 1.0 / math.sqrt(NX * NY * NZ)
    depth_cosine, depth_sine = phases(jnp.arange(MZ, dtype=jnp.int32), jnp.arange(NZ, dtype=jnp.int32), NZ)
    second_cosine, second_sine = phases(signed(jnp.arange(MY, dtype=jnp.int32), MY), jnp.arange(NY, dtype=jnp.int32), NY)
    first_cosine, first_sine = phases(signed(jnp.arange(MX, dtype=jnp.int32), MX), jnp.arange(NX, dtype=jnp.int32), NX)
    depth_cosine_low = lax.optimization_barrier(depth_cosine.astype(jnp.bfloat16)).astype(jnp.float32)
    depth_sine_low = lax.optimization_barrier(depth_sine.astype(jnp.bfloat16)).astype(jnp.float32)
    weight_real = spec_weight[0].astype(jnp.float32)
    weight_imaginary = spec_weight[1].astype(jnp.float32)

    def forward(values):
        depth_real = product('cxyz,kz->cxyk', values, depth_cosine_low)
        depth_imaginary = -product('cxyz,kz->cxyk', values, depth_sine_low)
        second_real = product('cxyk,my->cxmk', depth_real, second_cosine) + product('cxyk,my->cxmk', depth_imaginary, second_sine)
        second_imaginary = product('cxyk,my->cxmk', depth_imaginary, second_cosine) - product('cxyk,my->cxmk', depth_real, second_sine)
        first_real = product('cxmk,jx->ckmj', second_real, first_cosine) + product('cxmk,jx->ckmj', second_imaginary, first_sine)
        first_imaginary = product('cxmk,jx->ckmj', second_imaginary, first_cosine) - product('cxmk,jx->ckmj', second_real, first_sine)
        return (first_real * norm_scale, first_imaginary * norm_scale)

    def inverse(spectra_real, spectra_imaginary):
        first_real = product('ckmj,jx->ckmx', spectra_real, first_cosine) - product('ckmj,jx->ckmx', spectra_imaginary, first_sine)
        first_imaginary = product('ckmj,jx->ckmx', spectra_imaginary, first_cosine) + product('ckmj,jx->ckmx', spectra_real, first_sine)
        second_real = product('ckmx,my->ckxy', first_real, second_cosine) - product('ckmx,my->ckxy', first_imaginary, second_sine)
        second_imaginary = product('ckmx,my->ckxy', first_imaginary, second_cosine) + product('ckmx,my->ckxy', first_real, second_sine)
        synthesis = product('ckxy,kz->cxyz', second_real, depth_cosine) - product('ckxy,kz->cxyz', second_imaginary, depth_sine)
        return synthesis * norm_scale

    def per_sample(sample_pair):
        values, upstream = sample_pair
        input_real, input_imaginary = forward(values)
        mixed_real = product('ckmj,cokmj->okmj', input_real, weight_real) - product('ckmj,cokmj->okmj', input_imaginary, weight_imaginary)
        mixed_imaginary = product('ckmj,cokmj->okmj', input_imaginary, weight_real) + product('ckmj,cokmj->okmj', input_real, weight_imaginary)
        preact = inverse(mixed_real, mixed_imaginary) + product('oc,cxyz->oxyz', skip_weight, values) + skip_bias.astype(jnp.float32)[:, None, None, None]
        hidden = jax.nn.gelu(preact).astype(jnp.bfloat16)
        inner_sum = product('hc,cxyz->hxyz', mlp_in, hidden)
        activated = jax.nn.gelu(inner_sum).astype(jnp.bfloat16)
        d_activated = product('ch,cxyz->hxyz', mlp_out, upstream)
        inner_back = jax.vjp(jax.nn.gelu, inner_sum)[1]
        d_inner = inner_back(d_activated)[0].astype(jnp.bfloat16)
        d_hidden = product('hc,hxyz->cxyz', mlp_in, d_inner)
        preact_back = jax.vjp(jax.nn.gelu, preact)[1]
        d_preact = preact_back(d_hidden)[0].astype(jnp.bfloat16)
        grad_real, grad_imaginary = forward(d_preact)
        back_real = product('okmj,cokmj->ckmj', grad_real, weight_real) + product('okmj,cokmj->ckmj', grad_imaginary, weight_imaginary)
        back_imaginary = product('okmj,cokmj->ckmj', grad_imaginary, weight_real) - product('okmj,cokmj->ckmj', grad_real, weight_imaginary)
        input_grad = (product('oc,oxyz->cxyz', skip_weight, d_preact) + inverse(back_real, back_imaginary)).astype(jnp.bfloat16)
        spectral_real = product('ckmj,okmj->cokmj', input_real, grad_real) + product('ckmj,okmj->cokmj', input_imaginary, grad_imaginary)
        spectral_imaginary = product('ckmj,okmj->cokmj', input_real, grad_imaginary) - product('ckmj,okmj->cokmj', input_imaginary, grad_real)
        skip_grad = product('oxyz,cxyz->oc', d_preact, values)
        bias_grad = lax.optimization_barrier(jnp.sum(d_preact.astype(jnp.float32), axis=(1, 2, 3)))
        inner_grad = product('hxyz,cxyz->hc', d_inner, hidden)
        outer_grad = product('cxyz,hxyz->ch', upstream, activated)
        return (input_grad, jnp.stack([spectral_real, spectral_imaginary]), skip_grad, bias_grad, inner_grad, outer_grad)
    results = lax.map(per_sample, (field, cotangent))
    grad_scale = 1.0 / math.sqrt(BATCH * NX * NY * NZ)
    return (results[0], lax.optimization_barrier(jnp.sum(results[1], axis=0)), lax.optimization_barrier(jnp.sum(results[2], axis=0)) * grad_scale, lax.optimization_barrier(jnp.sum(results[3], axis=0)) * grad_scale, lax.optimization_barrier(jnp.sum(results[4], axis=0)) * grad_scale, lax.optimization_barrier(jnp.sum(results[5], axis=0)) * grad_scale)
```

```python
import math

import jax
import jax.numpy as jnp
import ml_dtypes
import numpy as np
from jax import lax
from jax.experimental import pallas as pl
from jax.experimental.pallas import tpu as pltpu
from jax.sharding import PartitionSpec as P

f32 = jnp.float32
bf16 = jnp.bfloat16
C = 16
N = 128
PX, PY, NB = 4, 16, 8
XL, YL = N // PX, N // PY
XY = XL * YL
ML = C // PX
PEERS = PX * PY
LANES = 128
SIGMA = 1.0 / math.sqrt(N**3)
RHO = 1.0 / math.sqrt(NB * N**3)
NT = (((1,), (1,)), ((), ()))


def tables():
    turn = lambda r, n: 2.0 * np.pi * (np.mod(r, n) / n)
    freq = np.where(np.arange(C) < C // 2, np.arange(C), np.arange(C) - C)
    depth = turn(np.arange(C)[:, None] * np.arange(N)[None, :], N)
    cos_z, sin_z = np.cos(depth), np.sin(depth)
    low = np.concatenate([cos_z, -sin_z]).astype(ml_dtypes.bfloat16)
    ax = turn(np.arange(XL)[:, None] * freq[None, :], N)
    ay = turn(np.arange(YL)[:, None] * freq[None, :], N)
    phase = ax[:, None, None, :] + ay[None, :, :, None]
    phase = phase.reshape(XY, PX, ML * C)
    co, si = np.cos(phase), np.sin(phase)
    upper = np.stack([co, -si], axis=2)
    lower = np.stack([si, co], axis=2)
    plane = np.concatenate([upper, lower]).reshape(2 * XY, PX * 2 * ML * C)
    plane_hi = plane.astype(ml_dtypes.bfloat16)
    plane_lo = (plane - plane_hi.astype(np.float64)).astype(ml_dtypes.bfloat16)
    ox = turn(np.arange(PX)[:, None] * XL * freq[None, :], N)
    oy = turn(np.arange(PY)[:, None] * YL * freq[None, :], N)
    off = ox[:, None, None, :] + oy[None, :, :, None]
    off = off.reshape(PEERS, PX, ML * C)
    cs = np.concatenate([np.cos(off), np.cos(off)], axis=2)
    sn = np.concatenate([np.sin(off), -np.sin(off)], axis=2)
    offset = (np.concatenate([cs, sn], axis=1) * SIGMA).astype(np.float32)
    eye = np.eye(8)
    synth = np.concatenate(
        [
            np.einsum("ab,kz->akbz", eye, cos_z).reshape(8 * C, 8 * N),
            np.einsum("ab,kz->akbz", eye, -sin_z).reshape(8 * C, 8 * N),
        ]
    ).astype(ml_dtypes.bfloat16)
    return low, plane_hi, plane_lo, offset, synth


def dot(a, b):
    return jnp.dot(a, b, preferred_element_type=f32)


def dot_nt(a, b):
    return lax.dot_general(a, b, NT, preferred_element_type=f32)


def split(a):
    hi = a.astype(bf16)
    return hi, (a - hi.astype(f32)).astype(bf16)


def my_offset(offset_ref):
    me = lax.axis_index("px") * PY + lax.axis_index("py")
    return offset_ref[me]


def forward_part(get, low_ref, hi_ref, lo_ref, offset_ref, turn_ref, out_ref):
    low = low_ref[...]
    rows = []
    for c in range(C):
        z = dot_nt(low, get(c))
        rows.append(jnp.concatenate([z[:C], z[C:]], axis=1))
    x_hi, x_lo = split(jnp.concatenate(rows, axis=0))
    off = my_offset(offset_ref)
    for mb in range(PX):
        cols = slice(mb * LANES, (mb + 1) * LANES)
        hi = hi_ref[:, cols]
        part = dot(x_hi, hi) + dot(x_lo, hi) + dot(x_hi, lo_ref[:, cols])
        turned = part * off[mb] + pltpu.roll(part, LANES // 2, 1) * off[PX + mb]
        turn_ref[mb] = turned
    for mb in range(PX):
        for k in range(C):
            out_ref[mb * PY + k, 0:C, :] = turn_ref[mb, pl.ds(k, C, stride=C), :]


def inverse_part(recv_ref, hi_ref, lo_ref, offset_ref, synth_ref, turn_ref, g_ref):
    off = my_offset(offset_ref)
    for mb in range(PX):
        v = recv_ref[mb * PY : (mb + 1) * PY].reshape(PY * C, LANES)
        turn_ref[mb] = v * off[mb] - pltpu.roll(v, LANES // 2, 1) * off[PX + mb]
    rows = []
    for o in range(C):
        rows.append(
            jnp.concatenate(
                [turn_ref[mb, pl.ds(o, C, stride=C), :] for mb in range(PX)], axis=1
            )
        )
    v_hi, v_lo = split(jnp.concatenate(rows, axis=0))
    hi = hi_ref[...]
    z = dot_nt(hi, v_hi) + dot_nt(hi, v_lo) + dot_nt(lo_ref[...], v_hi)
    z = z.astype(bf16)
    for ob in range(2):
        cols = slice(ob * LANES, (ob + 1) * LANES)
        zb = jnp.concatenate([z[:XY, cols], z[XY:, cols]], axis=1)
        g = dot(zb, synth_ref[...])
        for o in range(8):
            g_ref[ob * 8 + o] = g[:, o * N : (o + 1) * N]


def k_forward(field_ref, low_ref, hi_ref, lo_ref, offset_ref, out_ref, turn_ref):
    forward_part(
        lambda c: field_ref[c], low_ref, hi_ref, lo_ref, offset_ref, turn_ref, out_ref
    )


def k_mix(recv_ref, wa_ref, wb_ref, u_ref, out_ref):
    u = jnp.sum(recv_ref[...], axis=0)
    us = pltpu.roll(u, LANES // 2, 1)
    u_ref[...] = u
    v = jnp.zeros((C, LANES), f32)
    for c in range(C):
        v = v + wa_ref[c] * u[c : c + 1, :] + wb_ref[c] * us[c : c + 1, :]
    out_ref[...] = jnp.broadcast_to(v[None], (PEERS, C, LANES))


def gelu_parts(x):
    a = math.sqrt(2.0 / math.pi)
    b = a * 0.044715
    x2 = x * x
    h = 0.5 * jnp.tanh(x * (a + b * x2)) + 0.5
    g = x * h
    d = h + g * (1.0 - h) * (2.0 * a + (6.0 * b) * x2)
    return g, d


def tile(ref, p):
    left = ref[:, pl.ds(p * 32, 16), :].reshape(C * 16, N)
    right = ref[:, pl.ds(p * 32 + 16, 16), :].reshape(C * 16, N)
    return jnp.concatenate([left, right], axis=1)


def untile(ref, p, value):
    ref[:, pl.ds(p * 32, 16), :] = value[:, :N].reshape(C, 16, N)
    ref[:, pl.ds(p * 32 + 16, 16), :] = value[:, N:].reshape(C, 16, N)


def pack_rows(acc):
    r = lax.broadcasted_iota(jnp.int32, (256, 256), 0)
    l = lax.broadcasted_iota(jnp.int32, (256, 256), 1)
    kept = jnp.where(r % 16 == l % 16, acc, 0.0).reshape(C, 16, 256).sum(axis=1)
    r = lax.broadcasted_iota(jnp.int32, (256, LANES), 0)
    l = lax.broadcasted_iota(jnp.int32, (256, LANES), 1)
    pick = jnp.where(r // 16 == l % 16, 1.0, 0.0)
    spread = jnp.dot(kept, pick, precision=lax.Precision.HIGHEST, preferred_element_type=f32)
    r = lax.broadcasted_iota(jnp.int32, (C, LANES), 0)
    l = lax.broadcasted_iota(jnp.int32, (C, LANES), 1)
    spread = jnp.where(r % 8 == l // 16, spread, 0.0)
    return spread.reshape(2, 8, LANES).sum(axis=1)


def k_middle(
    recv_ref, field_ref, cot_ref, kron_ref, bias_ref, low_ref, hi_ref, lo_ref, offset_ref, synth_ref,
    out_ref, dpre_ref,
    turn_ref, g_ref, skip_acc, bias_acc, in_acc, out_acc,
):
    inverse_part(recv_ref, hi_ref, lo_ref, offset_ref, synth_ref, turn_ref, g_ref)
    skip_acc[...] = jnp.zeros_like(skip_acc)
    in_acc[...] = jnp.zeros_like(in_acc)
    out_acc[...] = jnp.zeros_like(out_acc)
    bias_acc[...] = jnp.zeros_like(bias_acc)

    def step(p, carry):
        f = tile(field_ref, p)
        cot = tile(cot_ref, p)
        pre = tile(g_ref, p) + dot(kron_ref[0], f) + bias_ref[...]
        hid, d_hid = gelu_parts(pre)
        hid = hid.astype(bf16)
        act, d_act = gelu_parts(dot(kron_ref[1], hid))
        act = act.astype(bf16)
        d_inner = (dot(kron_ref[2], cot) * d_act).astype(bf16)
        dpre = dot(kron_ref[3], d_inner) * d_hid
        dpre = dpre.astype(bf16)
        untile(dpre_ref, p, dpre)
        skip_acc[...] += dot_nt(dpre, f)
        in_acc[...] += dot_nt(d_inner, hid)
        out_acc[...] += dot_nt(cot, act)
        bias_acc[...] += dpre.astype(f32)
        return carry

    lax.fori_loop(0, XY // 32, step, 0)
    forward_part(
        lambda c: dpre_ref[c], low_ref, hi_ref, lo_ref, offset_ref, turn_ref, out_ref
    )
    bias = bias_acc[...].reshape(C, 16, 256).sum(axis=1)
    total = jnp.sum(bias, axis=1, keepdims=True)
    r = lax.broadcasted_iota(jnp.int32, (C, LANES), 0)
    l = lax.broadcasted_iota(jnp.int32, (C, LANES), 1)
    bias_row = jnp.sum(jnp.where(r == l, total, 0.0), axis=0, keepdims=True)
    small = jnp.concatenate(
        [pack_rows(skip_acc[...]), pack_rows(in_acc[...]), pack_rows(out_acc[...]),
         bias_row, jnp.zeros((1, LANES), f32)], axis=0
    )
    out_ref[:, C : C + 8, :] = jnp.broadcast_to(small[None], (PEERS, 8, LANES))


def k_mix_back(recv_ref, u_ref, wa_ref, wb_ref, out_ref, share_ref):
    got = jnp.sum(recv_ref[...], axis=0)
    g = got[:C]
    gs = pltpu.roll(g, LANES // 2, 1)
    rows = []
    for c in range(C):
        rows.append(jnp.sum(wa_ref[c] * g - wb_ref[c] * gs, axis=0, keepdims=True))
    du = jnp.concatenate(rows, axis=0)
    out_ref[...] = jnp.broadcast_to(du[None], (PEERS, C, LANES))
    share = jnp.concatenate([u_ref[...], got], axis=0)
    share_ref[...] = jnp.broadcast_to(share[None], (NB, 2 * C + 8, LANES))


def k_input(recv_ref, dpre_ref, kron_ref, hi_ref, lo_ref, offset_ref, synth_ref, out_ref, turn_ref, g_ref):
    inverse_part(recv_ref, hi_ref, lo_ref, offset_ref, synth_ref, turn_ref, g_ref)

    def step(p, carry):
        untile(out_ref, p, (dot(kron_ref[4], tile(dpre_ref, p)) + tile(g_ref, p)).astype(bf16))
        return carry

    lax.fori_loop(0, XY // 32, step, 0)


def k_shared(recv_ref, spec_ref, skip_ref, bias_ref, in_ref, outer_ref, pa_ref, pb_ref):
    for c in range(C):
        pa = jnp.zeros((C, LANES), f32)
        pb = jnp.zeros((C, LANES), f32)
        for s in range(NB):
            u = recv_ref[s, c : c + 1, :]
            g = recv_ref[s, C : 2 * C, :]
            pa = pa + u * g
            pb = pb + u * pltpu.roll(g, LANES // 2, 1)
        pa_ref[c * C : (c + 1) * C, :] = pa
        pb_ref[c * C : (c + 1) * C, :] = pb
    b = lax.axis_index("batch")
    r = lax.broadcasted_iota(jnp.int32, (8, LANES), 0)
    l = lax.broadcasted_iota(jnp.int32, (8, LANES), 1)
    mine = ((l % 64) // C == r // 2) & (l % C == 2 * b + r % 2)
    sel_a = jnp.where(mine, 1.0, 0.0)
    sel_b = jnp.where(l < 64, sel_a, -sel_a)
    full = lambda x, y: lax.dot_general(
        x, y, NT, precision=lax.Precision.HIGHEST, preferred_element_type=f32
    )
    spec_ref[0] = full(sel_a, pa_ref[...])
    spec_ref[1] = full(sel_b, pb_ref[...])
    small = jnp.sum(recv_ref[:, 2 * C :, :], axis=0) * RHO
    r = lax.broadcasted_iota(jnp.int32, (C, LANES), 0)
    l = lax.broadcasted_iota(jnp.int32, (C, LANES), 1)
    pr = lax.broadcasted_iota(jnp.int32, (LANES, C), 0)
    pc = lax.broadcasted_iota(jnp.int32, (LANES, C), 1)
    pick = jnp.where(pr % C == pc, 1.0, 0.0)
    for i, ref in enumerate((skip_ref, in_ref, outer_ref)):
        two = jnp.concatenate(
            [jnp.broadcast_to(small[2 * i + h : 2 * i + h + 1], (8, LANES)) for h in range(2)], axis=0
        )
        two = jnp.where(l // C == r % 8, two, 0.0)
        ref[...] = jnp.dot(two, pick, precision=lax.Precision.HIGHEST, preferred_element_type=f32)
    bias_ref[...] = jnp.broadcast_to(small[6:7], (8, LANES))


def call(body, name, outs, scratch, *args):
    vm = pl.BlockSpec(memory_space=pltpu.VMEM)
    many = isinstance(outs, (list, tuple))
    return pl.pallas_call(
        body,
        out_shape=outs,
        in_specs=[vm] * len(args),
        out_specs=[vm] * len(outs) if many else vm,
        scratch_shapes=scratch,
        compiler_params=pltpu.CompilerParams(vmem_limit_bytes=48 * 2**20),
        name=name,
    )(*args)


def shape(*dims, dtype=f32):
    return jax.ShapeDtypeStruct(dims, dtype)


def shards(field, cotangent, spec_weight, skip_weight, skip_bias, mlp_in, mlp_out):
    low, hi, lo, offset, synth = [jnp.asarray(t) for t in tables()]
    field = field.reshape(C, XY, N)
    cotangent = cotangent.reshape(C, XY, N)
    weight = spec_weight.reshape(2, C, C, ML * C)
    wa = jnp.concatenate([weight[0], weight[0]], axis=2)
    wb = jnp.concatenate([-weight[1], weight[1]], axis=2)
    maps = jnp.stack([skip_weight, mlp_in, mlp_out.T, mlp_in.T, skip_weight.T])
    same = jnp.eye(16, dtype=bf16)
    kron = (maps[:, :, None, :, None] * same[None, None, :, None, :]).reshape(5, 256, 256)
    bias = jnp.broadcast_to(skip_bias[:, None, None], (C, 16, 2 * N)).reshape(256, 2 * N)
    turn = pltpu.VMEM((PX, PY * C, LANES), f32)
    cells = pltpu.VMEM((C, XY, N), f32)
    square = pltpu.VMEM((256, 256), f32)

    def exchange(block):
        return lax.all_to_all(block, ("px", "py"), 0, 0, tiled=True)

    sent = call(k_forward, "forward", shape(PEERS, C, LANES), [turn], field, low, hi, lo, offset)
    u, sent = call(
        k_mix, "mix", [shape(C, LANES), shape(PEERS, C, LANES)], [], exchange(sent), wa, wb
    )
    sent, dpre = call(
        k_middle, "middle",
        [shape(PEERS, C + 8, LANES), shape(C, XY, N, dtype=bf16)],
        [turn, cells, square, square, square, square],
        exchange(sent), field, cotangent, kron, bias, low, hi, lo, offset, synth,
    )
    sent, share = call(
        k_mix_back, "mix_back",
        [shape(PEERS, C, LANES), shape(NB, 2 * C + 8, LANES)],
        [], exchange(sent), u, wa, wb,
    )
    back = exchange(sent)
    share = lax.all_to_all(share, "batch", 0, 0, tiled=True)
    grad_input = call(
        k_input, "input_grad", shape(C, XY, N, dtype=bf16), [turn, cells],
        back, dpre, kron, hi, lo, offset, synth,
    )
    spec, skip, b, inner, outer = call(
        k_shared, "shared",
        [shape(2, 8, 256), shape(C, C), shape(8, LANES), shape(C, C), shape(C, C)],
        [pltpu.VMEM((256, LANES), f32)] * 2, share,
    )
    spec = spec.reshape(2, ML, 2, C, C).transpose(0, 3, 4, 1, 2).reshape(2, C, C, 1, ML, 2)
    return (grad_input.reshape(1, C, XL, YL, N), spec, skip, b[0, :C], inner, outer)


def solution(mesh):
    placed = (
        P("batch", None, "px", "py", None),
        P("batch", None, "px", "py", None),
        P(None, None, None, "py", "px", None),
        P(),
        P(),
        P(),
        P(),
    )
    return jax.shard_map(
        shards,
        mesh=mesh,
        in_specs=placed,
        out_specs=(
            P("batch", None, "px", "py", None),
            P(None, None, None, "py", "px", "batch"),
            P(),
            P(),
            P(),
            P(),
        ),
        check_vma=False,
    )
```

```python
import math

import jax
import jax.numpy as jnp
import ml_dtypes
import numpy as np
from jax import lax
from jax.experimental import pallas as pl
from jax.experimental.pallas import tpu as pltpu
from jax.sharding import PartitionSpec as P

f32 = jnp.float32
bf16 = jnp.bfloat16
C = 16
N = 128
PX, PY, NB = 4, 16, 8
XL, YL = N // PX, N // PY
XY = XL * YL
ML = C // PX
PEERS = PX * PY
SMALL = 7
ROWS = C + SMALL
LANES = 128
SIGMA = 1.0 / math.sqrt(N**3)
RHO = 1.0 / math.sqrt(NB * N**3)
NT = (((1,), (1,)), ((), ()))


def tables():
    turn = lambda r, n: 2.0 * np.pi * (np.mod(r, n) / n)
    freq = np.where(np.arange(C) < C // 2, np.arange(C), np.arange(C) - C)
    depth = turn(np.arange(C)[:, None] * np.arange(N)[None, :], N)
    cos_z, sin_z = np.cos(depth), np.sin(depth)
    low = np.concatenate([cos_z, -sin_z]).astype(ml_dtypes.bfloat16)
    ax = turn(np.arange(XL)[:, None] * freq[None, :], N)
    ay = turn(np.arange(YL)[:, None] * freq[None, :], N)
    phase = ax[:, None, None, :] + ay[None, :, :, None]
    phase = phase.reshape(XY, PX, ML * C)
    co, si = np.cos(phase), np.sin(phase)
    plane = np.stack([co, -si], axis=2).reshape(XY, PX * LANES)
    plane_hi = plane.astype(ml_dtypes.bfloat16)
    plane_lo = (plane - plane_hi.astype(np.float64)).astype(ml_dtypes.bfloat16)
    ox = turn(np.arange(PX)[:, None] * XL * freq[None, :], N)
    oy = turn(np.arange(PY)[:, None] * YL * freq[None, :], N)
    off = ox[:, None, None, :] + oy[None, :, :, None]
    off = off.reshape(PEERS, PX, ML * C)
    cs = np.concatenate([np.cos(off), np.cos(off)], axis=2)
    sn = np.concatenate([np.sin(off), np.sin(off)], axis=2)
    offset = (np.concatenate([cs, sn], axis=1) * SIGMA).astype(np.float32)
    eye = np.eye(8)
    synth = np.concatenate(
        [
            np.einsum("ab,kz->akbz", eye, cos_z).reshape(8 * C, 8 * N),
            np.einsum("ab,kz->akbz", eye, -sin_z).reshape(8 * C, 8 * N),
        ]
    ).astype(ml_dtypes.bfloat16)
    return low, plane_hi, plane_lo, offset, synth


def dot(a, b):
    return jnp.dot(a, b, preferred_element_type=f32)


def dot_nt(a, b):
    return lax.dot_general(a, b, NT, preferred_element_type=f32)


def split(a):
    hi = a.astype(bf16)
    return hi, (a - hi.astype(f32)).astype(bf16)


def halves():
    lane = lax.broadcasted_iota(jnp.int32, (1, LANES), 1)
    return jnp.where(lane < LANES // 2, -1.0, 1.0)


def turned(v):
    return halves() * pltpu.roll(v, LANES // 2, 1)


def my_place():
    return lax.axis_index("px") * PY + lax.axis_index("py")


def forward_part(get, low_ref, hi_ref, lo_ref, off_ref, turn_ref, put):
    low = low_ref[...]
    rows = [dot_nt(low, get(c)) for c in range(C)]
    both = jnp.concatenate([r[:C] for r in rows] + [r[C:] for r in rows], axis=0)
    x_hi, x_lo = split(both)
    hi = hi_ref[...]
    part = dot(x_hi, hi) + dot(x_lo, hi) + dot(x_hi, lo_ref[...])
    for mb in range(PX):
        pa = part[: C * C, mb * LANES : (mb + 1) * LANES]
        pb = part[C * C :, mb * LANES : (mb + 1) * LANES]
        co, si = off_ref[mb : mb + 1, :], off_ref[PX + mb : PX + mb + 1, :]
        turn_ref[mb] = (pa * co + pb * si) + turned(pb * co - pa * si)
    for mb in range(PX):
        for k in range(C):
            put(mb * PY + k, turn_ref[mb, pl.ds(k, C, stride=C), :])


def inverse_part(recv_ref, hi_ref, lo_ref, off_ref, synth_ref, turn_ref, g_ref):
    for mb in range(PX):
        v = recv_ref[mb * PY : (mb + 1) * PY].reshape(PY * C, LANES)
        r = turned(v)
        co, si = off_ref[mb : mb + 1, :], off_ref[PX + mb : PX + mb + 1, :]
        turn_ref[mb] = v * co + r * si
        turn_ref[PX + mb] = v * si - r * co
    rows = []
    for half in range(2):
        for o in range(C):
            rows.append(
                jnp.concatenate(
                    [turn_ref[half * PX + mb, pl.ds(o, C, stride=C), :] for mb in range(PX)], axis=1
                )
            )
    v_hi, v_lo = split(jnp.concatenate(rows, axis=0))
    hi = hi_ref[...]
    z = dot_nt(hi, v_hi) + dot_nt(hi, v_lo) + dot_nt(lo_ref[...], v_hi)
    z = z.astype(bf16)
    for ob in range(2):
        re = z[:, ob * LANES : (ob + 1) * LANES]
        im = z[:, C * C + ob * LANES : C * C + (ob + 1) * LANES]
        g = dot(jnp.concatenate([re, im], axis=1), synth_ref[...])
        for o in range(8):
            g_ref[ob * 8 + o] = g[:, o * N : (o + 1) * N]


def k_forward(
    field_hbm, low_hbm, hi_hbm, lo_hbm, offset_hbm, out_ref,
    field_ref, low_ref, hi_ref, lo_ref, off_ref, turn_ref, sems,
):
    copies = [
        pltpu.make_async_copy(a, b, sems.at[i])
        for i, (a, b) in enumerate(
            (
                (low_hbm, low_ref),
                (field_hbm, field_ref),
                (hi_hbm, hi_ref),
                (lo_hbm, lo_ref),
                (offset_hbm.at[my_place()], off_ref),
            )
        )
    ]
    for copy in copies:
        copy.start()
    for copy in copies:
        copy.wait()

    def put(d, value):
        out_ref[d] = value

    forward_part(lambda c: field_ref[c], low_ref, hi_ref, lo_ref, off_ref, turn_ref, put)


def spread_map(w, transpose):
    r = lax.broadcasted_iota(jnp.int32, (256, C), 0)
    l = lax.broadcasted_iota(jnp.int32, (256, C), 1)
    rep = jnp.where(r // 16 == l, 1.0, 0.0).astype(bf16)
    if transpose:
        wide = lax.dot_general(w, rep, (((0,), (1,)), ((), ())), preferred_element_type=f32)
    else:
        wide = dot_nt(w, rep)
    full = dot(rep, wide.astype(bf16))
    r = lax.broadcasted_iota(jnp.int32, (256, 256), 0)
    l = lax.broadcasted_iota(jnp.int32, (256, 256), 1)
    return jnp.where(r % 16 == l % 16, full, 0.0).astype(bf16)


def k_maps(skip_ref, in_ref, outer_ref, bias_in_ref, kron_ref, bias_ref):
    kron_ref[0] = spread_map(skip_ref[...], False)
    kron_ref[1] = spread_map(in_ref[...], False)
    kron_ref[2] = spread_map(outer_ref[...], True)
    kron_ref[3] = spread_map(in_ref[...], True)
    kron_ref[4] = spread_map(skip_ref[...], True)
    r = lax.broadcasted_iota(jnp.int32, (256, C), 0)
    l = lax.broadcasted_iota(jnp.int32, (256, C), 1)
    column = jnp.sum(jnp.where(r // 16 == l, bias_in_ref[...], 0.0), axis=1, keepdims=True)
    bias_ref[...] = jnp.broadcast_to(column, (256, N))


def k_mix(recv_ref, wa_ref, wb_ref, u_ref, out_ref):
    u = jnp.sum(recv_ref[...], axis=0)
    us = pltpu.roll(u, LANES // 2, 1)
    u_ref[...] = u
    v = jnp.zeros((C, LANES), f32)
    for c in range(C):
        v = v + wa_ref[c] * u[c : c + 1, :] + wb_ref[c] * us[c : c + 1, :]
    out_ref[...] = jnp.broadcast_to(v[None], (PEERS, C, LANES))


def gelu_parts(x):
    a = math.sqrt(2.0 / math.pi)
    b = a * 0.044715
    x2 = x * x
    h = 0.5 * jnp.tanh(x * (a + b * x2)) + 0.5
    g = x * h
    d = h + g * (1.0 - h) * (2.0 * a + (6.0 * b) * x2)
    return g, d


def tile(ref, p):
    left = ref[:, pl.ds(p * 32, 16), :].reshape(C * 16, N)
    right = ref[:, pl.ds(p * 32 + 16, 16), :].reshape(C * 16, N)
    return jnp.concatenate([left, right], axis=1)


def untile(ref, p, value):
    ref[:, pl.ds(p * 32, 16), :] = value[:, :N].reshape(C, 16, N)
    ref[:, pl.ds(p * 32 + 16, 16), :] = value[:, N:].reshape(C, 16, N)


def pack_rows(acc):
    r = lax.broadcasted_iota(jnp.int32, (256, 256), 0)
    l = lax.broadcasted_iota(jnp.int32, (256, 256), 1)
    kept = jnp.where(r % 16 == l % 16, acc, 0.0).reshape(C, 16, 256).sum(axis=1)
    r = lax.broadcasted_iota(jnp.int32, (256, LANES), 0)
    l = lax.broadcasted_iota(jnp.int32, (256, LANES), 1)
    pick = jnp.where(r // 16 == l % 16, 1.0, 0.0)
    spread = jnp.dot(kept, pick, precision=lax.Precision.HIGHEST, preferred_element_type=f32)
    r = lax.broadcasted_iota(jnp.int32, (C, LANES), 0)
    l = lax.broadcasted_iota(jnp.int32, (C, LANES), 1)
    spread = jnp.where(r % 8 == l // 16, spread, 0.0)
    return spread.reshape(2, 8, LANES).sum(axis=1)


def k_middle(
    recv_ref, field_ref, cot_ref, kron_ref, bias_ref, low_ref, hi_ref, lo_ref, offset_ref, synth_ref,
    out_ref, dpre_hbm,
    dpre_ref, sem, turn_ref, g_ref, skip_acc, bias_acc, in_acc, out_acc,
):
    off_ref = offset_ref.at[my_place()]
    inverse_part(recv_ref, hi_ref, lo_ref, off_ref, synth_ref, turn_ref, g_ref)
    bias = jnp.concatenate([bias_ref[...], bias_ref[...]], axis=1)
    skip_acc[...] = jnp.zeros_like(skip_acc)
    in_acc[...] = jnp.zeros_like(in_acc)
    out_acc[...] = jnp.zeros_like(out_acc)
    bias_acc[...] = jnp.zeros_like(bias_acc)

    def step(p, carry):
        f = tile(field_ref, p)
        cot = tile(cot_ref, p)
        pre = tile(g_ref, p) + dot(kron_ref[0], f) + bias
        hid, d_hid = gelu_parts(pre)
        hid = hid.astype(bf16)
        act, d_act = gelu_parts(dot(kron_ref[1], hid))
        act = act.astype(bf16)
        d_inner = (dot(kron_ref[2], cot) * d_act).astype(bf16)
        dpre = dot(kron_ref[3], d_inner) * d_hid
        dpre = dpre.astype(bf16)
        untile(dpre_ref, p, dpre)
        skip_acc[...] += dot_nt(dpre, f)
        in_acc[...] += dot_nt(d_inner, hid)
        out_acc[...] += dot_nt(cot, act)
        bias_acc[...] += dpre.astype(f32)
        return carry

    lax.fori_loop(0, XY // 32, step, 0)
    copy = pltpu.make_async_copy(dpre_ref, dpre_hbm, sem)
    copy.start()
    bias = bias_acc[...].reshape(C, 16, 256).sum(axis=1)
    total = jnp.sum(bias, axis=1, keepdims=True)
    r = lax.broadcasted_iota(jnp.int32, (C, LANES), 0)
    l = lax.broadcasted_iota(jnp.int32, (C, LANES), 1)
    bias_row = jnp.sum(jnp.where(r == l, total, 0.0), axis=0, keepdims=True)
    small = jnp.concatenate(
        [pack_rows(skip_acc[...]), pack_rows(in_acc[...]), pack_rows(out_acc[...]),
         bias_row, jnp.zeros((1, LANES), f32)], axis=0
    )
    small = small[:SMALL]

    def put(d, value):
        out_ref[d * ROWS : (d + 1) * ROWS, :] = jnp.concatenate([value, small], axis=0)

    forward_part(lambda c: dpre_ref[c], low_ref, hi_ref, lo_ref, off_ref, turn_ref, put)
    copy.wait()


def k_mix_back(recv_ref, u_ref, wa_ref, wb_ref, out_ref, share_ref):
    slabs = recv_ref[...].reshape(8, 8 * ROWS, LANES).sum(axis=0)
    got = slabs[:ROWS]
    for i in range(1, 8):
        got = got + slabs[i * ROWS : (i + 1) * ROWS]
    g = got[:C]
    gs = pltpu.roll(g, LANES // 2, 1)
    rows = []
    for c in range(C):
        rows.append(jnp.sum(wa_ref[c] * g - wb_ref[c] * gs, axis=0, keepdims=True))
    du = jnp.concatenate(rows, axis=0)
    out_ref[...] = jnp.broadcast_to(du[None], (PEERS, C, LANES))
    share = jnp.concatenate([u_ref[...], got, jnp.zeros((8 - SMALL, LANES), f32)], axis=0)
    share_ref[...] = jnp.broadcast_to(share[None], (NB, 2 * C + 8, LANES))


def k_input(
    recv_ref, dpre_ref, kron_ref, hi_ref, lo_ref, offset_ref, synth_ref, out_hbm,
    out_ref, turn_ref, g_ref, sems,
):
    off_ref = offset_ref.at[my_place()]
    inverse_part(recv_ref, hi_ref, lo_ref, off_ref, synth_ref, turn_ref, g_ref)
    steps = XY // 32
    copies = []
    for p in range(steps):
        untile(out_ref, p, (dot(kron_ref[4], tile(dpre_ref, p)) + tile(g_ref, p)).astype(bf16))
        part = pl.ds(p * 32, 32)
        copies.append(pltpu.make_async_copy(out_ref.at[:, part], out_hbm.at[:, part], sems.at[p]))
        copies[-1].start()
    for copy in copies:
        copy.wait()


def k_shared(recv_ref, spec_ref, skip_ref, bias_ref, in_ref, outer_ref, pa_ref, pb_ref):
    for c in range(C):
        pa = jnp.zeros((C, LANES), f32)
        pb = jnp.zeros((C, LANES), f32)
        for s in range(NB):
            u = recv_ref[s, c : c + 1, :]
            g = recv_ref[s, C : 2 * C, :]
            pa = pa + u * g
            pb = pb + u * pltpu.roll(g, LANES // 2, 1)
        pa_ref[c * C : (c + 1) * C, :] = pa
        pb_ref[c * C : (c + 1) * C, :] = pb
    b = lax.axis_index("batch")
    r = lax.broadcasted_iota(jnp.int32, (8, LANES), 0)
    l = lax.broadcasted_iota(jnp.int32, (8, LANES), 1)
    mine = ((l % 64) // C == r // 2) & (l % C == 2 * b + r % 2)
    sel_a = jnp.where(mine, 1.0, 0.0)
    sel_b = jnp.where(l < 64, sel_a, -sel_a)
    full = lambda x, y: lax.dot_general(
        x, y, NT, precision=lax.Precision.HIGHEST, preferred_element_type=f32
    )
    for i, part in enumerate((full(sel_a, pa_ref[...]), full(sel_b, pb_ref[...]))):
        for c in range(C):
            for m in range(ML):
                spec_ref[i, c, m] = part[2 * m : 2 * m + 2, c * C : (c + 1) * C]
    small = jnp.sum(recv_ref[:, 2 * C :, :], axis=0) * RHO
    r = lax.broadcasted_iota(jnp.int32, (C, LANES), 0)
    l = lax.broadcasted_iota(jnp.int32, (C, LANES), 1)
    pr = lax.broadcasted_iota(jnp.int32, (LANES, C), 0)
    pc = lax.broadcasted_iota(jnp.int32, (LANES, C), 1)
    pick = jnp.where(pr % C == pc, 1.0, 0.0)
    for i, ref in enumerate((skip_ref, in_ref, outer_ref)):
        two = jnp.concatenate(
            [jnp.broadcast_to(small[2 * i + h : 2 * i + h + 1], (8, LANES)) for h in range(2)], axis=0
        )
        two = jnp.where(l // C == r % 8, two, 0.0)
        ref[...] = jnp.dot(two, pick, precision=lax.Precision.HIGHEST, preferred_element_type=f32)
    bias_ref[...] = jnp.broadcast_to(small[6:7], (8, LANES))


def call(body, name, outs, scratch, *args, hbm_in=(), hbm_out=()):
    vm = pl.BlockSpec(memory_space=pltpu.VMEM)
    hbm = pl.BlockSpec(memory_space=pltpu.HBM)
    many = isinstance(outs, (list, tuple))
    out_specs = [hbm if i in hbm_out else vm for i in range(len(outs) if many else 1)]
    return pl.pallas_call(
        body,
        out_shape=outs,
        in_specs=[hbm if i in hbm_in else vm for i in range(len(args))],
        out_specs=out_specs if many else out_specs[0],
        scratch_shapes=scratch,
        compiler_params=pltpu.CompilerParams(vmem_limit_bytes=40 * 2**20),
        name=name,
    )(*args)


def shape(*dims, dtype=f32):
    return jax.ShapeDtypeStruct(dims, dtype)


def shards(field, cotangent, spec_weight, skip_weight, skip_bias, mlp_in, mlp_out):
    low, hi, lo, offset, synth = [jnp.asarray(t) for t in tables()]
    field = field.reshape(C, XY, N)
    cotangent = cotangent.reshape(C, XY, N)
    weight = spec_weight.reshape(2, C, C, ML * C)
    wa = jnp.concatenate([weight[0], weight[0]], axis=2)
    wb = jnp.concatenate([-weight[1], weight[1]], axis=2)
    turn = pltpu.VMEM((PX, PY * C, LANES), f32)
    twice = pltpu.VMEM((2 * PX, PY * C, LANES), f32)
    cells = pltpu.VMEM((C, XY, N), f32)
    cells_low = pltpu.VMEM((C, XY, N), bf16)
    square = pltpu.VMEM((256, 256), f32)
    own = pltpu.VMEM((8, LANES), f32)
    plane = pltpu.VMEM((XY, PX * LANES), bf16)

    def exchange(block):
        return lax.all_to_all(block, ("px", "py"), 0, 0, tiled=True)

    sent = call(
        k_forward, "forward", shape(PEERS, C, LANES),
        [cells_low, pltpu.VMEM((2 * C, N), bf16), plane, plane, own, turn, pltpu.SemaphoreType.DMA((5,))],
        field, low, hi, lo, offset, hbm_in=range(5),
    )
    kron, bias = call(
        k_maps, "maps", [shape(5, 256, 256, dtype=bf16), shape(256, N)], [],
        skip_weight, mlp_in, mlp_out, skip_bias.reshape(1, C),
    )
    u, sent = call(
        k_mix, "mix", [shape(C, LANES), shape(PEERS, C, LANES)], [], exchange(sent), wa, wb
    )
    sent, dpre = call(
        k_middle, "middle",
        [shape(PEERS * ROWS, LANES), shape(C, XY, N, dtype=bf16)],
        [cells_low, pltpu.SemaphoreType.DMA, twice, cells, square, square, square, square],
        exchange(sent), field, cotangent, kron, bias, low, hi, lo, offset, synth, hbm_out=(1,),
    )
    sent = exchange(sent.reshape(PEERS, 1, ROWS * LANES)).reshape(PEERS * ROWS, LANES)
    sent, share = call(
        k_mix_back, "mix_back",
        [shape(PEERS, C, LANES), shape(NB, 2 * C + 8, LANES)],
        [], sent, u, wa, wb,
    )
    back, share = lax.optimization_barrier((exchange(sent), share))
    share = lax.all_to_all(share, "batch", 0, 0, tiled=True)
    grad_input = call(
        k_input, "input_grad", shape(C, XY, N, dtype=bf16),
        [cells_low, twice, cells, pltpu.SemaphoreType.DMA((XY // 32,))],
        back, dpre, kron, hi, lo, offset, synth, hbm_out=(0,),
    )
    spec, skip, b, inner, outer = call(
        k_shared, "shared",
        [shape(2, C, ML, 2, C), shape(C, C), shape(8, LANES), shape(C, C), shape(C, C)],
        [pltpu.VMEM((256, LANES), f32)] * 2, share,
    )
    spec = spec.transpose(0, 1, 4, 2, 3).reshape(2, C, C, 1, ML, 2)
    return (grad_input.reshape(1, C, XL, YL, N), spec, skip, b[0, :C], inner, outer)


def solution(mesh):
    placed = (
        P("batch", None, "px", "py", None),
        P("batch", None, "px", "py", None),
        P(None, None, None, "py", "px", None),
        P(),
        P(),
        P(),
        P(),
    )
    return jax.shard_map(
        shards,
        mesh=mesh,
        in_specs=placed,
        out_specs=(
            P("batch", None, "px", "py", None),
            P(None, None, None, "py", "px", "batch"),
            P(),
            P(),
            P(),
            P(),
        ),
        check_vma=False,
    )
```

```python
import math

import jax
import jax.numpy as jnp
import ml_dtypes
import numpy as np
from jax import lax
from jax.experimental import pallas as pl
from jax.experimental.pallas import tpu as pltpu
from jax.sharding import PartitionSpec as P

f32 = jnp.float32
bf16 = jnp.bfloat16
C = 16
N = 128
PX, PY, NB = 4, 16, 8
XL, YL = N // PX, N // PY
XY = XL * YL
ML = C // PX
PEERS = PX * PY
ROWS = C + 1
LANES = 128
SIGMA = 1.0 / math.sqrt(N**3)
RHO = 1.0 / math.sqrt(NB * N**3)
NT = (((1,), (1,)), ((), ()))


def tables():
    turn = lambda r, n: 2.0 * np.pi * (np.mod(r, n) / n)
    freq = np.where(np.arange(C) < C // 2, np.arange(C), np.arange(C) - C)
    depth = turn(np.arange(C)[:, None] * np.arange(N)[None, :], N)
    cos_z, sin_z = np.cos(depth), np.sin(depth)
    low = np.concatenate([cos_z, -sin_z]).astype(ml_dtypes.bfloat16)
    ax = turn(np.arange(XL)[:, None] * freq[None, :], N)
    ay = turn(np.arange(YL)[:, None] * freq[None, :], N)
    phase = ax[:, None, None, :] + ay[None, :, :, None]
    phase = phase.reshape(XY, PX, ML * C)
    co, si = np.cos(phase), np.sin(phase)
    plane = np.stack([co, -si], axis=2).reshape(XY, PX * LANES)
    plane_hi = plane.astype(ml_dtypes.bfloat16)
    plane_lo = (plane - plane_hi.astype(np.float64)).astype(ml_dtypes.bfloat16)
    ox = turn(np.arange(PX)[:, None] * XL * freq[None, :], N)
    oy = turn(np.arange(PY)[:, None] * YL * freq[None, :], N)
    off = ox[:, None, None, :] + oy[None, :, :, None]
    off = off.reshape(PEERS, PX, ML * C)
    cs = np.concatenate([np.cos(off), np.cos(off)], axis=2)
    sn = np.concatenate([np.sin(off), np.sin(off)], axis=2)
    offset = (np.concatenate([cs, sn], axis=1) * SIGMA).astype(np.float32)
    eye = np.eye(8)
    synth = np.concatenate(
        [
            np.einsum("ab,kz->akbz", eye, cos_z).reshape(8 * C, 8 * N),
            np.einsum("ab,kz->akbz", eye, -sin_z).reshape(8 * C, 8 * N),
        ]
    ).astype(ml_dtypes.bfloat16)
    return low, plane_hi, plane_lo, offset, synth


def dot(a, b):
    return jnp.dot(a, b, preferred_element_type=f32)


def dot_nt(a, b):
    return lax.dot_general(a, b, NT, preferred_element_type=f32)


def split(a):
    hi = a.astype(bf16)
    return hi, (a - hi.astype(f32)).astype(bf16)


def halves():
    lane = lax.broadcasted_iota(jnp.int32, (1, LANES), 1)
    return jnp.where(lane < LANES // 2, -1.0, 1.0)


def turned(v):
    return halves() * pltpu.roll(v, LANES // 2, 1)


def my_place():
    return lax.axis_index("px") * PY + lax.axis_index("py")


def forward_part(get, low_ref, hi_ref, lo_ref, off_ref, turn_ref, put):
    low = low_ref[...]
    rows = [dot_nt(low, get(c)) for c in range(C)]
    both = jnp.concatenate([r[:C] for r in rows] + [r[C:] for r in rows], axis=0)
    x_hi, x_lo = split(both)
    hi = hi_ref[...]
    part = dot(x_hi, hi) + dot(x_lo, hi) + dot(x_hi, lo_ref[...])
    for mb in range(PX):
        pa = part[: C * C, mb * LANES : (mb + 1) * LANES]
        pb = part[C * C :, mb * LANES : (mb + 1) * LANES]
        co, si = off_ref[mb : mb + 1, :], off_ref[PX + mb : PX + mb + 1, :]
        turn_ref[mb] = (pa * co + pb * si) + turned(pb * co - pa * si)
    for mb in range(PX):
        for k in range(C):
            put(mb * PY + k, turn_ref[mb, pl.ds(k, C, stride=C), :])


def inverse_part(block, hi_ref, lo_ref, off_ref, synth_ref, turn_ref, g_ref):
    for mb in range(PX):
        v = jnp.concatenate([block(mb * PY + k) for k in range(PY)], axis=0)
        r = turned(v)
        co, si = off_ref[mb : mb + 1, :], off_ref[PX + mb : PX + mb + 1, :]
        turn_ref[mb] = v * co + r * si
        turn_ref[PX + mb] = v * si - r * co
    rows = []
    for half in range(2):
        for o in range(C):
            rows.append(
                jnp.concatenate(
                    [turn_ref[half * PX + mb, pl.ds(o, C, stride=C), :] for mb in range(PX)], axis=1
                )
            )
    v_hi, v_lo = split(jnp.concatenate(rows, axis=0))
    hi = hi_ref[...]
    z = dot_nt(hi, v_hi) + dot_nt(hi, v_lo) + dot_nt(lo_ref[...], v_hi)
    z = z.astype(bf16)
    for ob in range(2):
        re = z[:, ob * LANES : (ob + 1) * LANES]
        im = z[:, C * C + ob * LANES : C * C + (ob + 1) * LANES]
        g = dot(jnp.concatenate([re, im], axis=1), synth_ref[...])
        for o in range(8):
            g_ref[ob * 8 + o] = g[:, o * N : (o + 1) * N]


def k_forward(
    field_hbm, low_hbm, hi_hbm, lo_hbm, offset_hbm, out_ref,
    field_ref, low_ref, hi_ref, lo_ref, off_ref, turn_ref, sems,
):
    copies = [
        pltpu.make_async_copy(a, b, sems.at[i])
        for i, (a, b) in enumerate(
            (
                (low_hbm, low_ref),
                (field_hbm, field_ref),
                (hi_hbm, hi_ref),
                (lo_hbm, lo_ref),
                (offset_hbm.at[my_place()], off_ref),
            )
        )
    ]
    for copy in copies:
        copy.start()
    for copy in copies:
        copy.wait()

    def put(d, value):
        out_ref[d] = value

    forward_part(lambda c: field_ref[c], low_ref, hi_ref, lo_ref, off_ref, turn_ref, put)


def spread_map(w, transpose):
    r = lax.broadcasted_iota(jnp.int32, (256, C), 0)
    l = lax.broadcasted_iota(jnp.int32, (256, C), 1)
    rep = jnp.where(r // 16 == l, 1.0, 0.0).astype(bf16)
    if transpose:
        wide = lax.dot_general(w, rep, (((0,), (1,)), ((), ())), preferred_element_type=f32)
    else:
        wide = dot_nt(w, rep)
    full = dot(rep, wide.astype(bf16))
    r = lax.broadcasted_iota(jnp.int32, (256, 256), 0)
    l = lax.broadcasted_iota(jnp.int32, (256, 256), 1)
    return jnp.where(r % 16 == l % 16, full, 0.0).astype(bf16)


def k_maps(skip_ref, in_ref, outer_ref, bias_in_ref, kron_ref, bias_ref):
    kron_ref[0] = spread_map(skip_ref[...], False)
    kron_ref[1] = spread_map(in_ref[...], False)
    kron_ref[2] = spread_map(outer_ref[...], True)
    kron_ref[3] = spread_map(in_ref[...], True)
    kron_ref[4] = spread_map(skip_ref[...], True)
    r = lax.broadcasted_iota(jnp.int32, (256, C), 0)
    l = lax.broadcasted_iota(jnp.int32, (256, C), 1)
    column = jnp.sum(jnp.where(r // 16 == l, bias_in_ref[...], 0.0), axis=1, keepdims=True)
    bias_ref[...] = jnp.broadcast_to(column, (256, N))


def k_mix(recv_ref, wa_ref, wb_ref, u_ref, out_ref):
    u = jnp.sum(recv_ref[...], axis=0)
    us = pltpu.roll(u, LANES // 2, 1)
    u_ref[...] = u
    v = jnp.zeros((C, LANES), f32)
    for c in range(C):
        v = v + wa_ref[c] * u[c : c + 1, :] + wb_ref[c] * us[c : c + 1, :]
    out_ref[...] = jnp.broadcast_to(v[None], (PEERS, C, LANES))


def gelu_parts(x):
    a = math.sqrt(2.0 / math.pi)
    b = a * 0.044715
    x2 = x * x
    h = 0.5 * jnp.tanh(x * (a + b * x2)) + 0.5
    g = x * h
    d = h + g * (1.0 - h) * (2.0 * a + (6.0 * b) * x2)
    return g, d


def tile(ref, p):
    left = ref[:, pl.ds(p * 32, 16), :].reshape(C * 16, N)
    right = ref[:, pl.ds(p * 32 + 16, 16), :].reshape(C * 16, N)
    return jnp.concatenate([left, right], axis=1)


def untile(ref, p, value):
    ref[:, pl.ds(p * 32, 16), :] = value[:, :N].reshape(C, 16, N)
    ref[:, pl.ds(p * 32 + 16, 16), :] = value[:, N:].reshape(C, 16, N)


def pack_rows(acc):
    r = lax.broadcasted_iota(jnp.int32, (256, 256), 0)
    l = lax.broadcasted_iota(jnp.int32, (256, 256), 1)
    kept = jnp.where(r % 16 == l % 16, acc, 0.0).reshape(C, 16, 256).sum(axis=1)
    r = lax.broadcasted_iota(jnp.int32, (256, LANES), 0)
    l = lax.broadcasted_iota(jnp.int32, (256, LANES), 1)
    pick = jnp.where(r // 16 == l % 16, 1.0, 0.0)
    spread = jnp.dot(kept, pick, precision=lax.Precision.HIGHEST, preferred_element_type=f32)
    r = lax.broadcasted_iota(jnp.int32, (C, LANES), 0)
    l = lax.broadcasted_iota(jnp.int32, (C, LANES), 1)
    return jnp.where(r % 8 == l // 16, spread, 0.0)


def k_middle(
    recv_ref, field_hbm, cot_hbm, bias_hbm, kron_ref, low_ref, hi_ref, lo_ref, offset_ref, synth_ref,
    out_ref, dpre_hbm,
    field_ref, cot_ref, bias_ref, dpre_ref, sems, turn_ref, g_ref, skip_acc, bias_acc, in_acc, out_acc,
):
    copies = [
        pltpu.make_async_copy(a, b, sems.at[i])
        for i, (a, b) in enumerate(
            ((field_hbm, field_ref), (cot_hbm, cot_ref), (bias_hbm, bias_ref))
        )
    ]
    for copy in copies:
        copy.start()
    off_ref = offset_ref.at[my_place()]
    inverse_part(lambda d: recv_ref[d], hi_ref, lo_ref, off_ref, synth_ref, turn_ref, g_ref)
    for copy in copies:
        copy.wait()
    bias = jnp.concatenate([bias_ref[...], bias_ref[...]], axis=1)
    skip_acc[...] = jnp.zeros_like(skip_acc)
    in_acc[...] = jnp.zeros_like(in_acc)
    out_acc[...] = jnp.zeros_like(out_acc)
    bias_acc[...] = jnp.zeros_like(bias_acc)

    def step(p, carry):
        f = tile(field_ref, p)
        cot = tile(cot_ref, p)
        pre = tile(g_ref, p) + dot(kron_ref[0], f) + bias
        hid, d_hid = gelu_parts(pre)
        hid = hid.astype(bf16)
        act, d_act = gelu_parts(dot(kron_ref[1], hid))
        act = act.astype(bf16)
        d_inner = (dot(kron_ref[2], cot) * d_act).astype(bf16)
        dpre = dot(kron_ref[3], d_inner) * d_hid
        dpre = dpre.astype(bf16)
        untile(dpre_ref, p, dpre)
        skip_acc[...] += dot_nt(dpre, f)
        in_acc[...] += dot_nt(d_inner, hid)
        out_acc[...] += dot_nt(cot, act)
        bias_acc[...] += dpre.astype(f32)
        return carry

    lax.fori_loop(0, XY // 32, step, 0)
    copy = pltpu.make_async_copy(dpre_ref, dpre_hbm, sems.at[3])
    copy.start()
    bias = bias_acc[...].reshape(C, 16, 256).sum(axis=1)
    total = jnp.sum(bias, axis=1, keepdims=True)
    r = lax.broadcasted_iota(jnp.int32, (C, LANES), 0)
    l = lax.broadcasted_iota(jnp.int32, (C, LANES), 1)
    bias_row = jnp.sum(jnp.where(r == l, total, 0.0), axis=0, keepdims=True)
    small = jnp.concatenate(
        [pack_rows(skip_acc[...]), pack_rows(in_acc[...]), pack_rows(out_acc[...]),
         bias_row, jnp.zeros((C - 1, LANES), f32)], axis=0
    )

    def put(d, value):
        out_ref[d * ROWS : (d + 1) * ROWS, :] = jnp.concatenate([value, small[d : d + 1]], axis=0)

    forward_part(lambda c: dpre_ref[c], low_ref, hi_ref, lo_ref, off_ref, turn_ref, put)
    copy.wait()


def k_mix_back(recv_ref, wa_ref, wb_ref, out_ref, g_ref):
    slabs = recv_ref[...].reshape(8, 8 * ROWS, LANES).sum(axis=0)
    got = slabs[:ROWS]
    for i in range(1, 8):
        got = got + slabs[i * ROWS : (i + 1) * ROWS]
    g = got[:C]
    g_ref[...] = g
    gs = pltpu.roll(g, LANES // 2, 1)
    rows = []
    for c in range(C):
        rows.append(jnp.sum(wa_ref[c] * g - wb_ref[c] * gs, axis=0, keepdims=True))
    block = jnp.concatenate(rows + [got[C:]], axis=0)
    slab = jnp.concatenate([block] * 8, axis=0)
    for i in range(8):
        out_ref[i * 8 * ROWS : (i + 1) * 8 * ROWS, :] = slab


def k_share(back_ref, u_ref, g_ref, share_ref):
    small = back_ref[pl.ds(C, PEERS, stride=ROWS), :].reshape(8, 8, LANES).sum(axis=1)
    share = jnp.concatenate([u_ref[...], g_ref[...], small], axis=0)
    share_ref[...] = jnp.broadcast_to(share[None], (NB, 2 * C + 8, LANES))


def k_input(
    recv_ref, dpre_ref, kron_ref, hi_ref, lo_ref, offset_ref, synth_ref, out_hbm,
    out_ref, turn_ref, g_ref, sems,
):
    off_ref = offset_ref.at[my_place()]
    inverse_part(
        lambda d: recv_ref[d * ROWS : d * ROWS + C, :],
        hi_ref, lo_ref, off_ref, synth_ref, turn_ref, g_ref,
    )
    steps = XY // 32
    copies = []
    for p in range(steps):
        untile(out_ref, p, (dot(kron_ref[4], tile(dpre_ref, p)) + tile(g_ref, p)).astype(bf16))
        part = pl.ds(p * 32, 32)
        copies.append(pltpu.make_async_copy(out_ref.at[:, part], out_hbm.at[:, part], sems.at[p]))
        copies[-1].start()
    for copy in copies:
        copy.wait()


def k_shared(recv_ref, spec_ref, skip_ref, bias_ref, in_ref, outer_ref, pa_ref, pb_ref):
    for c in range(C):
        pa = jnp.zeros((C, LANES), f32)
        pb = jnp.zeros((C, LANES), f32)
        for s in range(NB):
            u = recv_ref[s, c : c + 1, :]
            g = recv_ref[s, C : 2 * C, :]
            pa = pa + u * g
            pb = pb + u * pltpu.roll(g, LANES // 2, 1)
        pa_ref[c * C : (c + 1) * C, :] = pa
        pb_ref[c * C : (c + 1) * C, :] = pb
    b = lax.axis_index("batch")
    r = lax.broadcasted_iota(jnp.int32, (8, LANES), 0)
    l = lax.broadcasted_iota(jnp.int32, (8, LANES), 1)
    mine = ((l % 64) // C == r // 2) & (l % C == 2 * b + r % 2)
    sel_a = jnp.where(mine, 1.0, 0.0)
    sel_b = jnp.where(l < 64, sel_a, -sel_a)
    full = lambda x, y: lax.dot_general(
        x, y, NT, precision=lax.Precision.HIGHEST, preferred_element_type=f32
    )
    for i, part in enumerate((full(sel_a, pa_ref[...]), full(sel_b, pb_ref[...]))):
        for c in range(C):
            for m in range(ML):
                spec_ref[i, c, m] = part[2 * m : 2 * m + 2, c * C : (c + 1) * C]
    small = jnp.sum(recv_ref[:, 2 * C :, :], axis=0) * RHO
    r = lax.broadcasted_iota(jnp.int32, (C, LANES), 0)
    l = lax.broadcasted_iota(jnp.int32, (C, LANES), 1)
    pr = lax.broadcasted_iota(jnp.int32, (LANES, C), 0)
    pc = lax.broadcasted_iota(jnp.int32, (LANES, C), 1)
    pick = jnp.where(pr % C == pc, 1.0, 0.0)
    for i, ref in enumerate((skip_ref, in_ref, outer_ref)):
        two = jnp.concatenate(
            [jnp.broadcast_to(small[2 * i + h : 2 * i + h + 1], (8, LANES)) for h in range(2)], axis=0
        )
        two = jnp.where(l // C == r % 8, two, 0.0)
        ref[...] = jnp.dot(two, pick, precision=lax.Precision.HIGHEST, preferred_element_type=f32)
    bias_ref[...] = jnp.broadcast_to(small[6:7], (8, LANES))


def call(body, name, outs, scratch, *args, hbm_in=(), hbm_out=()):
    vm = pl.BlockSpec(memory_space=pltpu.VMEM)
    hbm = pl.BlockSpec(memory_space=pltpu.HBM)
    many = isinstance(outs, (list, tuple))
    out_specs = [hbm if i in hbm_out else vm for i in range(len(outs) if many else 1)]
    args = [
        pltpu.with_memory_space_constraint(a, pltpu.HBM) if i in hbm_in else a
        for i, a in enumerate(args)
    ]
    return pl.pallas_call(
        body,
        out_shape=outs,
        in_specs=[hbm if i in hbm_in else vm for i in range(len(args))],
        out_specs=out_specs if many else out_specs[0],
        scratch_shapes=scratch,
        compiler_params=pltpu.CompilerParams(vmem_limit_bytes=32 * 2**20),
        name=name,
    )(*args)


def shape(*dims, dtype=f32):
    return jax.ShapeDtypeStruct(dims, dtype)


def shards(field, cotangent, spec_weight, skip_weight, skip_bias, mlp_in, mlp_out):
    low, hi, lo, offset, synth = [jnp.asarray(t) for t in tables()]
    field = field.reshape(C, XY, N)
    cotangent = cotangent.reshape(C, XY, N)
    weight = spec_weight.reshape(2, C, C, ML * C)
    wa = jnp.concatenate([weight[0], weight[0]], axis=2)
    wb = jnp.concatenate([-weight[1], weight[1]], axis=2)
    turn = pltpu.VMEM((PX, PY * C, LANES), f32)
    twice = pltpu.VMEM((2 * PX, PY * C, LANES), f32)
    cells = pltpu.VMEM((C, XY, N), f32)
    cells_low = pltpu.VMEM((C, XY, N), bf16)
    square = pltpu.VMEM((256, 256), f32)
    own = pltpu.VMEM((8, LANES), f32)
    plane = pltpu.VMEM((XY, PX * LANES), bf16)

    def exchange(block):
        return lax.all_to_all(block, ("px", "py"), 0, 0, tiled=True)

    def exchange_rows(block):
        return exchange(block.reshape(PEERS, 1, ROWS * LANES)).reshape(PEERS * ROWS, LANES)

    sent = call(
        k_forward, "forward", shape(PEERS, C, LANES),
        [cells_low, pltpu.VMEM((2 * C, N), bf16), plane, plane, own, turn, pltpu.SemaphoreType.DMA((5,))],
        field, low, hi, lo, offset, hbm_in=range(5),
    )
    kron, bias = call(
        k_maps, "maps", [shape(5, 256, 256, dtype=bf16), shape(256, N)], [],
        skip_weight, mlp_in, mlp_out, skip_bias.reshape(1, C),
    )
    u, sent = call(
        k_mix, "mix", [shape(C, LANES), shape(PEERS, C, LANES)], [], exchange(sent), wa, wb
    )
    sent, dpre = call(
        k_middle, "middle",
        [shape(PEERS * ROWS, LANES), pltpu.HBM((C, XY, N), bf16)],
        [cells_low, cells_low, pltpu.VMEM((256, N), f32), cells_low, pltpu.SemaphoreType.DMA((4,)),
         twice, cells, square, square, square, square],
        exchange(sent), field, cotangent, bias, kron, low, hi, lo, offset, synth,
        hbm_in=(1, 2, 3), hbm_out=(1,),
    )
    sent, g = call(
        k_mix_back, "mix_back", [shape(PEERS * ROWS, LANES), shape(C, LANES)], [],
        exchange_rows(sent), wa, wb,
    )
    back = exchange_rows(sent)
    share = call(k_share, "share", shape(NB, 2 * C + 8, LANES), [], back, u, g)
    share = lax.all_to_all(share, "batch", 0, 0, tiled=True)
    grad_input = call(
        k_input, "input_grad", shape(C, XY, N, dtype=bf16),
        [cells_low, twice, cells, pltpu.SemaphoreType.DMA((XY // 32,))],
        back, dpre, kron, hi, lo, offset, synth, hbm_out=(0,),
    )
    spec, skip, b, inner, outer = call(
        k_shared, "shared",
        [shape(2, C, ML, 2, C), shape(C, C), shape(8, LANES), shape(C, C), shape(C, C)],
        [pltpu.VMEM((256, LANES), f32)] * 2, share,
    )
    spec = spec.transpose(0, 1, 4, 2, 3).reshape(2, C, C, 1, ML, 2)
    return (grad_input.reshape(1, C, XL, YL, N), spec, skip, b[0, :C], inner, outer)


def solution(mesh):
    placed = (
        P("batch", None, "px", "py", None),
        P("batch", None, "px", "py", None),
        P(None, None, None, "py", "px", None),
        P(),
        P(),
        P(),
        P(),
    )
    return jax.shard_map(
        shards,
        mesh=mesh,
        in_specs=placed,
        out_specs=(
            P("batch", None, "px", "py", None),
            P(None, None, None, "py", "px", "batch"),
            P(),
            P(),
            P(),
            P(),
        ),
        check_vma=False,
    )
```

```python
import math

import jax
import jax.numpy as jnp
import ml_dtypes
import numpy as np
from jax import lax
from jax.experimental import pallas as pl
from jax.experimental.pallas import tpu as pltpu
from jax.sharding import PartitionSpec as P

f32 = jnp.float32
bf16 = jnp.bfloat16
C = 16
N = 128
PX, PY, NB = 4, 16, 8
XL, YL = N // PX, N // PY
XY = XL * YL
ML = C // PX
PEERS = PX * PY
ROWS = C + 1
LANES = 128
SIGMA = 1.0 / math.sqrt(N**3)
RHO = 1.0 / math.sqrt(NB * N**3)
NT = (((1,), (1,)), ((), ()))


def tables():
    turn = lambda r, n: 2.0 * np.pi * (np.mod(r, n) / n)
    freq = np.where(np.arange(C) < C // 2, np.arange(C), np.arange(C) - C)
    depth = turn(np.arange(C)[:, None] * np.arange(N)[None, :], N)
    cos_z, sin_z = np.cos(depth), np.sin(depth)
    low = np.concatenate([cos_z, -sin_z]).astype(ml_dtypes.bfloat16)
    ax = turn(np.arange(XL)[:, None] * freq[None, :], N)
    ay = turn(np.arange(YL)[:, None] * freq[None, :], N)
    phase = ax[:, None, None, :] + ay[None, :, :, None]
    phase = phase.reshape(XY, PX, ML * C)
    co, si = np.cos(phase), np.sin(phase)
    plane = np.stack([co, -si], axis=2).reshape(XY, PX * LANES)
    plane_hi = plane.astype(ml_dtypes.bfloat16)
    plane_lo = (plane - plane_hi.astype(np.float64)).astype(ml_dtypes.bfloat16)
    ox = turn(np.arange(PX)[:, None] * XL * freq[None, :], N)
    oy = turn(np.arange(PY)[:, None] * YL * freq[None, :], N)
    off = ox[:, None, None, :] + oy[None, :, :, None]
    off = off.reshape(PEERS, PX, ML * C)
    cs = np.concatenate([np.cos(off), np.cos(off)], axis=2)
    sn = np.concatenate([np.sin(off), np.sin(off)], axis=2)
    offset = (np.concatenate([cs, sn], axis=1) * SIGMA).astype(np.float32)
    eye = np.eye(8)
    synth = np.concatenate(
        [
            np.einsum("ab,kz->akbz", eye, cos_z).reshape(8 * C, 8 * N),
            np.einsum("ab,kz->akbz", eye, -sin_z).reshape(8 * C, 8 * N),
        ]
    ).astype(ml_dtypes.bfloat16)
    return low, plane_hi, plane_lo, offset, synth


def dot(a, b):
    return jnp.dot(a, b, preferred_element_type=f32)


def dot_nt(a, b):
    return lax.dot_general(a, b, NT, preferred_element_type=f32)


def split(a):
    hi = a.astype(bf16)
    return hi, (a - hi.astype(f32)).astype(bf16)


def halves():
    lane = lax.broadcasted_iota(jnp.int32, (1, LANES), 1)
    return jnp.where(lane < LANES // 2, -1.0, 1.0)


def turned(v):
    return halves() * pltpu.roll(v, LANES // 2, 1)


def my_place():
    return lax.axis_index("px") * PY + lax.axis_index("py")


def forward_part(get, low_ref, hi_ref, lo_ref, off_ref, turn_ref, put, ready=None):
    low = low_ref[...]
    rows = [dot_nt(low, get(c)) for c in range(C)]
    both = jnp.concatenate([r[:C] for r in rows] + [r[C:] for r in rows], axis=0)
    x_hi, x_lo = split(both)
    if ready is not None:
        ready()
    hi = hi_ref[...]
    part = dot(x_hi, hi) + dot(x_lo, hi) + dot(x_hi, lo_ref[...])
    for mb in range(PX):
        pa = part[: C * C, mb * LANES : (mb + 1) * LANES]
        pb = part[C * C :, mb * LANES : (mb + 1) * LANES]
        co, si = off_ref[mb : mb + 1, :], off_ref[PX + mb : PX + mb + 1, :]
        turn_ref[mb] = (pa * co + pb * si) + turned(pb * co - pa * si)
    for mb in range(PX):
        for k in range(C):
            put(mb * PY + k, turn_ref[mb, pl.ds(k, C, stride=C), :])


def inverse_part(block, hi_ref, lo_ref, off_ref, synth_ref, turn_ref, g_ref):
    for mb in range(PX):
        v = jnp.concatenate([block(mb * PY + k) for k in range(PY)], axis=0)
        r = turned(v)
        co, si = off_ref[mb : mb + 1, :], off_ref[PX + mb : PX + mb + 1, :]
        turn_ref[mb] = v * co + r * si
        turn_ref[PX + mb] = v * si - r * co
    rows = []
    for half in range(2):
        for o in range(C):
            rows.append(
                jnp.concatenate(
                    [turn_ref[half * PX + mb, pl.ds(o, C, stride=C), :] for mb in range(PX)], axis=1
                )
            )
    v_hi, v_lo = split(jnp.concatenate(rows, axis=0))
    hi = hi_ref[...]
    z = dot_nt(hi, v_hi) + dot_nt(hi, v_lo) + dot_nt(lo_ref[...], v_hi)
    z = z.astype(bf16)
    for ob in range(2):
        re = z[:, ob * LANES : (ob + 1) * LANES]
        im = z[:, C * C + ob * LANES : C * C + (ob + 1) * LANES]
        g = dot(jnp.concatenate([re, im], axis=1), synth_ref[...])
        for o in range(8):
            g_ref[ob * 8 + o] = g[:, o * N : (o + 1) * N]


def k_forward(
    field_hbm, low_hbm, hi_hbm, lo_hbm, offset_hbm, out_ref,
    field_ref, low_ref, hi_ref, lo_ref, off_ref, turn_ref, sems,
):
    pairs = [(low_hbm, low_ref)]
    for i in range(4):
        part = pl.ds(4 * i, 4)
        pairs.append((field_hbm.at[part], field_ref.at[part]))
    pairs += [(hi_hbm, hi_ref), (lo_hbm, lo_ref), (offset_hbm.at[my_place()], off_ref)]
    copies = [pltpu.make_async_copy(a, b, sems.at[i]) for i, (a, b) in enumerate(pairs)]
    for copy in copies:
        copy.start()
    copies[0].wait()

    def get(c):
        if c % 4 == 0:
            copies[1 + c // 4].wait()
        return field_ref[c]

    def ready():
        for copy in copies[5:]:
            copy.wait()

    def put(d, value):
        out_ref[d] = value

    forward_part(get, low_ref, hi_ref, lo_ref, off_ref, turn_ref, put, ready)


def spread_map(w, transpose):
    r = lax.broadcasted_iota(jnp.int32, (256, C), 0)
    l = lax.broadcasted_iota(jnp.int32, (256, C), 1)
    rep = jnp.where(r // 16 == l, 1.0, 0.0).astype(bf16)
    if transpose:
        wide = lax.dot_general(w, rep, (((0,), (1,)), ((), ())), preferred_element_type=f32)
    else:
        wide = dot_nt(w, rep)
    full = dot(rep, wide.astype(bf16))
    r = lax.broadcasted_iota(jnp.int32, (256, 256), 0)
    l = lax.broadcasted_iota(jnp.int32, (256, 256), 1)
    return jnp.where(r % 16 == l % 16, full, 0.0).astype(bf16)


def k_prepare(
    skip_ref, in_ref, outer_ref, bias_in_ref, field_hbm, cot_hbm,
    kron_ref, pre_ref, dact_ref, field_ref, cot_ref, sems,
):
    copies = [
        pltpu.make_async_copy(field_hbm, field_ref, sems.at[0]),
        pltpu.make_async_copy(cot_hbm, cot_ref, sems.at[1]),
    ]
    for copy in copies:
        copy.start()
    skip = spread_map(skip_ref[...], False)
    outer = spread_map(outer_ref[...], True)
    kron_ref[0] = spread_map(in_ref[...], False)
    kron_ref[1] = spread_map(in_ref[...], True)
    kron_ref[2] = spread_map(skip_ref[...], True)
    r = lax.broadcasted_iota(jnp.int32, (256, C), 0)
    l = lax.broadcasted_iota(jnp.int32, (256, C), 1)
    bias = jnp.sum(jnp.where(r // 16 == l, bias_in_ref[...], 0.0), axis=1, keepdims=True)
    for copy in copies:
        copy.wait()

    def step(p, carry):
        untile(pre_ref, p, dot(skip, tile(field_ref, p)) + bias)
        untile(dact_ref, p, dot(outer, tile(cot_ref, p)))
        return carry

    lax.fori_loop(0, XY // 32, step, 0, unroll=2)


def k_mix(recv_ref, wa_ref, wb_ref, u_ref, out_ref):
    u = jnp.sum(recv_ref[...], axis=0)
    us = pltpu.roll(u, LANES // 2, 1)
    u_ref[...] = u
    v = jnp.zeros((C, LANES), f32)
    for c in range(C):
        v = v + wa_ref[c] * u[c : c + 1, :] + wb_ref[c] * us[c : c + 1, :]
    out_ref[...] = jnp.broadcast_to(v[None], (PEERS, C, LANES))


def gelu_parts(x):
    a = math.sqrt(2.0 / math.pi)
    b = a * 0.044715
    x2 = x * x
    h = 0.5 * jnp.tanh(x * (a + b * x2)) + 0.5
    g = x * h
    d = h + g * (1.0 - h) * (2.0 * a + (6.0 * b) * x2)
    return g, d


def tile(ref, p):
    left = ref[:, pl.ds(p * 32, 16), :].reshape(C * 16, N)
    right = ref[:, pl.ds(p * 32 + 16, 16), :].reshape(C * 16, N)
    return jnp.concatenate([left, right], axis=1)


def untile(ref, p, value):
    ref[:, pl.ds(p * 32, 16), :] = value[:, :N].reshape(C, 16, N)
    ref[:, pl.ds(p * 32 + 16, 16), :] = value[:, N:].reshape(C, 16, N)


def pack_rows(acc):
    r = lax.broadcasted_iota(jnp.int32, (256, 256), 0)
    l = lax.broadcasted_iota(jnp.int32, (256, 256), 1)
    kept = jnp.where(r % 16 == l % 16, acc, 0.0).reshape(C, 16, 256).sum(axis=1)
    r = lax.broadcasted_iota(jnp.int32, (256, LANES), 0)
    l = lax.broadcasted_iota(jnp.int32, (256, LANES), 1)
    pick = jnp.where(r // 16 == l % 16, 1.0, 0.0)
    spread = jnp.dot(kept, pick, precision=lax.Precision.HIGHEST, preferred_element_type=f32)
    r = lax.broadcasted_iota(jnp.int32, (C, LANES), 0)
    l = lax.broadcasted_iota(jnp.int32, (C, LANES), 1)
    return jnp.where(r % 8 == l // 16, spread, 0.0)


def k_middle(
    recv_ref, field_ref, cot_ref, pre_ref, dact_ref, kron_ref, low_ref, hi_ref, lo_ref, offset_ref, synth_ref,
    out_ref, dpre_hbm,
    dpre_ref, sems, turn_ref, g_ref, skip_acc, bias_acc, in_acc, out_acc,
):
    off_ref = offset_ref.at[my_place()]
    inverse_part(lambda d: recv_ref[d], hi_ref, lo_ref, off_ref, synth_ref, turn_ref, g_ref)
    skip_acc[...] = jnp.zeros_like(skip_acc)
    in_acc[...] = jnp.zeros_like(in_acc)
    out_acc[...] = jnp.zeros_like(out_acc)
    bias_acc[...] = jnp.zeros_like(bias_acc)

    def step(p, carry):
        f = tile(field_ref, p)
        cot = tile(cot_ref, p)
        pre = tile(g_ref, p) + tile(pre_ref, p)
        hid, d_hid = gelu_parts(pre)
        hid = hid.astype(bf16)
        act, d_act = gelu_parts(dot(kron_ref[0], hid))
        act = act.astype(bf16)
        d_inner = (tile(dact_ref, p) * d_act).astype(bf16)
        dpre = dot(kron_ref[1], d_inner) * d_hid
        dpre = dpre.astype(bf16)
        untile(dpre_ref, p, dpre)
        skip_acc[...] += dot_nt(dpre, f)
        in_acc[...] += dot_nt(d_inner, hid)
        out_acc[...] += dot_nt(cot, act)
        bias_acc[...] += dpre.astype(f32)
        return carry

    lax.fori_loop(0, XY // 32, step, 0, unroll=XY // 32)
    copy = pltpu.make_async_copy(dpre_ref, dpre_hbm, sems.at[0])
    copy.start()
    bias = bias_acc[...].reshape(C, 16, 256).sum(axis=1)
    total = jnp.sum(bias, axis=1, keepdims=True)
    r = lax.broadcasted_iota(jnp.int32, (C, LANES), 0)
    l = lax.broadcasted_iota(jnp.int32, (C, LANES), 1)
    bias_row = jnp.sum(jnp.where(r == l, total, 0.0), axis=0, keepdims=True)
    small = jnp.concatenate(
        [pack_rows(skip_acc[...]), pack_rows(in_acc[...]), pack_rows(out_acc[...]),
         bias_row, jnp.zeros((C - 1, LANES), f32)], axis=0
    )

    def put(d, value):
        out_ref[d * ROWS : (d + 1) * ROWS, :] = jnp.concatenate([value, small[d : d + 1]], axis=0)

    forward_part(lambda c: dpre_ref[c], low_ref, hi_ref, lo_ref, off_ref, turn_ref, put)
    copy.wait()


def k_mix_back(recv_ref, wa_ref, wb_ref, out_ref, g_ref):
    slabs = recv_ref[...].reshape(8, 8 * ROWS, LANES).sum(axis=0)
    got = slabs[:ROWS]
    for i in range(1, 8):
        got = got + slabs[i * ROWS : (i + 1) * ROWS]
    g = got[:C]
    g_ref[...] = g
    gs = pltpu.roll(g, LANES // 2, 1)
    rows = []
    for c in range(C):
        rows.append(jnp.sum(wa_ref[c] * g - wb_ref[c] * gs, axis=0, keepdims=True))
    block = jnp.concatenate(rows + [got[C:]], axis=0)
    slab = jnp.concatenate([block] * 8, axis=0)
    for i in range(8):
        out_ref[i * 8 * ROWS : (i + 1) * 8 * ROWS, :] = slab


def k_share(back_ref, u_ref, g_ref, share_ref):
    small = back_ref[pl.ds(C, PEERS, stride=ROWS), :].reshape(8, 8, LANES).sum(axis=1)
    share = jnp.concatenate([u_ref[...], g_ref[...], small], axis=0)
    share_ref[...] = jnp.broadcast_to(share[None], (NB, 2 * C + 8, LANES))


def k_input(
    recv_ref, dpre_ref, kron_ref, hi_ref, lo_ref, offset_ref, synth_ref, out_hbm,
    out_ref, turn_ref, g_ref, sems,
):
    off_ref = offset_ref.at[my_place()]
    inverse_part(
        lambda d: recv_ref[d * ROWS : d * ROWS + C, :],
        hi_ref, lo_ref, off_ref, synth_ref, turn_ref, g_ref,
    )
    steps = XY // 32
    copies = []
    for p in range(steps):
        untile(out_ref, p, (dot(kron_ref[2], tile(dpre_ref, p)) + tile(g_ref, p)).astype(bf16))
        part = pl.ds(p * 32, 32)
        copies.append(pltpu.make_async_copy(out_ref.at[:, part], out_hbm.at[:, part], sems.at[p]))
        copies[-1].start()
    for copy in copies:
        copy.wait()


def k_shared(recv_ref, spec_ref, skip_ref, bias_ref, in_ref, outer_ref, pa_ref, pb_ref):
    for c in range(C):
        pa = jnp.zeros((C, LANES), f32)
        pb = jnp.zeros((C, LANES), f32)
        for s in range(NB):
            u = recv_ref[s, c : c + 1, :]
            g = recv_ref[s, C : 2 * C, :]
            pa = pa + u * g
            pb = pb + u * pltpu.roll(g, LANES // 2, 1)
        pa_ref[c * C : (c + 1) * C, :] = pa
        pb_ref[c * C : (c + 1) * C, :] = pb
    b = lax.axis_index("batch")
    r = lax.broadcasted_iota(jnp.int32, (8, LANES), 0)
    l = lax.broadcasted_iota(jnp.int32, (8, LANES), 1)
    mine = ((l % 64) // C == r // 2) & (l % C == 2 * b + r % 2)
    sel_a = jnp.where(mine, 1.0, 0.0)
    sel_b = jnp.where(l < 64, sel_a, -sel_a)
    full = lambda x, y: lax.dot_general(
        x, y, NT, precision=lax.Precision.HIGHEST, preferred_element_type=f32
    )
    for i, part in enumerate((full(sel_a, pa_ref[...]), full(sel_b, pb_ref[...]))):
        for c in range(C):
            for m in range(ML):
                spec_ref[i, c, m] = part[2 * m : 2 * m + 2, c * C : (c + 1) * C]
    small = jnp.sum(recv_ref[:, 2 * C :, :], axis=0) * RHO
    r = lax.broadcasted_iota(jnp.int32, (C, LANES), 0)
    l = lax.broadcasted_iota(jnp.int32, (C, LANES), 1)
    pr = lax.broadcasted_iota(jnp.int32, (LANES, C), 0)
    pc = lax.broadcasted_iota(jnp.int32, (LANES, C), 1)
    pick = jnp.where(pr % C == pc, 1.0, 0.0)
    for i, ref in enumerate((skip_ref, in_ref, outer_ref)):
        two = jnp.concatenate(
            [jnp.broadcast_to(small[2 * i + h : 2 * i + h + 1], (8, LANES)) for h in range(2)], axis=0
        )
        two = jnp.where(l // C == r % 8, two, 0.0)
        ref[...] = jnp.dot(two, pick, precision=lax.Precision.HIGHEST, preferred_element_type=f32)
    bias_ref[...] = small[6, :C]


def call(body, name, outs, scratch, *args, hbm_in=(), vmem_in=(), hbm_out=()):
    vm = pl.BlockSpec(memory_space=pltpu.VMEM)
    hbm = pl.BlockSpec(memory_space=pltpu.HBM)
    many = isinstance(outs, (list, tuple))
    out_specs = [hbm if i in hbm_out else vm for i in range(len(outs) if many else 1)]
    args = [
        pltpu.with_memory_space_constraint(a, pltpu.HBM) if i in hbm_in
        else pltpu.with_memory_space_constraint(a, pltpu.VMEM) if i in vmem_in
        else a
        for i, a in enumerate(args)
    ]
    return pl.pallas_call(
        body,
        out_shape=outs,
        in_specs=[hbm if i in hbm_in else vm for i in range(len(args))],
        out_specs=out_specs if many else out_specs[0],
        scratch_shapes=scratch,
        compiler_params=pltpu.CompilerParams(vmem_limit_bytes=32 * 2**20),
        name=name,
    )(*args)


def shape(*dims, dtype=f32):
    return jax.ShapeDtypeStruct(dims, dtype)


def run_prepare(skip_weight, mlp_in, mlp_out, skip_bias, field, cotangent):
    return call(
        k_prepare, "prepare",
        [pltpu.VMEM((3, 256, 256), bf16), pltpu.VMEM((C, XY, N), f32), pltpu.VMEM((C, XY, N), f32),
         pltpu.VMEM((C, XY, N), bf16), pltpu.VMEM((C, XY, N), bf16)],
        [pltpu.SemaphoreType.DMA((2,))],
        skip_weight, mlp_in, mlp_out, skip_bias.reshape(1, C), field, cotangent, hbm_in=(4, 5),
    )


def run_middle(recv, field, cotangent, pre, dact, kron, low, hi, lo, offset, synth):
    turn = pltpu.VMEM((2 * PX, PY * C, LANES), f32)
    cells = pltpu.VMEM((C, XY, N), f32)
    square = pltpu.VMEM((256, 256), f32)
    return call(
        k_middle, "middle",
        [pltpu.VMEM((PEERS * ROWS, LANES), f32), pltpu.HBM((C, XY, N), bf16)],
        [pltpu.VMEM((C, XY, N), bf16), pltpu.SemaphoreType.DMA((1,)),
         turn, cells, square, square, square, square],
        recv, field, cotangent, pre, dact, kron, low, hi, lo, offset, synth,
        hbm_out=(1,), vmem_in=(1, 2, 3, 4, 5),
    )


def shards(field, cotangent, spec_weight, skip_weight, skip_bias, mlp_in, mlp_out):
    low, hi, lo, offset, synth = [jnp.asarray(t) for t in tables()]
    field = field.reshape(C, XY, N)
    cotangent = cotangent.reshape(C, XY, N)
    weight = spec_weight.reshape(2, C, C, ML * C)
    wa = jnp.concatenate([weight[0], weight[0]], axis=2)
    wb = jnp.concatenate([-weight[1], weight[1]], axis=2)
    turn = pltpu.VMEM((PX, PY * C, LANES), f32)
    twice = pltpu.VMEM((2 * PX, PY * C, LANES), f32)
    cells = pltpu.VMEM((C, XY, N), f32)
    cells_low = pltpu.VMEM((C, XY, N), bf16)
    own = pltpu.VMEM((8, LANES), f32)
    plane = pltpu.VMEM((XY, PX * LANES), bf16)

    def exchange(block):
        return lax.all_to_all(block, ("px", "py"), 0, 0, tiled=True)

    def exchange_rows(block):
        return exchange(block.reshape(PEERS, 1, ROWS * LANES)).reshape(PEERS * ROWS, LANES)

    sent = call(
        k_forward, "forward", pltpu.VMEM((PEERS, C, LANES), f32),
        [cells_low, pltpu.VMEM((2 * C, N), bf16), plane, plane, own, turn, pltpu.SemaphoreType.DMA((8,))],
        field, low, hi, lo, offset, hbm_in=range(5),
    )
    kron, pre, dact, field, cotangent = run_prepare(
        skip_weight, mlp_in, mlp_out, skip_bias, field, cotangent
    )
    u, sent = call(
        k_mix, "mix", [shape(C, LANES), pltpu.VMEM((PEERS, C, LANES), f32)], [],
        exchange(sent), wa, wb, vmem_in=(1, 2),
    )
    sent, dpre = run_middle(
        exchange(sent), field, cotangent, pre, dact, kron, low, hi, lo, offset, synth
    )
    sent, g = call(
        k_mix_back, "mix_back", [pltpu.VMEM((PEERS * ROWS, LANES), f32), shape(C, LANES)], [],
        exchange_rows(sent), wa, wb, vmem_in=(1, 2),
    )
    back = exchange_rows(sent)
    share = call(k_share, "share", shape(NB, 2 * C + 8, LANES), [], back, u, g)
    share = lax.all_to_all(share, "batch", 0, 0, tiled=True)
    grad_input = call(
        k_input, "input_grad", shape(C, XY, N, dtype=bf16),
        [cells_low, twice, cells, pltpu.SemaphoreType.DMA((XY // 32,))],
        back, dpre, kron, hi, lo, offset, synth, hbm_out=(0,),
    )
    spec, skip, b, inner, outer = call(
        k_shared, "shared",
        [shape(2, C, ML, 2, C), shape(C, C), shape(C), shape(C, C), shape(C, C)],
        [pltpu.VMEM((256, LANES), f32)] * 2, share,
    )
    spec = spec.transpose(0, 1, 4, 2, 3).reshape(2, C, C, 1, ML, 2)
    return (grad_input.reshape(1, C, XL, YL, N), spec, skip, b, inner, outer)


def solution(mesh):
    placed = (
        P("batch", None, "px", "py", None),
        P("batch", None, "px", "py", None),
        P(None, None, None, "py", "px", None),
        P(),
        P(),
        P(),
        P(),
    )
    return jax.shard_map(
        shards,
        mesh=mesh,
        in_specs=placed,
        out_specs=(
            P("batch", None, "px", "py", None),
            P(None, None, None, "py", "px", "batch"),
            P(),
            P(),
            P(),
            P(),
        ),
        check_vma=False,
    )
```

```python
import math

import jax
import jax.numpy as jnp
import ml_dtypes
import numpy as np
from jax import lax
from jax.experimental import pallas as pl
from jax.experimental.pallas import tpu as pltpu
from jax.sharding import PartitionSpec as P

f32 = jnp.float32
bf16 = jnp.bfloat16
C = 16
N = 128
PX, PY, NB = 4, 16, 8
XL, YL = N // PX, N // PY
XY = XL * YL
ML = C // PX
PEERS = PX * PY
STEPS = XY // 32
HALF = XY // 2
ROWS = C + 1
LANES = 128
SIGMA = 1.0 / math.sqrt(N**3)
RHO = 1.0 / math.sqrt(NB * N**3)
KEPT = f32
NT = (((1,), (1,)), ((), ()))


def tables():
    turn = lambda r, n: 2.0 * np.pi * (np.mod(r, n) / n)
    freq = np.where(np.arange(C) < C // 2, np.arange(C), np.arange(C) - C)
    depth = turn(np.arange(C)[:, None] * np.arange(N)[None, :], N)
    cos_z, sin_z = np.cos(depth), np.sin(depth)
    low = np.concatenate([cos_z, -sin_z]).astype(ml_dtypes.bfloat16)
    ax = turn(np.arange(XL)[:, None] * freq[None, :], N)
    ay = turn(np.arange(YL)[:, None] * freq[None, :], N)
    phase = ax[:, None, None, :] + ay[None, :, :, None]
    phase = phase.reshape(XY, PX, ML * C)
    co, si = np.cos(phase), np.sin(phase)
    plane = np.stack([co, -si], axis=2).reshape(XY, PX * LANES)
    plane_hi = plane.astype(ml_dtypes.bfloat16)
    plane_lo = (plane - plane_hi.astype(np.float64)).astype(ml_dtypes.bfloat16)
    ox = turn(np.arange(PX)[:, None] * XL * freq[None, :], N)
    oy = turn(np.arange(PY)[:, None] * YL * freq[None, :], N)
    off = ox[:, None, None, :] + oy[None, :, :, None]
    off = off.reshape(PEERS, PX, ML * C)
    cs = np.concatenate([np.cos(off), np.cos(off)], axis=2)
    sn = np.concatenate([np.sin(off), np.sin(off)], axis=2)
    offset = (np.concatenate([cs, sn], axis=1) * SIGMA).astype(np.float32)
    eye = np.eye(8)
    synth = np.concatenate(
        [
            np.einsum("ab,kz->akbz", eye, cos_z).reshape(8 * C, 8 * N),
            np.einsum("ab,kz->akbz", eye, -sin_z).reshape(8 * C, 8 * N),
        ]
    ).astype(ml_dtypes.bfloat16)
    low = np.pad(low.astype(np.float32), ((0, 0), (0, PX * LANES - N))).astype(ml_dtypes.bfloat16)
    table = np.concatenate([plane_hi, plane_lo, synth[:, : 4 * N], synth[:, 4 * N :], low])
    return table, offset


class Table:
    def __init__(self, ref):
        self.hi = ref.at[0:XY, :]
        self.lo = ref.at[XY : 2 * XY, :]
        self.synth = [ref.at[2 * XY : 3 * XY, :], ref.at[3 * XY : 4 * XY, :]]
        self.low = ref.at[4 * XY : 4 * XY + 2 * C, 0:N]


def dot(a, b):
    return jnp.dot(a, b, preferred_element_type=f32)


def dot_nt(a, b):
    return lax.dot_general(a, b, NT, preferred_element_type=f32)


def split(a):
    hi = a.astype(bf16)
    return hi, (a - hi.astype(f32)).astype(bf16)


def halves():
    lane = lax.broadcasted_iota(jnp.int32, (1, LANES), 1)
    return jnp.where(lane < LANES // 2, -1.0, 1.0)


def turned(v):
    return halves() * pltpu.roll(v, LANES // 2, 1)


def my_place():
    return lax.axis_index("px") * PY + lax.axis_index("py")


def forward_part(get, table, off_ref, turn_ref, put, ready=None):
    low = table.low[...]
    rows = [dot_nt(low, get(c)) for c in range(C)]
    both = jnp.concatenate([r[:C] for r in rows] + [r[C:] for r in rows], axis=0)
    x_hi, x_lo = split(both)
    if ready is not None:
        ready()
    hi = table.hi[...]
    part = dot(x_hi, hi) + dot(x_lo, hi) + dot(x_hi, table.lo[...])
    for mb in range(PX):
        pa = part[: C * C, mb * LANES : (mb + 1) * LANES]
        pb = part[C * C :, mb * LANES : (mb + 1) * LANES]
        co, si = off_ref[mb : mb + 1, :], off_ref[PX + mb : PX + mb + 1, :]
        turn_ref[mb] = (pa * co + pb * si) + turned(pb * co - pa * si)
    for mb in range(PX):
        for k in range(C):
            put(mb * PY + k, turn_ref[mb, pl.ds(k, C, stride=C), :])


def inverse_part(block, table, off_ref, turn_ref, g_ref):
    for mb in range(PX):
        v = jnp.concatenate([block(mb * PY + k) for k in range(PY)], axis=0)
        r = turned(v)
        co, si = off_ref[mb : mb + 1, :], off_ref[PX + mb : PX + mb + 1, :]
        turn_ref[mb] = v * co + r * si
        turn_ref[PX + mb] = v * si - r * co
    rows = []
    for half in range(2):
        for o in range(C):
            rows.append(
                jnp.concatenate(
                    [turn_ref[half * PX + mb, pl.ds(o, C, stride=C), :] for mb in range(PX)], axis=1
                )
            )
    v_hi, v_lo = split(jnp.concatenate(rows, axis=0))
    hi = table.hi[...]
    z = dot_nt(hi, v_hi) + dot_nt(hi, v_lo) + dot_nt(table.lo[...], v_hi)
    z = z.astype(bf16)
    for ob in range(2):
        re = z[:, ob * LANES : (ob + 1) * LANES]
        im = z[:, C * C + ob * LANES : C * C + (ob + 1) * LANES]
        both = jnp.concatenate([re, im], axis=1)
        for half in range(2):
            g = dot(both, table.synth[half][...])
            for o in range(4):
                g_ref[ob * 8 + half * 4 + o] = g[:, o * N : (o + 1) * N]


def k_forward(field_hbm, table_hbm, offset_hbm, out_ref, field_ref, table_ref, off_ref, turn_ref, sems):
    low_rows, plane_rows = pl.ds(4 * XY, 2 * C), pl.ds(0, 2 * XY)
    pairs = [(table_hbm.at[low_rows], table_ref.at[low_rows])]
    for i in range(4):
        part = pl.ds(4 * i, 4)
        pairs.append((field_hbm.at[part], field_ref.at[part]))
    pairs.append((table_hbm.at[plane_rows], table_ref.at[plane_rows]))
    pairs.append((offset_hbm.at[my_place()], off_ref))
    copies = [pltpu.make_async_copy(a, b, sems.at[i]) for i, (a, b) in enumerate(pairs)]
    for copy in copies:
        copy.start()
    copies[0].wait()

    def get(c):
        if c % 4 == 0:
            copies[1 + c // 4].wait()
        return field_ref[c]

    def ready():
        for copy in copies[5:]:
            copy.wait()

    def put(d, value):
        out_ref[d] = value

    forward_part(get, Table(table_ref), off_ref, turn_ref, put, ready)


def spread_map(w, transpose):
    r = lax.broadcasted_iota(jnp.int32, (256, C), 0)
    l = lax.broadcasted_iota(jnp.int32, (256, C), 1)
    rep = jnp.where(r // 16 == l, 1.0, 0.0).astype(bf16)
    if transpose:
        wide = lax.dot_general(w, rep, (((0,), (1,)), ((), ())), preferred_element_type=f32)
    else:
        wide = dot_nt(w, rep)
    full = dot(rep, wide.astype(bf16))
    r = lax.broadcasted_iota(jnp.int32, (256, 256), 0)
    l = lax.broadcasted_iota(jnp.int32, (256, 256), 1)
    return jnp.where(r % 16 == l % 16, full, 0.0).astype(bf16)


def k_prepare(
    skip_ref, in_ref, outer_ref, bias_in_ref, field_hbm, cot_hbm,
    kron_ref, pre_hbm, dact_hbm, field_ref, cot_ref, pre_ref, dact_ref, sems,
):
    copies = [
        pltpu.make_async_copy(field_hbm, field_ref, sems.at[0]),
        pltpu.make_async_copy(cot_hbm, cot_ref, sems.at[1]),
    ]
    for copy in copies:
        copy.start()
    skip = spread_map(skip_ref[...], False)
    outer = spread_map(outer_ref[...], True)
    kron_ref[0] = spread_map(in_ref[...], False)
    kron_ref[1] = spread_map(in_ref[...], True)
    kron_ref[2] = spread_map(skip_ref[...], True)
    r = lax.broadcasted_iota(jnp.int32, (256, C), 0)
    l = lax.broadcasted_iota(jnp.int32, (256, C), 1)
    bias = jnp.sum(jnp.where(r // 16 == l, bias_in_ref[...], 0.0), axis=1, keepdims=True)
    for copy in copies:
        copy.wait()

    def step(p, carry):
        untile(pre_ref, p, (dot(skip, tile(field_ref, p)) + bias).astype(KEPT))
        untile(dact_ref, p, dot(outer, tile(cot_ref, p)).astype(KEPT))
        return carry

    lax.fori_loop(0, STEPS, step, 0, unroll=2)
    copies = [
        pltpu.make_async_copy(pre_ref, pre_hbm, sems.at[0]),
        pltpu.make_async_copy(dact_ref, dact_hbm, sems.at[1]),
    ]
    for copy in copies:
        copy.start()
    for copy in copies:
        copy.wait()


def k_mix(recv_ref, wa_ref, wb_ref, u_ref, out_hbm, eight_ref, sems):
    u = jnp.sum(recv_ref[...], axis=0)
    us = pltpu.roll(u, LANES // 2, 1)
    u_ref[...] = u
    v = jnp.zeros((C, LANES), f32)
    for c in range(C):
        v = v + wa_ref[c] * u[c : c + 1, :] + wb_ref[c] * us[c : c + 1, :]
    eight_ref[...] = jnp.broadcast_to(v[None], (8, C, LANES))
    copies = [
        pltpu.make_async_copy(eight_ref, out_hbm.at[pl.ds(8 * i, 8)], sems.at[i])
        for i in range(PEERS // 8)
    ]
    for copy in copies:
        copy.start()
    for copy in copies:
        copy.wait()


def gelu_parts(x):
    a = math.sqrt(2.0 / math.pi)
    b = a * 0.044715
    x2 = x * x
    h = 0.5 * jnp.tanh(x * (a + b * x2)) + 0.5
    g = x * h
    d = h + g * (1.0 - h) * (2.0 * a + (6.0 * b) * x2)
    return g, d


def tile(ref, p):
    left = ref[:, pl.ds(p * 32, 16), :].reshape(C * 16, N)
    right = ref[:, pl.ds(p * 32 + 16, 16), :].reshape(C * 16, N)
    return jnp.concatenate([left, right], axis=1)


def untile(ref, p, value):
    ref[:, pl.ds(p * 32, 16), :] = value[:, :N].reshape(C, 16, N)
    ref[:, pl.ds(p * 32 + 16, 16), :] = value[:, N:].reshape(C, 16, N)


def pack_rows(acc):
    r = lax.broadcasted_iota(jnp.int32, (256, 256), 0)
    l = lax.broadcasted_iota(jnp.int32, (256, 256), 1)
    kept = jnp.where(r % 16 == l % 16, acc, 0.0).reshape(C, 16, 256).sum(axis=1)
    r = lax.broadcasted_iota(jnp.int32, (256, LANES), 0)
    l = lax.broadcasted_iota(jnp.int32, (256, LANES), 1)
    pick = jnp.where(r // 16 == l % 16, 1.0, 0.0)
    spread = jnp.dot(kept, pick, precision=lax.Precision.HIGHEST, preferred_element_type=f32)
    r = lax.broadcasted_iota(jnp.int32, (C, LANES), 0)
    l = lax.broadcasted_iota(jnp.int32, (C, LANES), 1)
    return jnp.where(r % 8 == l // 16, spread, 0.0)


def k_middle(
    recv_ref, field_ref, cot_ref, pre_hbm, dact_hbm, kron_hbm, table_ref, offset_ref,
    out_ref, dpre_hbm,
    pre_ref, dact_ref, kron_ref, dpre_ref, sems, turn_ref, g_ref, skip_acc, bias_acc, in_acc, out_acc,
):
    pairs = [(kron_hbm.at[0:2], kron_ref)]
    for i in range(2):
        part = pl.ds(i * HALF, HALF)
        pairs.append((pre_hbm.at[:, part], pre_ref.at[:, part]))
        pairs.append((dact_hbm.at[:, part], dact_ref.at[:, part]))
    copies = [pltpu.make_async_copy(a, b, sems.at[i]) for i, (a, b) in enumerate(pairs)]
    for copy in copies:
        copy.start()
    off_ref = offset_ref.at[my_place()]
    table = Table(table_ref)
    inverse_part(lambda d: recv_ref[d], table, off_ref, turn_ref, g_ref)
    skip_acc[...] = jnp.zeros_like(skip_acc)
    in_acc[...] = jnp.zeros_like(in_acc)
    out_acc[...] = jnp.zeros_like(out_acc)
    bias_acc[...] = jnp.zeros_like(bias_acc)

    def step(p):
        f = tile(field_ref, p)
        cot = tile(cot_ref, p)
        pre = tile(g_ref, p) + tile(pre_ref, p)
        hid, d_hid = gelu_parts(pre)
        hid = hid.astype(bf16)
        act, d_act = gelu_parts(dot(kron_ref[0], hid))
        act = act.astype(bf16)
        d_inner = (tile(dact_ref, p) * d_act).astype(bf16)
        dpre = dot(kron_ref[1], d_inner) * d_hid
        dpre = dpre.astype(bf16)
        untile(dpre_ref, p, dpre)
        skip_acc[...] += dot_nt(dpre, f)
        in_acc[...] += dot_nt(d_inner, hid)
        out_acc[...] += dot_nt(cot, act)
        bias_acc[...] += dpre.astype(f32)

    copies[0].wait()
    for p in range(STEPS):
        if p % (STEPS // 2) == 0:
            copies[1 + 2 * (p // (STEPS // 2))].wait()
            copies[2 + 2 * (p // (STEPS // 2))].wait()
        step(p)
    copy = pltpu.make_async_copy(dpre_ref, dpre_hbm, sems.at[5])
    copy.start()
    bias = bias_acc[...].reshape(C, 16, 256).sum(axis=1)
    total = jnp.sum(bias, axis=1, keepdims=True)
    r = lax.broadcasted_iota(jnp.int32, (C, LANES), 0)
    l = lax.broadcasted_iota(jnp.int32, (C, LANES), 1)
    bias_row = jnp.sum(jnp.where(r == l, total, 0.0), axis=0, keepdims=True)
    small = jnp.concatenate(
        [pack_rows(skip_acc[...]), pack_rows(in_acc[...]), pack_rows(out_acc[...]),
         bias_row, jnp.zeros((C - 1, LANES), f32)], axis=0
    )

    def put(d, value):
        out_ref[d * ROWS : (d + 1) * ROWS, :] = jnp.concatenate([value, small[d : d + 1]], axis=0)

    forward_part(lambda c: dpre_ref[c], table, off_ref, turn_ref, put)
    copy.wait()


def k_mix_back(recv_ref, wa_ref, wb_ref, out_ref, g_ref):
    slabs = recv_ref[...].reshape(8, 8 * ROWS, LANES).sum(axis=0)
    got = slabs[:ROWS]
    for i in range(1, 8):
        got = got + slabs[i * ROWS : (i + 1) * ROWS]
    g = got[:C]
    g_ref[...] = g
    gs = pltpu.roll(g, LANES // 2, 1)
    rows = []
    for c in range(C):
        rows.append(jnp.sum(wa_ref[c] * g - wb_ref[c] * gs, axis=0, keepdims=True))
    block = jnp.concatenate(rows + [got[C:]], axis=0)
    slab = jnp.concatenate([block] * 8, axis=0)
    for i in range(8):
        out_ref[i * 8 * ROWS : (i + 1) * 8 * ROWS, :] = slab


def k_share(back_ref, u_ref, g_ref, share_hbm, block_ref, sems):
    small = back_ref[pl.ds(C, PEERS, stride=ROWS), :].reshape(8, 8, LANES).sum(axis=1)
    block_ref[...] = jnp.concatenate([u_ref[...], g_ref[...], small], axis=0)
    copies = [pltpu.make_async_copy(block_ref, share_hbm.at[i], sems.at[i]) for i in range(NB)]
    for copy in copies:
        copy.start()
    for copy in copies:
        copy.wait()


def k_input(
    recv_ref, dpre_ref, kron_ref, table_ref, offset_ref, out_hbm,
    out_ref, turn_ref, g_ref, sems,
):
    steps = XY // 32
    off_ref = offset_ref.at[my_place()]
    inverse_part(
        lambda d: recv_ref[d * ROWS : d * ROWS + C, :], Table(table_ref), off_ref, turn_ref, g_ref
    )
    copies = []
    for p in range(steps):
        untile(out_ref, p, (dot(kron_ref[2], tile(dpre_ref, p)) + tile(g_ref, p)).astype(bf16))
        part = pl.ds(p * 32, 32)
        copies.append(pltpu.make_async_copy(out_ref.at[:, part], out_hbm.at[:, part], sems.at[p]))
        copies[-1].start()
    for copy in copies:
        copy.wait()


def k_shared(recv_ref, spec_ref, skip_ref, bias_ref, in_ref, outer_ref, pa_ref, pb_ref):
    for c in range(C):
        pa = jnp.zeros((C, LANES), f32)
        pb = jnp.zeros((C, LANES), f32)
        for s in range(NB):
            u = recv_ref[s, c : c + 1, :]
            g = recv_ref[s, C : 2 * C, :]
            pa = pa + u * g
            pb = pb + u * pltpu.roll(g, LANES // 2, 1)
        pa_ref[c * C : (c + 1) * C, :] = pa
        pb_ref[c * C : (c + 1) * C, :] = pb
    b = lax.axis_index("batch")
    r = lax.broadcasted_iota(jnp.int32, (8, LANES), 0)
    l = lax.broadcasted_iota(jnp.int32, (8, LANES), 1)
    mine = ((l % 64) // C == r // 2) & (l % C == 2 * b + r % 2)
    sel_a = jnp.where(mine, 1.0, 0.0)
    sel_b = jnp.where(l < 64, sel_a, -sel_a)
    full = lambda x, y: lax.dot_general(
        x, y, NT, precision=lax.Precision.HIGHEST, preferred_element_type=f32
    )
    for i, part in enumerate((full(sel_a, pa_ref[...]), full(sel_b, pb_ref[...]))):
        for c in range(C):
            for m in range(ML):
                spec_ref[i, c, m] = part[2 * m : 2 * m + 2, c * C : (c + 1) * C]
    small = jnp.sum(recv_ref[:, 2 * C :, :], axis=0) * RHO
    r = lax.broadcasted_iota(jnp.int32, (C, LANES), 0)
    l = lax.broadcasted_iota(jnp.int32, (C, LANES), 1)
    pr = lax.broadcasted_iota(jnp.int32, (LANES, C), 0)
    pc = lax.broadcasted_iota(jnp.int32, (LANES, C), 1)
    pick = jnp.where(pr % C == pc, 1.0, 0.0)
    for i, ref in enumerate((skip_ref, in_ref, outer_ref)):
        two = jnp.concatenate(
            [jnp.broadcast_to(small[2 * i + h : 2 * i + h + 1], (8, LANES)) for h in range(2)], axis=0
        )
        two = jnp.where(l // C == r % 8, two, 0.0)
        ref[...] = jnp.dot(two, pick, precision=lax.Precision.HIGHEST, preferred_element_type=f32)
    bias_ref[...] = small[6, :C]


def call(body, name, outs, scratch, *args, hbm_in=(), vmem_in=(), hbm_out=()):
    vm = pl.BlockSpec(memory_space=pltpu.VMEM)
    hbm = pl.BlockSpec(memory_space=pltpu.HBM)
    many = isinstance(outs, (list, tuple))
    out_specs = [hbm if i in hbm_out else vm for i in range(len(outs) if many else 1)]
    args = [
        pltpu.with_memory_space_constraint(a, pltpu.HBM) if i in hbm_in
        else pltpu.with_memory_space_constraint(a, pltpu.VMEM) if i in vmem_in
        else a
        for i, a in enumerate(args)
    ]
    return pl.pallas_call(
        body,
        out_shape=outs,
        in_specs=[hbm if i in hbm_in else vm for i in range(len(args))],
        out_specs=out_specs if many else out_specs[0],
        scratch_shapes=scratch,
        compiler_params=pltpu.CompilerParams(vmem_limit_bytes=32 * 2**20),
        name=name,
    )(*args)


def shape(*dims, dtype=f32):
    return jax.ShapeDtypeStruct(dims, dtype)


CELLS = pltpu.VMEM((C, XY, N), f32)
CELLS_LOW = pltpu.VMEM((C, XY, N), bf16)
CELLS_KEPT = pltpu.VMEM((C, XY, N), KEPT)
OWN = pltpu.VMEM((8, LANES), f32)


def run_prepare(skip_weight, mlp_in, mlp_out, skip_bias, field, cotangent):
    return call(
        k_prepare, "prepare",
        [shape(3, 256, 256, dtype=bf16), pltpu.HBM((C, XY, N), KEPT), pltpu.HBM((C, XY, N), KEPT)],
        [CELLS_LOW, CELLS_LOW, CELLS_KEPT, CELLS_KEPT, pltpu.SemaphoreType.DMA((2,))],
        skip_weight, mlp_in, mlp_out, skip_bias.reshape(1, C), field, cotangent, hbm_in=(4, 5), hbm_out=(1, 2),
    )


def run_middle(recv, field, cotangent, pre, dact, kron, table, offset):
    turn = pltpu.VMEM((2 * PX, PY * C, LANES), f32)
    square = pltpu.VMEM((256, 256), f32)
    return call(
        k_middle, "middle",
        [shape(PEERS * ROWS, LANES), pltpu.HBM((C, XY, N), bf16)],
        [CELLS_KEPT, CELLS_KEPT, pltpu.VMEM((2, 256, 256), bf16), CELLS_LOW,
         pltpu.SemaphoreType.DMA((6,)), turn, CELLS, square, square, square, square],
        recv, field, cotangent, pre, dact, kron, table, offset, hbm_in=(3, 4, 5), hbm_out=(1,),
    )


def shards(field, cotangent, spec_weight, skip_weight, skip_bias, mlp_in, mlp_out):
    table, offset = [jnp.asarray(t) for t in tables()]
    field = field.reshape(C, XY, N)
    cotangent = cotangent.reshape(C, XY, N)
    weight = spec_weight.reshape(2, C, C, ML * C)
    wa = jnp.concatenate([weight[0], weight[0]], axis=2)
    wb = jnp.concatenate([-weight[1], weight[1]], axis=2)
    turn = pltpu.VMEM((PX, PY * C, LANES), f32)
    twice = pltpu.VMEM((2 * PX, PY * C, LANES), f32)
    whole = pltpu.VMEM((4 * XY + 2 * C, PX * LANES), bf16)

    def exchange(block):
        return lax.all_to_all(block, ("px", "py"), 0, 0, tiled=True)

    def exchange_rows(block):
        return exchange(block.reshape(PEERS, 1, ROWS * LANES)).reshape(PEERS * ROWS, LANES)

    sent = call(
        k_forward, "forward", shape(PEERS, C, LANES),
        [CELLS_LOW, whole, OWN, turn, pltpu.SemaphoreType.DMA((7,))],
        field, table, offset, hbm_in=range(3),
    )
    kron, pre, dact = run_prepare(
        skip_weight, mlp_in, mlp_out, skip_bias, field, cotangent
    )
    u, sent = call(
        k_mix, "mix", [shape(C, LANES), pltpu.HBM((PEERS, C, LANES), f32)],
        [pltpu.VMEM((8, C, LANES), f32), pltpu.SemaphoreType.DMA((PEERS // 8,))],
        exchange(sent), wa, wb, vmem_in=(1, 2), hbm_out=(1,),
    )
    sent, dpre = run_middle(
        exchange(sent), field, cotangent, pre, dact, kron, table, offset
    )
    sent, g = call(
        k_mix_back, "mix_back", [shape(PEERS * ROWS, LANES), shape(C, LANES)], [],
        exchange_rows(sent), wa, wb, vmem_in=(1, 2),
    )
    back = exchange_rows(sent)
    share = call(
        k_share, "share", pltpu.HBM((NB, 2 * C + 8, LANES), f32),
        [pltpu.VMEM((2 * C + 8, LANES), f32), pltpu.SemaphoreType.DMA((NB,))], back, u, g, hbm_out=(0,),
    )
    share = lax.all_to_all(share, "batch", 0, 0, tiled=True)
    grad_input = call(
        k_input, "input_grad", shape(C, XY, N, dtype=bf16),
        [CELLS_LOW, twice, CELLS, pltpu.SemaphoreType.DMA((STEPS,))],
        back, dpre, kron, table, offset, hbm_out=(0,),
    )
    spec, skip, b, inner, outer = call(
        k_shared, "shared",
        [shape(2, C, ML, 2, C), shape(C, C), shape(C), shape(C, C), shape(C, C)],
        [pltpu.VMEM((256, LANES), f32)] * 2, share,
    )
    spec = spec.transpose(0, 1, 4, 2, 3).reshape(2, C, C, 1, ML, 2)
    return (grad_input.reshape(1, C, XL, YL, N), spec, skip, b, inner, outer)


def solution(mesh):
    placed = (
        P("batch", None, "px", "py", None),
        P("batch", None, "px", "py", None),
        P(None, None, None, "py", "px", None),
        P(),
        P(),
        P(),
        P(),
    )
    return jax.shard_map(
        shards,
        mesh=mesh,
        in_specs=placed,
        out_specs=(
            P("batch", None, "px", "py", None),
            P(None, None, None, "py", "px", "batch"),
            P(),
            P(),
            P(),
            P(),
        ),
        check_vma=False,
    )
```

```python
import math

import jax
import jax.numpy as jnp
import ml_dtypes
import numpy as np
from jax import lax
from jax.experimental import pallas as pl
from jax.experimental.pallas import tpu as pltpu
from jax.sharding import PartitionSpec as P

f32 = jnp.float32
bf16 = jnp.bfloat16
C = 16
N = 128
PX, PY, NB = 4, 16, 8
XL, YL = N // PX, N // PY
XY = XL * YL
ML = C // PX
PEERS = PX * PY
STEPS = XY // 32
HALF = XY // 2
ROWS = C + 1
LANES = 128
SIGMA = 1.0 / math.sqrt(N**3)
RHO = 1.0 / math.sqrt(NB * N**3)
KEPT = f32
NT = (((1,), (1,)), ((), ()))


def tables():
    turn = lambda r, n: 2.0 * np.pi * (np.mod(r, n) / n)
    freq = np.where(np.arange(C) < C // 2, np.arange(C), np.arange(C) - C)
    depth = turn(np.arange(C)[:, None] * np.arange(N)[None, :], N)
    cos_z, sin_z = np.cos(depth), np.sin(depth)
    low = np.concatenate([cos_z, -sin_z]).astype(ml_dtypes.bfloat16)
    ax = turn(np.arange(XL)[:, None] * freq[None, :], N)
    ay = turn(np.arange(YL)[:, None] * freq[None, :], N)
    phase = ax[:, None, None, :] + ay[None, :, :, None]
    phase = phase.reshape(XY, PX, ML * C)
    co, si = np.cos(phase), np.sin(phase)
    plane = np.stack([co, -si], axis=2).reshape(XY, PX * LANES)
    plane_hi = plane.astype(ml_dtypes.bfloat16)
    plane_lo = (plane - plane_hi.astype(np.float64)).astype(ml_dtypes.bfloat16)
    ox = turn(np.arange(PX)[:, None] * XL * freq[None, :], N)
    oy = turn(np.arange(PY)[:, None] * YL * freq[None, :], N)
    off = ox[:, None, None, :] + oy[None, :, :, None]
    off = off.reshape(PEERS, PX, ML * C)
    cs = np.concatenate([np.cos(off), np.cos(off)], axis=2)
    sn = np.concatenate([np.sin(off), np.sin(off)], axis=2)
    offset = (np.concatenate([cs, sn], axis=1) * SIGMA).astype(np.float32)
    eye = np.eye(8)
    synth = np.concatenate(
        [
            np.einsum("ab,kz->akbz", eye, cos_z).reshape(8 * C, 8 * N),
            np.einsum("ab,kz->akbz", eye, -sin_z).reshape(8 * C, 8 * N),
        ]
    ).astype(ml_dtypes.bfloat16)
    low = np.pad(low.astype(np.float32), ((0, 0), (0, PX * LANES - N))).astype(ml_dtypes.bfloat16)
    table = np.concatenate([plane_hi, plane_lo, synth[:, : 4 * N], synth[:, 4 * N :], low])
    return table, offset


class Table:
    def __init__(self, ref):
        self.hi = ref.at[0:XY, :]
        self.lo = ref.at[XY : 2 * XY, :]
        self.synth = [ref.at[2 * XY : 3 * XY, :], ref.at[3 * XY : 4 * XY, :]]
        self.low = ref.at[4 * XY : 4 * XY + 2 * C, 0:N]


def dot(a, b):
    return jnp.dot(a, b, preferred_element_type=f32)


def dot_nt(a, b):
    return lax.dot_general(a, b, NT, preferred_element_type=f32)


def split(a):
    hi = a.astype(bf16)
    return hi, (a - hi.astype(f32)).astype(bf16)


def halves():
    lane = lax.broadcasted_iota(jnp.int32, (1, LANES), 1)
    return jnp.where(lane < LANES // 2, -1.0, 1.0)


def turned(v):
    return halves() * pltpu.roll(v, LANES // 2, 1)


def my_place():
    return lax.axis_index("px") * PY + lax.axis_index("py")


def forward_part(get, table, off_ref, turn_ref, put, ready=None):
    low = table.low[...]
    rows = [dot_nt(low, get(c)) for c in range(C)]
    both = jnp.concatenate([r[:C] for r in rows] + [r[C:] for r in rows], axis=0)
    x_hi, x_lo = split(both)
    if ready is not None:
        ready()
    hi = table.hi[...]
    part = dot(x_hi, hi) + dot(x_lo, hi) + dot(x_hi, table.lo[...])
    for mb in range(PX):
        pa = part[: C * C, mb * LANES : (mb + 1) * LANES]
        pb = part[C * C :, mb * LANES : (mb + 1) * LANES]
        co, si = off_ref[mb : mb + 1, :], off_ref[PX + mb : PX + mb + 1, :]
        turn_ref[mb] = (pa * co + pb * si) + turned(pb * co - pa * si)
    for mb in range(PX):
        for k in range(C):
            put(mb * PY + k, turn_ref[mb, pl.ds(k, C, stride=C), :])


def inverse_part(block, table, off_ref, turn_ref, g_ref):
    for mb in range(PX):
        v = jnp.concatenate([block(mb * PY + k) for k in range(PY)], axis=0)
        r = turned(v)
        co, si = off_ref[mb : mb + 1, :], off_ref[PX + mb : PX + mb + 1, :]
        turn_ref[mb] = v * co + r * si
        turn_ref[PX + mb] = v * si - r * co
    rows = []
    for half in range(2):
        for o in range(C):
            rows.append(
                jnp.concatenate(
                    [turn_ref[half * PX + mb, pl.ds(o, C, stride=C), :] for mb in range(PX)], axis=1
                )
            )
    v_hi, v_lo = split(jnp.concatenate(rows, axis=0))
    hi = table.hi[...]
    z = dot_nt(hi, v_hi) + dot_nt(hi, v_lo) + dot_nt(table.lo[...], v_hi)
    z = z.astype(bf16)
    for ob in range(2):
        re = z[:, ob * LANES : (ob + 1) * LANES]
        im = z[:, C * C + ob * LANES : C * C + (ob + 1) * LANES]
        both = jnp.concatenate([re, im], axis=1)
        for half in range(2):
            g = dot(both, table.synth[half][...])
            for o in range(4):
                g_ref[ob * 8 + half * 4 + o] = g[:, o * N : (o + 1) * N]


def k_forward(field_hbm, table_hbm, offset_hbm, out_ref, field_ref, table_ref, off_ref, turn_ref, sems):
    low_rows, plane_rows = pl.ds(4 * XY, 2 * C), pl.ds(0, 2 * XY)
    pairs = [(table_hbm.at[low_rows], table_ref.at[low_rows])]
    for i in range(4):
        part = pl.ds(4 * i, 4)
        pairs.append((field_hbm.at[part], field_ref.at[part]))
    pairs.append((table_hbm.at[plane_rows], table_ref.at[plane_rows]))
    pairs.append((offset_hbm.at[my_place()], off_ref))
    copies = [pltpu.make_async_copy(a, b, sems.at[i]) for i, (a, b) in enumerate(pairs)]
    for copy in copies:
        copy.start()
    copies[0].wait()

    def get(c):
        if c % 4 == 0:
            copies[1 + c // 4].wait()
        return field_ref[c]

    def ready():
        for copy in copies[5:]:
            copy.wait()

    def put(d, value):
        out_ref[d] = value

    forward_part(get, Table(table_ref), off_ref, turn_ref, put, ready)


def spread_map(w, transpose):
    r = lax.broadcasted_iota(jnp.int32, (256, C), 0)
    l = lax.broadcasted_iota(jnp.int32, (256, C), 1)
    rep = jnp.where(r // 16 == l, 1.0, 0.0).astype(bf16)
    if transpose:
        wide = lax.dot_general(w, rep, (((0,), (1,)), ((), ())), preferred_element_type=f32)
    else:
        wide = dot_nt(w, rep)
    full = dot(rep, wide.astype(bf16))
    r = lax.broadcasted_iota(jnp.int32, (256, 256), 0)
    l = lax.broadcasted_iota(jnp.int32, (256, 256), 1)
    return jnp.where(r % 16 == l % 16, full, 0.0).astype(bf16)


def k_prepare(
    skip_ref, in_ref, outer_ref, bias_in_ref, field_hbm, cot_hbm,
    kron_ref, pre_hbm, dact_hbm, field_ref, cot_ref, pre_ref, dact_ref, sems,
):
    copies = [
        pltpu.make_async_copy(field_hbm, field_ref, sems.at[0]),
        pltpu.make_async_copy(cot_hbm, cot_ref, sems.at[1]),
    ]
    for copy in copies:
        copy.start()
    skip = spread_map(skip_ref[...], False)
    outer = spread_map(outer_ref[...], True)
    kron_ref[0] = spread_map(in_ref[...], False)
    kron_ref[1] = spread_map(in_ref[...], True)
    kron_ref[2] = spread_map(skip_ref[...], True)
    r = lax.broadcasted_iota(jnp.int32, (256, C), 0)
    l = lax.broadcasted_iota(jnp.int32, (256, C), 1)
    bias = jnp.sum(jnp.where(r // 16 == l, bias_in_ref[...], 0.0), axis=1, keepdims=True)
    for copy in copies:
        copy.wait()

    def step(p, carry):
        untile(pre_ref, p, (dot(skip, tile(field_ref, p)) + bias).astype(KEPT))
        untile(dact_ref, p, dot(outer, tile(cot_ref, p)).astype(KEPT))
        return carry

    lax.fori_loop(0, STEPS, step, 0, unroll=2)
    copies = [
        pltpu.make_async_copy(pre_ref, pre_hbm, sems.at[0]),
        pltpu.make_async_copy(dact_ref, dact_hbm, sems.at[1]),
    ]
    for copy in copies:
        copy.start()
    for copy in copies:
        copy.wait()


def k_mix(recv_ref, wa_ref, wb_ref, u_ref, out_hbm, eight_ref, sems):
    u = jnp.sum(recv_ref[...], axis=0)
    us = pltpu.roll(u, LANES // 2, 1)
    u_ref[...] = u
    v = jnp.zeros((C, LANES), f32)
    for c in range(C):
        v = v + wa_ref[c] * u[c : c + 1, :] + wb_ref[c] * us[c : c + 1, :]
    eight_ref[...] = jnp.broadcast_to(v[None], (8, C, LANES))
    copies = [
        pltpu.make_async_copy(eight_ref, out_hbm.at[pl.ds(8 * i, 8)], sems.at[i])
        for i in range(PEERS // 8)
    ]
    for copy in copies:
        copy.start()
    for copy in copies:
        copy.wait()


def gelu_parts(x):
    a = math.sqrt(2.0 / math.pi)
    b = a * 0.044715
    x2 = x * x
    h = 0.5 * jnp.tanh(x * (a + b * x2)) + 0.5
    g = x * h
    d = h + g * (1.0 - h) * (2.0 * a + (6.0 * b) * x2)
    return g, d


def tile(ref, p):
    left = ref[:, pl.ds(p * 32, 16), :].reshape(C * 16, N)
    right = ref[:, pl.ds(p * 32 + 16, 16), :].reshape(C * 16, N)
    return jnp.concatenate([left, right], axis=1)


def untile(ref, p, value):
    ref[:, pl.ds(p * 32, 16), :] = value[:, :N].reshape(C, 16, N)
    ref[:, pl.ds(p * 32 + 16, 16), :] = value[:, N:].reshape(C, 16, N)


def pack_rows(acc):
    r = lax.broadcasted_iota(jnp.int32, (256, 256), 0)
    l = lax.broadcasted_iota(jnp.int32, (256, 256), 1)
    kept = jnp.where(r % 16 == l % 16, acc, 0.0).reshape(C, 16, 256).sum(axis=1)
    r = lax.broadcasted_iota(jnp.int32, (256, LANES), 0)
    l = lax.broadcasted_iota(jnp.int32, (256, LANES), 1)
    pick = jnp.where(r // 16 == l % 16, 1.0, 0.0)
    spread = jnp.dot(kept, pick, precision=lax.Precision.HIGHEST, preferred_element_type=f32)
    r = lax.broadcasted_iota(jnp.int32, (C, LANES), 0)
    l = lax.broadcasted_iota(jnp.int32, (C, LANES), 1)
    return jnp.where(r % 8 == l // 16, spread, 0.0)


def k_middle(
    recv_ref, field_hbm, cot_hbm, pre_hbm, dact_hbm, kron_hbm, table_ref, offset_ref,
    out_ref, dpre_hbm,
    field_ref, cot_ref, pre_ref, dact_ref, kron_ref, dpre_ref, sems, turn_ref, g_ref, skip_acc, bias_acc, in_acc, out_acc,
):
    pairs = [(kron_hbm.at[0:2], kron_ref)]
    for i in range(2):
        part = pl.ds(i * HALF, HALF)
        for a, b in ((pre_hbm, pre_ref), (dact_hbm, dact_ref), (field_hbm, field_ref), (cot_hbm, cot_ref)):
            pairs.append((a.at[:, part], b.at[:, part]))
    copies = [pltpu.make_async_copy(a, b, sems.at[i]) for i, (a, b) in enumerate(pairs)]
    for copy in copies:
        copy.start()
    off_ref = offset_ref.at[my_place()]
    table = Table(table_ref)
    inverse_part(lambda d: recv_ref[d], table, off_ref, turn_ref, g_ref)
    skip_acc[...] = jnp.zeros_like(skip_acc)
    in_acc[...] = jnp.zeros_like(in_acc)
    out_acc[...] = jnp.zeros_like(out_acc)
    bias_acc[...] = jnp.zeros_like(bias_acc)

    def step(p):
        f = tile(field_ref, p)
        cot = tile(cot_ref, p)
        pre = tile(g_ref, p) + tile(pre_ref, p)
        hid, d_hid = gelu_parts(pre)
        hid = hid.astype(bf16)
        act, d_act = gelu_parts(dot(kron_ref[0], hid))
        act = act.astype(bf16)
        d_inner = (tile(dact_ref, p) * d_act).astype(bf16)
        dpre = dot(kron_ref[1], d_inner) * d_hid
        dpre = dpre.astype(bf16)
        untile(dpre_ref, p, dpre)
        skip_acc[...] += dot_nt(dpre, f)
        in_acc[...] += dot_nt(d_inner, hid)
        out_acc[...] += dot_nt(cot, act)
        bias_acc[...] += dpre.astype(f32)

    copies[0].wait()
    for p in range(STEPS):
        if p % (STEPS // 2) == 0:
            first = 1 + 4 * (p // (STEPS // 2))
            for copy in copies[first : first + 4]:
                copy.wait()
        step(p)
    copy = pltpu.make_async_copy(dpre_ref, dpre_hbm, sems.at[9])
    copy.start()
    bias = bias_acc[...].reshape(C, 16, 256).sum(axis=1)
    total = jnp.sum(bias, axis=1, keepdims=True)
    r = lax.broadcasted_iota(jnp.int32, (C, LANES), 0)
    l = lax.broadcasted_iota(jnp.int32, (C, LANES), 1)
    bias_row = jnp.sum(jnp.where(r == l, total, 0.0), axis=0, keepdims=True)
    small = jnp.concatenate(
        [pack_rows(skip_acc[...]), pack_rows(in_acc[...]), pack_rows(out_acc[...]),
         bias_row, jnp.zeros((C - 1, LANES), f32)], axis=0
    )

    def put(d, value):
        out_ref[d * ROWS : (d + 1) * ROWS, :] = jnp.concatenate([value, small[d : d + 1]], axis=0)

    forward_part(lambda c: dpre_ref[c], table, off_ref, turn_ref, put)
    copy.wait()


def k_mix_back(recv_ref, wa_ref, wb_ref, out_ref, g_ref):
    slabs = recv_ref[...].reshape(8, 8 * ROWS, LANES).sum(axis=0)
    got = slabs[:ROWS]
    for i in range(1, 8):
        got = got + slabs[i * ROWS : (i + 1) * ROWS]
    g = got[:C]
    g_ref[...] = g
    gs = pltpu.roll(g, LANES // 2, 1)
    rows = []
    for c in range(C):
        rows.append(jnp.sum(wa_ref[c] * g - wb_ref[c] * gs, axis=0, keepdims=True))
    block = jnp.concatenate(rows + [got[C:]], axis=0)
    slab = jnp.concatenate([block] * 8, axis=0)
    for i in range(8):
        out_ref[i * 8 * ROWS : (i + 1) * 8 * ROWS, :] = slab


def k_share(back_ref, u_ref, g_ref, share_hbm, block_ref, sems):
    small = back_ref[pl.ds(C, PEERS, stride=ROWS), :].reshape(8, 8, LANES).sum(axis=1)
    block_ref[...] = jnp.concatenate([u_ref[...], g_ref[...], small], axis=0)
    copies = [pltpu.make_async_copy(block_ref, share_hbm.at[i], sems.at[i]) for i in range(NB)]
    for copy in copies:
        copy.start()
    for copy in copies:
        copy.wait()


def k_input(
    recv_ref, dpre_ref, kron_ref, table_ref, offset_ref, out_hbm,
    out_ref, turn_ref, g_ref, sems,
):
    steps = XY // 32
    off_ref = offset_ref.at[my_place()]
    inverse_part(
        lambda d: recv_ref[d * ROWS : d * ROWS + C, :], Table(table_ref), off_ref, turn_ref, g_ref
    )
    copies = []
    for p in range(steps):
        untile(out_ref, p, (dot(kron_ref[2], tile(dpre_ref, p)) + tile(g_ref, p)).astype(bf16))
        part = pl.ds(p * 32, 32)
        copies.append(pltpu.make_async_copy(out_ref.at[:, part], out_hbm.at[:, part], sems.at[p]))
        copies[-1].start()
    for copy in copies:
        copy.wait()


def k_shared(recv_ref, spec_ref, skip_ref, bias_ref, in_ref, outer_ref, pa_ref, pb_ref):
    for c in range(C):
        pa = jnp.zeros((C, LANES), f32)
        pb = jnp.zeros((C, LANES), f32)
        for s in range(NB):
            u = recv_ref[s, c : c + 1, :]
            g = recv_ref[s, C : 2 * C, :]
            pa = pa + u * g
            pb = pb + u * pltpu.roll(g, LANES // 2, 1)
        pa_ref[c * C : (c + 1) * C, :] = pa
        pb_ref[c * C : (c + 1) * C, :] = pb
    b = lax.axis_index("batch")
    r = lax.broadcasted_iota(jnp.int32, (8, LANES), 0)
    l = lax.broadcasted_iota(jnp.int32, (8, LANES), 1)
    mine = ((l % 64) // C == r // 2) & (l % C == 2 * b + r % 2)
    sel_a = jnp.where(mine, 1.0, 0.0)
    sel_b = jnp.where(l < 64, sel_a, -sel_a)
    full = lambda x, y: lax.dot_general(
        x, y, NT, precision=lax.Precision.HIGHEST, preferred_element_type=f32
    )
    for i, part in enumerate((full(sel_a, pa_ref[...]), full(sel_b, pb_ref[...]))):
        for c in range(C):
            for m in range(ML):
                spec_ref[i, c, m] = part[2 * m : 2 * m + 2, c * C : (c + 1) * C]
    small = jnp.sum(recv_ref[:, 2 * C :, :], axis=0) * RHO
    r = lax.broadcasted_iota(jnp.int32, (C, LANES), 0)
    l = lax.broadcasted_iota(jnp.int32, (C, LANES), 1)
    pr = lax.broadcasted_iota(jnp.int32, (LANES, C), 0)
    pc = lax.broadcasted_iota(jnp.int32, (LANES, C), 1)
    pick = jnp.where(pr % C == pc, 1.0, 0.0)
    for i, ref in enumerate((skip_ref, in_ref, outer_ref)):
        two = jnp.concatenate(
            [jnp.broadcast_to(small[2 * i + h : 2 * i + h + 1], (8, LANES)) for h in range(2)], axis=0
        )
        two = jnp.where(l // C == r % 8, two, 0.0)
        ref[...] = jnp.dot(two, pick, precision=lax.Precision.HIGHEST, preferred_element_type=f32)
    bias_ref[...] = small[6, :C]


def call(body, name, outs, scratch, *args, hbm_in=(), vmem_in=(), hbm_out=()):
    vm = pl.BlockSpec(memory_space=pltpu.VMEM)
    hbm = pl.BlockSpec(memory_space=pltpu.HBM)
    many = isinstance(outs, (list, tuple))
    out_specs = [hbm if i in hbm_out else vm for i in range(len(outs) if many else 1)]
    args = [
        pltpu.with_memory_space_constraint(a, pltpu.HBM) if i in hbm_in
        else pltpu.with_memory_space_constraint(a, pltpu.VMEM) if i in vmem_in
        else a
        for i, a in enumerate(args)
    ]
    return pl.pallas_call(
        body,
        out_shape=outs,
        in_specs=[hbm if i in hbm_in else vm for i in range(len(args))],
        out_specs=out_specs if many else out_specs[0],
        scratch_shapes=scratch,
        compiler_params=pltpu.CompilerParams(vmem_limit_bytes=32 * 2**20),
        name=name,
    )(*args)


def shape(*dims, dtype=f32):
    return jax.ShapeDtypeStruct(dims, dtype)


CELLS = pltpu.VMEM((C, XY, N), f32)
CELLS_LOW = pltpu.VMEM((C, XY, N), bf16)
CELLS_KEPT = pltpu.VMEM((C, XY, N), KEPT)
OWN = pltpu.VMEM((8, LANES), f32)


def run_prepare(skip_weight, mlp_in, mlp_out, skip_bias, field, cotangent):
    return call(
        k_prepare, "prepare",
        [shape(3, 256, 256, dtype=bf16), pltpu.HBM((C, XY, N), KEPT), pltpu.HBM((C, XY, N), KEPT)],
        [CELLS_LOW, CELLS_LOW, CELLS_KEPT, CELLS_KEPT, pltpu.SemaphoreType.DMA((2,))],
        skip_weight, mlp_in, mlp_out, skip_bias.reshape(1, C), field, cotangent, hbm_in=(4, 5), hbm_out=(1, 2),
    )


def run_middle(recv, field, cotangent, pre, dact, kron, table, offset):
    turn = pltpu.VMEM((2 * PX, PY * C, LANES), f32)
    square = pltpu.VMEM((256, 256), f32)
    return call(
        k_middle, "middle",
        [shape(PEERS * ROWS, LANES), pltpu.HBM((C, XY, N), bf16)],
        [CELLS_LOW, CELLS_LOW, CELLS_KEPT, CELLS_KEPT, pltpu.VMEM((2, 256, 256), bf16), CELLS_LOW,
         pltpu.SemaphoreType.DMA((10,)), turn, CELLS, square, square, square, square],
        recv, field, cotangent, pre, dact, kron, table, offset, hbm_in=(1, 2, 3, 4, 5), hbm_out=(1,),
    )


def shards(field, cotangent, spec_weight, skip_weight, skip_bias, mlp_in, mlp_out):
    table, offset = [jnp.asarray(t) for t in tables()]
    field = field.reshape(C, XY, N)
    cotangent = cotangent.reshape(C, XY, N)
    weight = spec_weight.reshape(2, C, C, ML * C)
    wa = jnp.concatenate([weight[0], weight[0]], axis=2)
    wb = jnp.concatenate([-weight[1], weight[1]], axis=2)
    turn = pltpu.VMEM((PX, PY * C, LANES), f32)
    twice = pltpu.VMEM((2 * PX, PY * C, LANES), f32)
    whole = pltpu.VMEM((4 * XY + 2 * C, PX * LANES), bf16)

    def exchange(block):
        return lax.all_to_all(block, ("px", "py"), 0, 0, tiled=True)

    def exchange_rows(block):
        return exchange(block.reshape(PEERS, 1, ROWS * LANES)).reshape(PEERS * ROWS, LANES)

    sent = call(
        k_forward, "forward", shape(PEERS, C, LANES),
        [CELLS_LOW, whole, OWN, turn, pltpu.SemaphoreType.DMA((7,))],
        field, table, offset, hbm_in=range(3),
    )
    kron, pre, dact = run_prepare(
        skip_weight, mlp_in, mlp_out, skip_bias, field, cotangent
    )
    u, sent = call(
        k_mix, "mix", [shape(C, LANES), pltpu.HBM((PEERS, C, LANES), f32)],
        [pltpu.VMEM((8, C, LANES), f32), pltpu.SemaphoreType.DMA((PEERS // 8,))],
        exchange(sent), wa, wb, vmem_in=(1, 2), hbm_out=(1,),
    )
    sent, dpre = run_middle(
        exchange(sent), field, cotangent, pre, dact, kron, table, offset
    )
    sent, g = call(
        k_mix_back, "mix_back", [shape(PEERS * ROWS, LANES), shape(C, LANES)], [],
        exchange_rows(sent), wa, wb, vmem_in=(1, 2),
    )
    back = exchange_rows(sent)
    share = call(
        k_share, "share", pltpu.HBM((NB, 2 * C + 8, LANES), f32),
        [pltpu.VMEM((2 * C + 8, LANES), f32), pltpu.SemaphoreType.DMA((NB,))], back, u, g, hbm_out=(0,),
    )
    share = lax.all_to_all(share, "batch", 0, 0, tiled=True)
    grad_input = call(
        k_input, "input_grad", shape(C, XY, N, dtype=bf16),
        [CELLS_LOW, twice, CELLS, pltpu.SemaphoreType.DMA((STEPS,))],
        back, dpre, kron, table, offset, hbm_out=(0,),
    )
    spec, skip, b, inner, outer = call(
        k_shared, "shared",
        [shape(2, C, ML, 2, C), shape(C, C), shape(C), shape(C, C), shape(C, C)],
        [pltpu.VMEM((256, LANES), f32)] * 2, share,
    )
    spec = spec.transpose(0, 1, 4, 2, 3).reshape(2, C, C, 1, ML, 2)
    return (grad_input.reshape(1, C, XL, YL, N), spec, skip, b, inner, outer)


def solution(mesh):
    placed = (
        P("batch", None, "px", "py", None),
        P("batch", None, "px", "py", None),
        P(None, None, None, "py", "px", None),
        P(),
        P(),
        P(),
        P(),
    )
    return jax.shard_map(
        shards,
        mesh=mesh,
        in_specs=placed,
        out_specs=(
            P("batch", None, "px", "py", None),
            P(None, None, None, "py", "px", "batch"),
            P(),
            P(),
            P(),
            P(),
        ),
        check_vma=False,
    )
```

```python
import math

import jax
import jax.numpy as jnp
import ml_dtypes
import numpy as np
from jax import lax
from jax.experimental import pallas as pl
from jax.experimental.pallas import tpu as pltpu
from jax.sharding import PartitionSpec as P

f32 = jnp.float32
bf16 = jnp.bfloat16
C = 16
N = 128
PX, PY, NB = 4, 16, 8
XL, YL = N // PX, N // PY
XY = XL * YL
ML = C // PX
PEERS = PX * PY
STEPS = XY // 32
HALF = XY // 2
ROWS = C + 1
LANES = 128
SIGMA = 1.0 / math.sqrt(N**3)
RHO = 1.0 / math.sqrt(NB * N**3)
KEPT = f32
NT = (((1,), (1,)), ((), ()))


def tables():
    turn = lambda r, n: 2.0 * np.pi * (np.mod(r, n) / n)
    freq = np.where(np.arange(C) < C // 2, np.arange(C), np.arange(C) - C)
    depth = turn(np.arange(C)[:, None] * np.arange(N)[None, :], N)
    cos_z, sin_z = np.cos(depth), np.sin(depth)
    low = np.concatenate([cos_z, -sin_z]).astype(ml_dtypes.bfloat16)
    ax = turn(np.arange(XL)[:, None] * freq[None, :], N)
    ay = turn(np.arange(YL)[:, None] * freq[None, :], N)
    phase = ax[:, None, None, :] + ay[None, :, :, None]
    phase = phase.reshape(XY, PX, ML * C)
    co, si = np.cos(phase), np.sin(phase)
    plane = np.stack([co, -si], axis=2).reshape(XY, PX * LANES)
    plane_hi = plane.astype(ml_dtypes.bfloat16)
    plane_lo = (plane - plane_hi.astype(np.float64)).astype(ml_dtypes.bfloat16)
    ox = turn(np.arange(PX)[:, None] * XL * freq[None, :], N)
    oy = turn(np.arange(PY)[:, None] * YL * freq[None, :], N)
    off = ox[:, None, None, :] + oy[None, :, :, None]
    off = off.reshape(PEERS, PX, ML * C)
    cs = np.concatenate([np.cos(off), np.cos(off)], axis=2)
    sn = np.concatenate([np.sin(off), np.sin(off)], axis=2)
    offset = (np.concatenate([cs, sn], axis=1) * SIGMA).astype(np.float32)
    eye = np.eye(8)
    synth = np.concatenate(
        [
            np.einsum("ab,kz->akbz", eye, cos_z).reshape(8 * C, 8 * N),
            np.einsum("ab,kz->akbz", eye, -sin_z).reshape(8 * C, 8 * N),
        ]
    ).astype(ml_dtypes.bfloat16)
    low = np.pad(low.astype(np.float32), ((0, 0), (0, PX * LANES - N))).astype(ml_dtypes.bfloat16)
    table = np.concatenate([plane_hi, plane_lo, synth[:, : 4 * N], synth[:, 4 * N :], low])
    return table, offset


class Table:
    def __init__(self, ref):
        self.hi = ref.at[0:XY, :]
        self.lo = ref.at[XY : 2 * XY, :]
        self.synth = [ref.at[2 * XY : 3 * XY, :], ref.at[3 * XY : 4 * XY, :]]
        self.low = ref.at[4 * XY : 4 * XY + 2 * C, 0:N]


def dot(a, b):
    return jnp.dot(a, b, preferred_element_type=f32)


def dot_nt(a, b):
    return lax.dot_general(a, b, NT, preferred_element_type=f32)


def split(a):
    hi = a.astype(bf16)
    return hi, (a - hi.astype(f32)).astype(bf16)


def halves():
    lane = lax.broadcasted_iota(jnp.int32, (1, LANES), 1)
    return jnp.where(lane < LANES // 2, -1.0, 1.0)


def turned(v):
    return halves() * pltpu.roll(v, LANES // 2, 1)


def my_place():
    return lax.axis_index("px") * PY + lax.axis_index("py")


def forward_part(get, table, off_ref, turn_ref, put, ready=None, done=None):
    low = table.low[...]
    rows = [dot_nt(low, get(c)) for c in range(C)]
    both = jnp.concatenate([r[:C] for r in rows] + [r[C:] for r in rows], axis=0)
    x_hi, x_lo = split(both)
    if ready is not None:
        ready()
    hi = table.hi[...]
    part = dot(x_hi, hi) + dot(x_lo, hi) + dot(x_hi, table.lo[...])
    for mb in range(PX):
        pa = part[: C * C, mb * LANES : (mb + 1) * LANES]
        pb = part[C * C :, mb * LANES : (mb + 1) * LANES]
        co, si = off_ref[mb : mb + 1, :], off_ref[PX + mb : PX + mb + 1, :]
        turn_ref[mb] = (pa * co + pb * si) + turned(pb * co - pa * si)
        for k in range(C):
            put(mb * PY + k, turn_ref[mb, pl.ds(k, C, stride=C), :])
        if done is not None:
            done(mb)


def inverse_part(block, table, off_ref, turn_ref, g_ref):
    for mb in range(PX):
        v = jnp.concatenate([block(mb * PY + k) for k in range(PY)], axis=0)
        r = turned(v)
        co, si = off_ref[mb : mb + 1, :], off_ref[PX + mb : PX + mb + 1, :]
        turn_ref[mb] = v * co + r * si
        turn_ref[PX + mb] = v * si - r * co
    rows = []
    for half in range(2):
        for o in range(C):
            rows.append(
                jnp.concatenate(
                    [turn_ref[half * PX + mb, pl.ds(o, C, stride=C), :] for mb in range(PX)], axis=1
                )
            )
    v_hi, v_lo = split(jnp.concatenate(rows, axis=0))
    hi = table.hi[...]
    z = dot_nt(hi, v_hi) + dot_nt(hi, v_lo) + dot_nt(table.lo[...], v_hi)
    z = z.astype(bf16)
    for ob in range(2):
        re = z[:, ob * LANES : (ob + 1) * LANES]
        im = z[:, C * C + ob * LANES : C * C + (ob + 1) * LANES]
        both = jnp.concatenate([re, im], axis=1)
        for half in range(2):
            g = dot(both, table.synth[half][...])
            for o in range(4):
                g_ref[ob * 8 + half * 4 + o] = g[:, o * N : (o + 1) * N]


def k_forward(
    field_hbm, table_hbm, offset_hbm, out_hbm, out_ref, field_ref, table_ref, off_ref, turn_ref, sems
):
    low_rows, plane_rows = pl.ds(4 * XY, 2 * C), pl.ds(0, 2 * XY)
    pairs = [(table_hbm.at[low_rows], table_ref.at[low_rows])]
    for i in range(4):
        part = pl.ds(4 * i, 4)
        pairs.append((field_hbm.at[part], field_ref.at[part]))
    pairs.append((table_hbm.at[plane_rows], table_ref.at[plane_rows]))
    pairs.append((offset_hbm.at[my_place()], off_ref))
    copies = [pltpu.make_async_copy(a, b, sems.at[i]) for i, (a, b) in enumerate(pairs)]
    for copy in copies:
        copy.start()
    copies[0].wait()

    def get(c):
        if c % 4 == 0:
            copies[1 + c // 4].wait()
        return field_ref[c]

    def ready():
        for copy in copies[5:]:
            copy.wait()

    def put(d, value):
        out_ref[d] = value

    sent = []

    def done(mb):
        part = pl.ds(mb * PY, PY)
        sent.append(pltpu.make_async_copy(out_ref.at[part], out_hbm.at[part], sems.at[7 + mb]))
        sent[-1].start()

    forward_part(get, Table(table_ref), off_ref, turn_ref, put, ready, done)
    for copy in sent:
        copy.wait()


def spread_map(w, transpose):
    r = lax.broadcasted_iota(jnp.int32, (256, C), 0)
    l = lax.broadcasted_iota(jnp.int32, (256, C), 1)
    rep = jnp.where(r // 16 == l, 1.0, 0.0).astype(bf16)
    if transpose:
        wide = lax.dot_general(w, rep, (((0,), (1,)), ((), ())), preferred_element_type=f32)
    else:
        wide = dot_nt(w, rep)
    full = dot(rep, wide.astype(bf16))
    r = lax.broadcasted_iota(jnp.int32, (256, 256), 0)
    l = lax.broadcasted_iota(jnp.int32, (256, 256), 1)
    return jnp.where(r % 16 == l % 16, full, 0.0).astype(bf16)


def k_prepare(
    skip_ref, in_ref, outer_ref, bias_in_ref, field_hbm, cot_hbm,
    kron_ref, pre_hbm, dact_hbm, field_ref, cot_ref, pre_ref, dact_ref, sems,
):
    copies = [
        pltpu.make_async_copy(field_hbm, field_ref, sems.at[0]),
        pltpu.make_async_copy(cot_hbm, cot_ref, sems.at[1]),
    ]
    for copy in copies:
        copy.start()
    skip = spread_map(skip_ref[...], False)
    outer = spread_map(outer_ref[...], True)
    kron_ref[0] = spread_map(in_ref[...], False)
    kron_ref[1] = spread_map(in_ref[...], True)
    kron_ref[2] = spread_map(skip_ref[...], True)
    r = lax.broadcasted_iota(jnp.int32, (256, C), 0)
    l = lax.broadcasted_iota(jnp.int32, (256, C), 1)
    bias = jnp.sum(jnp.where(r // 16 == l, bias_in_ref[...], 0.0), axis=1, keepdims=True)
    for copy in copies:
        copy.wait()

    def step(p, carry):
        untile(pre_ref, p, (dot(skip, tile(field_ref, p)) + bias).astype(KEPT))
        untile(dact_ref, p, dot(outer, tile(cot_ref, p)).astype(KEPT))
        return carry

    lax.fori_loop(0, STEPS, step, 0, unroll=2)
    copies = [
        pltpu.make_async_copy(pre_ref, pre_hbm, sems.at[0]),
        pltpu.make_async_copy(dact_ref, dact_hbm, sems.at[1]),
    ]
    for copy in copies:
        copy.start()
    for copy in copies:
        copy.wait()


def k_mix(recv_ref, wa_ref, wb_ref, u_ref, out_hbm, eight_ref, sems):
    u = jnp.sum(recv_ref[...], axis=0)
    us = pltpu.roll(u, LANES // 2, 1)
    u_ref[...] = u
    v = jnp.zeros((C, LANES), f32)
    for c in range(C):
        v = v + wa_ref[c] * u[c : c + 1, :] + wb_ref[c] * us[c : c + 1, :]
    eight_ref[...] = jnp.broadcast_to(v[None], (8, C, LANES))
    copies = [
        pltpu.make_async_copy(eight_ref, out_hbm.at[pl.ds(8 * i, 8)], sems.at[i])
        for i in range(PEERS // 8)
    ]
    for copy in copies:
        copy.start()
    for copy in copies:
        copy.wait()


def gelu_parts(x):
    a = math.sqrt(2.0 / math.pi)
    b = a * 0.044715
    x2 = x * x
    h = 0.5 * jnp.tanh(x * (a + b * x2)) + 0.5
    g = x * h
    d = h + g * (1.0 - h) * (2.0 * a + (6.0 * b) * x2)
    return g, d


def tile(ref, p):
    left = ref[:, pl.ds(p * 32, 16), :].reshape(C * 16, N)
    right = ref[:, pl.ds(p * 32 + 16, 16), :].reshape(C * 16, N)
    return jnp.concatenate([left, right], axis=1)


def untile(ref, p, value):
    ref[:, pl.ds(p * 32, 16), :] = value[:, :N].reshape(C, 16, N)
    ref[:, pl.ds(p * 32 + 16, 16), :] = value[:, N:].reshape(C, 16, N)


def thirds(x):
    hi, rest = x.astype(bf16), x - x.astype(bf16).astype(f32)
    mid = rest.astype(bf16)
    return [hi, mid, (rest - mid.astype(f32)).astype(bf16)]


def picked(x, pick):
    n = x.shape[0]
    out = dot(jnp.concatenate(thirds(x), axis=0), pick)
    return out[:n] + out[n : 2 * n] + out[2 * n :]


def pack_rows(accs):
    r = lax.broadcasted_iota(jnp.int32, (256, 256), 0)
    l = lax.broadcasted_iota(jnp.int32, (256, 256), 1)
    same = r % 16 == l % 16
    kept = [jnp.where(same, a, 0.0).reshape(C, 16, 256).sum(axis=1) for a in accs]
    r = lax.broadcasted_iota(jnp.int32, (256, LANES), 0)
    l = lax.broadcasted_iota(jnp.int32, (256, LANES), 1)
    pick = jnp.where(r // 16 == l % 16, 1.0, 0.0).astype(bf16)
    spread = picked(jnp.concatenate(kept, axis=0), pick)
    r = lax.broadcasted_iota(jnp.int32, (len(accs) * C, LANES), 0)
    l = lax.broadcasted_iota(jnp.int32, (len(accs) * C, LANES), 1)
    return jnp.where(r % 8 == l // 16, spread, 0.0)


def k_middle(
    recv_ref, field_hbm, cot_hbm, pre_hbm, dact_hbm, kron_hbm, table_ref, offset_ref,
    out_ref, dpre_hbm,
    field_ref, cot_ref, pre_ref, dact_ref, kron_ref, dpre_ref, sems, turn_ref, g_ref, skip_acc, in_acc, out_acc,
):
    pairs = [(kron_hbm.at[0:2], kron_ref)]
    for i in range(2):
        part = pl.ds(i * HALF, HALF)
        for a, b in ((pre_hbm, pre_ref), (dact_hbm, dact_ref), (field_hbm, field_ref), (cot_hbm, cot_ref)):
            pairs.append((a.at[:, part], b.at[:, part]))
    copies = [pltpu.make_async_copy(a, b, sems.at[i]) for i, (a, b) in enumerate(pairs)]
    for copy in copies:
        copy.start()
    off_ref = offset_ref.at[my_place()]
    table = Table(table_ref)
    inverse_part(lambda d: recv_ref[d], table, off_ref, turn_ref, g_ref)
    skip_acc[...] = jnp.zeros_like(skip_acc)
    in_acc[...] = jnp.zeros_like(in_acc)
    out_acc[...] = jnp.zeros_like(out_acc)

    kept, sums = [], []

    def step(p):
        f = tile(field_ref, p)
        cot = tile(cot_ref, p)
        pre = tile(g_ref, p) + tile(pre_ref, p)
        hid, d_hid = gelu_parts(pre)
        hid = hid.astype(bf16)
        act, d_act = gelu_parts(dot(kron_ref[0], hid))
        act = act.astype(bf16)
        d_inner = (tile(dact_ref, p) * d_act).astype(bf16)
        dpre = dot(kron_ref[1], d_inner) * d_hid
        dpre = dpre.astype(bf16)
        untile(dpre_ref, p, dpre)
        kept.append((dpre, f, d_inner, hid, cot, act))
        if p % 2:
            wide = lambda i: jnp.concatenate([k[i] for k in kept[-2:]], axis=1)
            skip_acc[...] += dot_nt(wide(0), wide(1))
            in_acc[...] += dot_nt(wide(2), wide(3))
            out_acc[...] += dot_nt(wide(4), wide(5))
        sums.append(dpre.astype(f32).reshape(C, 16, 256).sum(axis=1))

    copies[0].wait()
    for p in range(STEPS):
        if p % (STEPS // 2) == 0:
            first = 1 + 4 * (p // (STEPS // 2))
            for copy in copies[first : first + 4]:
                copy.wait()
        step(p)
    copy = pltpu.make_async_copy(dpre_ref, dpre_hbm, sems.at[9])
    copy.start()
    bias = sum(sums)
    total = jnp.sum(bias, axis=1, keepdims=True)
    r = lax.broadcasted_iota(jnp.int32, (C, LANES), 0)
    l = lax.broadcasted_iota(jnp.int32, (C, LANES), 1)
    bias_row = jnp.sum(jnp.where(r == l, total, 0.0), axis=0, keepdims=True)
    small = jnp.concatenate(
        [pack_rows([skip_acc[...], in_acc[...], out_acc[...]]),
         bias_row, jnp.zeros((C - 1, LANES), f32)], axis=0
    )

    def put(d, value):
        out_ref[d * ROWS : (d + 1) * ROWS, :] = jnp.concatenate([value, small[d : d + 1]], axis=0)

    forward_part(lambda c: dpre_ref[c], table, off_ref, turn_ref, put)
    copy.wait()


def k_mix_back(recv_ref, wa_ref, wb_ref, out_ref, g_ref):
    slabs = recv_ref[...].reshape(8, 8 * ROWS, LANES).sum(axis=0)
    got = slabs[:ROWS]
    for i in range(1, 8):
        got = got + slabs[i * ROWS : (i + 1) * ROWS]
    g = got[:C]
    g_ref[...] = g
    gs = pltpu.roll(g, LANES // 2, 1)
    rows = []
    for c in range(C):
        rows.append(jnp.sum(wa_ref[c] * g - wb_ref[c] * gs, axis=0, keepdims=True))
    block = jnp.concatenate(rows + [got[C:]], axis=0)
    slab = jnp.concatenate([block] * 8, axis=0)
    for i in range(8):
        out_ref[i * 8 * ROWS : (i + 1) * 8 * ROWS, :] = slab


def k_share(back_ref, u_ref, g_ref, share_hbm, block_ref, sems):
    small = back_ref[pl.ds(C, PEERS, stride=ROWS), :].reshape(8, 8, LANES).sum(axis=1)
    block_ref[...] = jnp.concatenate([u_ref[...], g_ref[...], small], axis=0)
    copies = [pltpu.make_async_copy(block_ref, share_hbm.at[i], sems.at[i]) for i in range(NB)]
    for copy in copies:
        copy.start()
    for copy in copies:
        copy.wait()


def k_input(
    recv_ref, dpre_ref, kron_ref, table_ref, offset_ref, out_hbm,
    out_ref, turn_ref, g_ref, sems,
):
    steps = XY // 32
    off_ref = offset_ref.at[my_place()]
    inverse_part(
        lambda d: recv_ref[d * ROWS : d * ROWS + C, :], Table(table_ref), off_ref, turn_ref, g_ref
    )
    copies = []
    for p in range(steps):
        untile(out_ref, p, (dot(kron_ref[2], tile(dpre_ref, p)) + tile(g_ref, p)).astype(bf16))
        part = pl.ds(p * 32, 32)
        copies.append(pltpu.make_async_copy(out_ref.at[:, part], out_hbm.at[:, part], sems.at[p]))
        copies[-1].start()
    for copy in copies:
        copy.wait()


def k_shared(recv_ref, spec_ref, skip_ref, bias_ref, in_ref, outer_ref, pa_ref, pb_ref):
    gs = [recv_ref[s, C : 2 * C, :] for s in range(NB)]
    turns = [pltpu.roll(g, LANES // 2, 1) for g in gs]
    for c in range(C):
        us = [recv_ref[s, c : c + 1, :] for s in range(NB)]
        pa_ref[c * C : (c + 1) * C, :] = sum(u * g for u, g in zip(us, gs))
        pb_ref[c * C : (c + 1) * C, :] = sum(u * g for u, g in zip(us, turns))
    b = lax.axis_index("batch")
    r = lax.broadcasted_iota(jnp.int32, (8, LANES), 0)
    l = lax.broadcasted_iota(jnp.int32, (8, LANES), 1)
    mine = ((l % 64) // C == r // 2) & (l % C == 2 * b + r % 2)
    sel_a = jnp.where(mine, 1.0, 0.0)
    sel_b = jnp.where(l < 64, sel_a, -sel_a)
    for i, (sel, ref) in enumerate(((sel_a, pa_ref), (sel_b, pb_ref))):
        part = sum(dot_nt(sel.astype(bf16), third) for third in thirds(ref[...]))
        for c in range(C):
            for m in range(ML):
                spec_ref[i, c, m] = part[2 * m : 2 * m + 2, c * C : (c + 1) * C]
    small = jnp.sum(recv_ref[:, 2 * C :, :], axis=0) * RHO
    r = lax.broadcasted_iota(jnp.int32, (3 * C, LANES), 0)
    l = lax.broadcasted_iota(jnp.int32, (3 * C, LANES), 1)
    pr = lax.broadcasted_iota(jnp.int32, (LANES, C), 0)
    pc = lax.broadcasted_iota(jnp.int32, (LANES, C), 1)
    pick = jnp.where(pr % C == pc, 1.0, 0.0).astype(bf16)
    rows = jnp.concatenate([jnp.broadcast_to(small[i : i + 1], (8, LANES)) for i in range(6)], axis=0)
    maps = picked(jnp.where(l // C == r % 8, rows, 0.0), pick)
    for i, ref in enumerate((skip_ref, in_ref, outer_ref)):
        ref[...] = maps[i * C : (i + 1) * C]
    bias_ref[...] = small[6, :C]


def call(body, name, outs, scratch, *args, hbm_in=(), vmem_in=(), hbm_out=()):
    vm = pl.BlockSpec(memory_space=pltpu.VMEM)
    hbm = pl.BlockSpec(memory_space=pltpu.HBM)
    many = isinstance(outs, (list, tuple))
    out_specs = [hbm if i in hbm_out else vm for i in range(len(outs) if many else 1)]
    args = [
        pltpu.with_memory_space_constraint(a, pltpu.HBM) if i in hbm_in
        else pltpu.with_memory_space_constraint(a, pltpu.VMEM) if i in vmem_in
        else a
        for i, a in enumerate(args)
    ]
    return pl.pallas_call(
        body,
        out_shape=outs,
        in_specs=[hbm if i in hbm_in else vm for i in range(len(args))],
        out_specs=out_specs if many else out_specs[0],
        scratch_shapes=scratch,
        compiler_params=pltpu.CompilerParams(vmem_limit_bytes=32 * 2**20),
        name=name,
    )(*args)


def shape(*dims, dtype=f32):
    return jax.ShapeDtypeStruct(dims, dtype)


CELLS = pltpu.VMEM((C, XY, N), f32)
CELLS_LOW = pltpu.VMEM((C, XY, N), bf16)
CELLS_KEPT = pltpu.VMEM((C, XY, N), KEPT)
OWN = pltpu.VMEM((8, LANES), f32)


def run_prepare(skip_weight, mlp_in, mlp_out, skip_bias, field, cotangent):
    return call(
        k_prepare, "prepare",
        [shape(3, 256, 256, dtype=bf16), pltpu.HBM((C, XY, N), KEPT), pltpu.HBM((C, XY, N), KEPT)],
        [CELLS_LOW, CELLS_LOW, CELLS_KEPT, CELLS_KEPT, pltpu.SemaphoreType.DMA((2,))],
        skip_weight, mlp_in, mlp_out, skip_bias.reshape(1, C), field, cotangent, hbm_in=(4, 5), hbm_out=(1, 2),
    )


def run_middle(recv, field, cotangent, pre, dact, kron, table, offset):
    turn = pltpu.VMEM((2 * PX, PY * C, LANES), f32)
    square = pltpu.VMEM((256, 256), f32)
    return call(
        k_middle, "middle",
        [shape(PEERS * ROWS, LANES), pltpu.HBM((C, XY, N), bf16)],
        [CELLS_LOW, CELLS_LOW, CELLS_KEPT, CELLS_KEPT, pltpu.VMEM((2, 256, 256), bf16), CELLS_LOW,
         pltpu.SemaphoreType.DMA((10,)), turn, CELLS, square, square, square],
        recv, field, cotangent, pre, dact, kron, table, offset, hbm_in=(1, 2, 3, 4, 5), hbm_out=(1,),
    )


def shards(field, cotangent, spec_weight, skip_weight, skip_bias, mlp_in, mlp_out):
    table, offset = [jnp.asarray(t) for t in tables()]
    field = field.reshape(C, XY, N)
    cotangent = cotangent.reshape(C, XY, N)
    weight = spec_weight.reshape(2, C, C, ML * C)
    wa = jnp.concatenate([weight[0], weight[0]], axis=2)
    wb = jnp.concatenate([-weight[1], weight[1]], axis=2)
    turn = pltpu.VMEM((PX, PY * C, LANES), f32)
    twice = pltpu.VMEM((2 * PX, PY * C, LANES), f32)
    whole = pltpu.VMEM((4 * XY + 2 * C, PX * LANES), bf16)

    def exchange(block):
        return lax.all_to_all(block, ("px", "py"), 0, 0, tiled=True)

    def exchange_rows(block):
        return exchange(block.reshape(PEERS, 1, ROWS * LANES)).reshape(PEERS * ROWS, LANES)

    sent = call(
        k_forward, "forward", pltpu.HBM((PEERS, C, LANES), f32),
        [pltpu.VMEM((PEERS, C, LANES), f32), CELLS_LOW, whole, OWN, turn, pltpu.SemaphoreType.DMA((7 + PX,))],
        field, table, offset, hbm_in=range(3), hbm_out=(0,),
    )
    kron, pre, dact = run_prepare(
        skip_weight, mlp_in, mlp_out, skip_bias, field, cotangent
    )
    u, sent = call(
        k_mix, "mix", [shape(C, LANES), pltpu.HBM((PEERS, C, LANES), f32)],
        [pltpu.VMEM((8, C, LANES), f32), pltpu.SemaphoreType.DMA((PEERS // 8,))],
        exchange(sent), wa, wb, vmem_in=(1, 2), hbm_out=(1,),
    )
    sent, dpre = run_middle(
        exchange(sent), field, cotangent, pre, dact, kron, table, offset
    )
    sent, g = call(
        k_mix_back, "mix_back", [shape(PEERS * ROWS, LANES), shape(C, LANES)], [],
        exchange_rows(sent), wa, wb, vmem_in=(1, 2),
    )
    back = exchange_rows(sent)
    share = call(
        k_share, "share", pltpu.HBM((NB, 2 * C + 8, LANES), f32),
        [pltpu.VMEM((2 * C + 8, LANES), f32), pltpu.SemaphoreType.DMA((NB,))], back, u, g, hbm_out=(0,),
    )
    share = lax.all_to_all(share, "batch", 0, 0, tiled=True)
    grad_input = call(
        k_input, "input_grad", shape(C, XY, N, dtype=bf16),
        [CELLS_LOW, twice, CELLS, pltpu.SemaphoreType.DMA((STEPS,))],
        back, dpre, kron, table, offset, hbm_out=(0,),
    )
    spec, skip, b, inner, outer = call(
        k_shared, "shared",
        [shape(2, C, ML, 2, C), shape(C, C), shape(C), shape(C, C), shape(C, C)],
        [pltpu.VMEM((256, LANES), f32)] * 2, share,
    )
    spec = spec.transpose(0, 1, 4, 2, 3).reshape(2, C, C, 1, ML, 2)
    return (grad_input.reshape(1, C, XL, YL, N), spec, skip, b, inner, outer)


def solution(mesh):
    placed = (
        P("batch", None, "px", "py", None),
        P("batch", None, "px", "py", None),
        P(None, None, None, "py", "px", None),
        P(),
        P(),
        P(),
        P(),
    )
    return jax.shard_map(
        shards,
        mesh=mesh,
        in_specs=placed,
        out_specs=(
            P("batch", None, "px", "py", None),
            P(None, None, None, "py", "px", "batch"),
            P(),
            P(),
            P(),
            P(),
        ),
        check_vma=False,
    )
```

```python
import math

import jax
import jax.numpy as jnp
import ml_dtypes
import numpy as np
from jax import lax
from jax.experimental import pallas as pl
from jax.experimental.pallas import tpu as pltpu
from jax.sharding import PartitionSpec as P

f32 = jnp.float32
bf16 = jnp.bfloat16
C = 16
N = 128
PX, PY, NB = 4, 16, 8
XL, YL = N // PX, N // PY
XY = XL * YL
ML = C // PX
PEERS = PX * PY
STEPS = XY // 32
HALF = XY // 2
ROWS = C + 1
LANES = 128
SIGMA = 1.0 / math.sqrt(N**3)
RHO = 1.0 / math.sqrt(NB * N**3)
KEPT = f32
NT = (((1,), (1,)), ((), ()))


def tables():
    turn = lambda r, n: 2.0 * np.pi * (np.mod(r, n) / n)
    freq = np.where(np.arange(C) < C // 2, np.arange(C), np.arange(C) - C)
    depth = turn(np.arange(C)[:, None] * np.arange(N)[None, :], N)
    cos_z, sin_z = np.cos(depth), np.sin(depth)
    low = np.concatenate([cos_z, -sin_z]).astype(ml_dtypes.bfloat16)
    ax = turn(np.arange(XL)[:, None] * freq[None, :], N)
    ay = turn(np.arange(YL)[:, None] * freq[None, :], N)
    phase = ax[:, None, None, :] + ay[None, :, :, None]
    phase = phase.reshape(XY, PX, ML * C)
    co, si = np.cos(phase), np.sin(phase)
    plane = np.stack([co, -si], axis=2).reshape(XY, PX * LANES)
    plane_hi = plane.astype(ml_dtypes.bfloat16)
    plane_lo = (plane - plane_hi.astype(np.float64)).astype(ml_dtypes.bfloat16)
    ox = turn(np.arange(PX)[:, None] * XL * freq[None, :], N)
    oy = turn(np.arange(PY)[:, None] * YL * freq[None, :], N)
    off = ox[:, None, None, :] + oy[None, :, :, None]
    off = off.reshape(PEERS, PX, ML * C)
    cs = np.concatenate([np.cos(off), np.cos(off)], axis=2)
    sn = np.concatenate([np.sin(off), np.sin(off)], axis=2)
    offset = (np.concatenate([cs, sn], axis=1) * SIGMA).astype(np.float32)
    eye = np.eye(8)
    synth = np.concatenate(
        [
            np.einsum("ab,kz->akbz", eye, cos_z).reshape(8 * C, 8 * N),
            np.einsum("ab,kz->akbz", eye, -sin_z).reshape(8 * C, 8 * N),
        ]
    ).astype(ml_dtypes.bfloat16)
    low = np.pad(low.astype(np.float32), ((0, 0), (0, PX * LANES - N))).astype(ml_dtypes.bfloat16)
    table = np.concatenate([plane_hi, plane_lo, synth[:, : 4 * N], synth[:, 4 * N :], low])
    return table, offset


class Table:
    def __init__(self, ref):
        self.hi = ref.at[0:XY, :]
        self.lo = ref.at[XY : 2 * XY, :]
        self.synth = [ref.at[2 * XY : 3 * XY, :], ref.at[3 * XY : 4 * XY, :]]
        self.low = ref.at[4 * XY : 4 * XY + 2 * C, 0:N]


def dot(a, b):
    return jnp.dot(a, b, preferred_element_type=f32)


def dot_nt(a, b):
    return lax.dot_general(a, b, NT, preferred_element_type=f32)


def split(a):
    hi = a.astype(bf16)
    return hi, (a - hi.astype(f32)).astype(bf16)


def halves():
    lane = lax.broadcasted_iota(jnp.int32, (1, LANES), 1)
    return jnp.where(lane < LANES // 2, -1.0, 1.0)


def turned(v):
    return halves() * pltpu.roll(v, LANES // 2, 1)


def my_place():
    return lax.axis_index("px") * PY + lax.axis_index("py")


def forward_part(get, table, off_ref, turn_ref, put, ready=None, done=None):
    low = table.low[...]
    rows = [dot_nt(low, get(c)) for c in range(C)]
    both = jnp.concatenate([r[:C] for r in rows] + [r[C:] for r in rows], axis=0)
    x_hi, x_lo = split(both)
    if ready is not None:
        ready()
    hi = table.hi[...]
    part = dot(x_hi, hi) + dot(x_lo, hi) + dot(x_hi, table.lo[...])
    for mb in range(PX):
        pa = part[: C * C, mb * LANES : (mb + 1) * LANES]
        pb = part[C * C :, mb * LANES : (mb + 1) * LANES]
        co, si = off_ref[mb : mb + 1, :], off_ref[PX + mb : PX + mb + 1, :]
        turn_ref[mb] = (pa * co + pb * si) + turned(pb * co - pa * si)
        for k in range(C):
            put(mb * PY + k, turn_ref[mb, pl.ds(k, C, stride=C), :])
        if done is not None:
            done(mb)


def inverse_part(block, table, off_ref, turn_ref, g_ref):
    for mb in range(PX):
        v = jnp.concatenate([block(mb * PY + k) for k in range(PY)], axis=0)
        r = turned(v)
        co, si = off_ref[mb : mb + 1, :], off_ref[PX + mb : PX + mb + 1, :]
        turn_ref[mb] = v * co + r * si
        turn_ref[PX + mb] = v * si - r * co
    rows = []
    for half in range(2):
        for o in range(C):
            rows.append(
                jnp.concatenate(
                    [turn_ref[half * PX + mb, pl.ds(o, C, stride=C), :] for mb in range(PX)], axis=1
                )
            )
    v_hi, v_lo = split(jnp.concatenate(rows, axis=0))
    hi = table.hi[...]
    z = dot_nt(hi, v_hi) + dot_nt(hi, v_lo) + dot_nt(table.lo[...], v_hi)
    z = z.astype(bf16)
    for ob in range(2):
        re = z[:, ob * LANES : (ob + 1) * LANES]
        im = z[:, C * C + ob * LANES : C * C + (ob + 1) * LANES]
        both = jnp.concatenate([re, im], axis=1)
        for half in range(2):
            g = dot(both, table.synth[half][...])
            for o in range(4):
                g_ref[ob * 8 + half * 4 + o] = g[:, o * N : (o + 1) * N]


def k_forward(
    field_hbm, table_hbm, offset_hbm, out_hbm, out_ref, field_ref, table_ref, off_ref, turn_ref, sems
):
    low_rows, plane_rows = pl.ds(4 * XY, 2 * C), pl.ds(0, 2 * XY)
    pairs = [(table_hbm.at[low_rows], table_ref.at[low_rows])]
    for i in range(4):
        part = pl.ds(4 * i, 4)
        pairs.append((field_hbm.at[part], field_ref.at[part]))
    pairs.append((table_hbm.at[plane_rows], table_ref.at[plane_rows]))
    pairs.append((offset_hbm.at[my_place()], off_ref))
    copies = [pltpu.make_async_copy(a, b, sems.at[i]) for i, (a, b) in enumerate(pairs)]
    for copy in copies:
        copy.start()
    copies[0].wait()

    def get(c):
        if c % 4 == 0:
            copies[1 + c // 4].wait()
        return field_ref[c]

    def ready():
        for copy in copies[5:]:
            copy.wait()

    def put(d, value):
        out_ref[d] = value

    sent = []

    def done(mb):
        part = pl.ds(mb * PY, PY)
        sent.append(pltpu.make_async_copy(out_ref.at[part], out_hbm.at[part], sems.at[7 + mb]))
        sent[-1].start()

    forward_part(get, Table(table_ref), off_ref, turn_ref, put, ready, done)
    for copy in sent:
        copy.wait()


def spread_map(w, transpose):
    r = lax.broadcasted_iota(jnp.int32, (256, C), 0)
    l = lax.broadcasted_iota(jnp.int32, (256, C), 1)
    rep = jnp.where(r // 16 == l, 1.0, 0.0).astype(bf16)
    if transpose:
        wide = lax.dot_general(w, rep, (((0,), (1,)), ((), ())), preferred_element_type=f32)
    else:
        wide = dot_nt(w, rep)
    full = dot(rep, wide.astype(bf16))
    r = lax.broadcasted_iota(jnp.int32, (256, 256), 0)
    l = lax.broadcasted_iota(jnp.int32, (256, 256), 1)
    return jnp.where(r % 16 == l % 16, full, 0.0).astype(bf16)


def k_prepare(
    skip_ref, in_ref, outer_ref, bias_in_ref, field_hbm, cot_hbm,
    kron_ref, pre_hbm, dact_hbm, field_ref, cot_ref, pre_ref, dact_ref, sems,
):
    copies = [
        pltpu.make_async_copy(field_hbm, field_ref, sems.at[0]),
        pltpu.make_async_copy(cot_hbm, cot_ref, sems.at[1]),
    ]
    for copy in copies:
        copy.start()
    skip = spread_map(skip_ref[...], False)
    outer = spread_map(outer_ref[...], True)
    kron_ref[0] = spread_map(in_ref[...], False)
    kron_ref[1] = spread_map(in_ref[...], True)
    kron_ref[2] = spread_map(skip_ref[...], True)
    r = lax.broadcasted_iota(jnp.int32, (256, C), 0)
    l = lax.broadcasted_iota(jnp.int32, (256, C), 1)
    bias = jnp.sum(jnp.where(r // 16 == l, bias_in_ref[...], 0.0), axis=1, keepdims=True)
    for copy in copies:
        copy.wait()

    def step(p, carry):
        untile(pre_ref, p, (dot(skip, tile(field_ref, p)) + bias).astype(KEPT))
        untile(dact_ref, p, dot(outer, tile(cot_ref, p)).astype(KEPT))
        return carry

    lax.fori_loop(0, STEPS, step, 0, unroll=2)
    copies = [
        pltpu.make_async_copy(pre_ref, pre_hbm, sems.at[0]),
        pltpu.make_async_copy(dact_ref, dact_hbm, sems.at[1]),
    ]
    for copy in copies:
        copy.start()
    for copy in copies:
        copy.wait()


def k_mix(recv_ref, wa_ref, wb_ref, u_ref, out_hbm, eight_ref, sems):
    u = jnp.sum(recv_ref[...], axis=0)
    us = pltpu.roll(u, LANES // 2, 1)
    u_ref[...] = u
    v = jnp.zeros((C, LANES), f32)
    for c in range(C):
        v = v + wa_ref[c] * u[c : c + 1, :] + wb_ref[c] * us[c : c + 1, :]
    eight_ref[...] = jnp.broadcast_to(v[None], (8, C, LANES))
    copies = [
        pltpu.make_async_copy(eight_ref, out_hbm.at[pl.ds(8 * i, 8)], sems.at[i])
        for i in range(PEERS // 8)
    ]
    for copy in copies:
        copy.start()
    for copy in copies:
        copy.wait()


def gelu_parts(x):
    a = math.sqrt(2.0 / math.pi)
    b = a * 0.044715
    x2 = x * x
    h = 0.5 * jnp.tanh(x * (a + b * x2)) + 0.5
    g = x * h
    d = h + g * (1.0 - h) * (2.0 * a + (6.0 * b) * x2)
    return g, d


def tile(ref, p):
    left = ref[:, pl.ds(p * 32, 16), :].reshape(C * 16, N)
    right = ref[:, pl.ds(p * 32 + 16, 16), :].reshape(C * 16, N)
    return jnp.concatenate([left, right], axis=1)


def untile(ref, p, value):
    ref[:, pl.ds(p * 32, 16), :] = value[:, :N].reshape(C, 16, N)
    ref[:, pl.ds(p * 32 + 16, 16), :] = value[:, N:].reshape(C, 16, N)


def thirds(x):
    hi, rest = x.astype(bf16), x - x.astype(bf16).astype(f32)
    mid = rest.astype(bf16)
    return [hi, mid, (rest - mid.astype(f32)).astype(bf16)]


def picked(x, pick):
    n = x.shape[0]
    out = dot(jnp.concatenate(thirds(x), axis=0), pick)
    return out[:n] + out[n : 2 * n] + out[2 * n :]


def pack_rows(accs):
    r = lax.broadcasted_iota(jnp.int32, (256, 256), 0)
    l = lax.broadcasted_iota(jnp.int32, (256, 256), 1)
    same = r % 16 == l % 16
    kept = [jnp.where(same, a, 0.0).reshape(C, 16, 256).sum(axis=1) for a in accs]
    r = lax.broadcasted_iota(jnp.int32, (256, LANES), 0)
    l = lax.broadcasted_iota(jnp.int32, (256, LANES), 1)
    pick = jnp.where(r // 16 == l % 16, 1.0, 0.0).astype(bf16)
    spread = picked(jnp.concatenate(kept, axis=0), pick)
    r = lax.broadcasted_iota(jnp.int32, (len(accs) * C, LANES), 0)
    l = lax.broadcasted_iota(jnp.int32, (len(accs) * C, LANES), 1)
    return jnp.where(r % 8 == l // 16, spread, 0.0)


def k_middle(
    recv_ref, field_hbm, cot_hbm, pre_hbm, dact_hbm, kron_hbm, table_ref, offset_ref,
    out_ref, dpre_hbm,
    field_ref, cot_ref, pre_ref, dact_ref, kron_ref, dpre_ref, sems, turn_ref, g_ref, skip_acc, in_acc, out_acc,
):
    pairs = [(kron_hbm.at[0:2], kron_ref)]
    for i in range(2):
        part = pl.ds(i * HALF, HALF)
        for a, b in ((pre_hbm, pre_ref), (dact_hbm, dact_ref), (field_hbm, field_ref), (cot_hbm, cot_ref)):
            pairs.append((a.at[:, part], b.at[:, part]))
    copies = [pltpu.make_async_copy(a, b, sems.at[i]) for i, (a, b) in enumerate(pairs)]
    for copy in copies:
        copy.start()
    off_ref = offset_ref.at[my_place()]
    table = Table(table_ref)
    inverse_part(lambda d: recv_ref[d], table, off_ref, turn_ref, g_ref)
    skip_acc[...] = jnp.zeros_like(skip_acc)
    in_acc[...] = jnp.zeros_like(in_acc)
    out_acc[...] = jnp.zeros_like(out_acc)

    kept, sums = [], []

    def step(p):
        f = tile(field_ref, p)
        cot = tile(cot_ref, p)
        pre = tile(g_ref, p) + tile(pre_ref, p)
        hid, d_hid = gelu_parts(pre)
        hid = hid.astype(bf16)
        act, d_act = gelu_parts(dot(kron_ref[0], hid))
        act = act.astype(bf16)
        d_inner = (tile(dact_ref, p) * d_act).astype(bf16)
        dpre = dot(kron_ref[1], d_inner) * d_hid
        dpre = dpre.astype(bf16)
        untile(dpre_ref, p, dpre)
        kept.append((dpre, f, d_inner, hid, cot, act))
        if p % 2:
            wide = lambda i: jnp.concatenate([k[i] for k in kept[-2:]], axis=1)
            skip_acc[...] += dot_nt(wide(0), wide(1))
            in_acc[...] += dot_nt(wide(2), wide(3))
            out_acc[...] += dot_nt(wide(4), wide(5))
        sums.append(dpre.astype(f32).reshape(C, 16, 256).sum(axis=1))

    copies[0].wait()
    left = []
    for p in range(STEPS):
        if p % (STEPS // 2) == 0:
            first = 1 + 4 * (p // (STEPS // 2))
            for copy in copies[first : first + 4]:
                copy.wait()
        step(p)
        if p % (STEPS // 2) == STEPS // 2 - 1:
            part = pl.ds((p // (STEPS // 2)) * HALF, HALF)
            left.append(pltpu.make_async_copy(dpre_ref.at[:, part], dpre_hbm.at[:, part], sems.at[9 + len(left)]))
            left[-1].start()
    bias = sum(sums)
    total = jnp.sum(bias, axis=1, keepdims=True)
    r = lax.broadcasted_iota(jnp.int32, (C, LANES), 0)
    l = lax.broadcasted_iota(jnp.int32, (C, LANES), 1)
    bias_row = jnp.sum(jnp.where(r == l, total, 0.0), axis=0, keepdims=True)
    small = jnp.concatenate(
        [pack_rows([skip_acc[...], in_acc[...], out_acc[...]]),
         bias_row, jnp.zeros((C - 1, LANES), f32)], axis=0
    )

    def put(d, value):
        out_ref[d * ROWS : (d + 1) * ROWS, :] = jnp.concatenate([value, small[d : d + 1]], axis=0)

    forward_part(lambda c: dpre_ref[c], table, off_ref, turn_ref, put)
    for copy in left:
        copy.wait()


def k_mix_back(recv_ref, wa_ref, wb_ref, out_ref, g_ref):
    slabs = recv_ref[...].reshape(8, 8 * ROWS, LANES).sum(axis=0)
    got = slabs[:ROWS]
    for i in range(1, 8):
        got = got + slabs[i * ROWS : (i + 1) * ROWS]
    g = got[:C]
    g_ref[...] = g
    gs = pltpu.roll(g, LANES // 2, 1)
    rows = []
    for c in range(C):
        rows.append(jnp.sum(wa_ref[c] * g - wb_ref[c] * gs, axis=0, keepdims=True))
    block = jnp.concatenate(rows + [got[C:]], axis=0)
    slab = jnp.concatenate([block] * 8, axis=0)
    for i in range(8):
        out_ref[i * 8 * ROWS : (i + 1) * 8 * ROWS, :] = slab


def k_share(back_ref, u_ref, g_ref, share_hbm, block_ref, sems):
    small = back_ref[pl.ds(C, PEERS, stride=ROWS), :].reshape(8, 8, LANES).sum(axis=1)
    block_ref[...] = jnp.concatenate([u_ref[...], g_ref[...], small], axis=0)
    copies = [pltpu.make_async_copy(block_ref, share_hbm.at[i], sems.at[i]) for i in range(NB)]
    for copy in copies:
        copy.start()
    for copy in copies:
        copy.wait()


def k_input(
    recv_ref, dpre_ref, kron_ref, table_ref, offset_ref, out_hbm,
    out_ref, turn_ref, g_ref, sems,
):
    steps = XY // 32
    off_ref = offset_ref.at[my_place()]
    inverse_part(
        lambda d: recv_ref[d * ROWS : d * ROWS + C, :], Table(table_ref), off_ref, turn_ref, g_ref
    )
    copies = []
    for p in range(steps):
        untile(out_ref, p, (dot(kron_ref[2], tile(dpre_ref, p)) + tile(g_ref, p)).astype(bf16))
        part = pl.ds(p * 32, 32)
        copies.append(pltpu.make_async_copy(out_ref.at[:, part], out_hbm.at[:, part], sems.at[p]))
        copies[-1].start()
    for copy in copies:
        copy.wait()


def k_shared(recv_ref, spec_ref, skip_ref, bias_ref, in_ref, outer_ref, pa_ref, pb_ref):
    gs = [recv_ref[s, C : 2 * C, :] for s in range(NB)]
    turns = [pltpu.roll(g, LANES // 2, 1) for g in gs]
    for c in range(C):
        us = [recv_ref[s, c : c + 1, :] for s in range(NB)]
        pa_ref[c * C : (c + 1) * C, :] = sum(u * g for u, g in zip(us, gs))
        pb_ref[c * C : (c + 1) * C, :] = sum(u * g for u, g in zip(us, turns))
    b = lax.axis_index("batch")
    r = lax.broadcasted_iota(jnp.int32, (8, LANES), 0)
    l = lax.broadcasted_iota(jnp.int32, (8, LANES), 1)
    mine = ((l % 64) // C == r // 2) & (l % C == 2 * b + r % 2)
    sel_a = jnp.where(mine, 1.0, 0.0)
    sel_b = jnp.where(l < 64, sel_a, -sel_a)
    for i, (sel, ref) in enumerate(((sel_a, pa_ref), (sel_b, pb_ref))):
        part = sum(dot_nt(sel.astype(bf16), third) for third in thirds(ref[...]))
        for c in range(C):
            for m in range(ML):
                spec_ref[i, c, m] = part[2 * m : 2 * m + 2, c * C : (c + 1) * C]
    small = jnp.sum(recv_ref[:, 2 * C :, :], axis=0) * RHO
    r = lax.broadcasted_iota(jnp.int32, (3 * C, LANES), 0)
    l = lax.broadcasted_iota(jnp.int32, (3 * C, LANES), 1)
    pr = lax.broadcasted_iota(jnp.int32, (LANES, C), 0)
    pc = lax.broadcasted_iota(jnp.int32, (LANES, C), 1)
    pick = jnp.where(pr % C == pc, 1.0, 0.0).astype(bf16)
    rows = jnp.concatenate([jnp.broadcast_to(small[i : i + 1], (8, LANES)) for i in range(6)], axis=0)
    maps = picked(jnp.where(l // C == r % 8, rows, 0.0), pick)
    for i, ref in enumerate((skip_ref, in_ref, outer_ref)):
        ref[...] = maps[i * C : (i + 1) * C]
    bias_ref[...] = small[6, :C]


def call(body, name, outs, scratch, *args, hbm_in=(), vmem_in=(), hbm_out=()):
    vm = pl.BlockSpec(memory_space=pltpu.VMEM)
    hbm = pl.BlockSpec(memory_space=pltpu.HBM)
    many = isinstance(outs, (list, tuple))
    out_specs = [hbm if i in hbm_out else vm for i in range(len(outs) if many else 1)]
    args = [
        pltpu.with_memory_space_constraint(a, pltpu.HBM) if i in hbm_in
        else pltpu.with_memory_space_constraint(a, pltpu.VMEM) if i in vmem_in
        else a
        for i, a in enumerate(args)
    ]
    return pl.pallas_call(
        body,
        out_shape=outs,
        in_specs=[hbm if i in hbm_in else vm for i in range(len(args))],
        out_specs=out_specs if many else out_specs[0],
        scratch_shapes=scratch,
        compiler_params=pltpu.CompilerParams(vmem_limit_bytes=32 * 2**20),
        name=name,
    )(*args)


def shape(*dims, dtype=f32):
    return jax.ShapeDtypeStruct(dims, dtype)


CELLS = pltpu.VMEM((C, XY, N), f32)
CELLS_LOW = pltpu.VMEM((C, XY, N), bf16)
CELLS_KEPT = pltpu.VMEM((C, XY, N), KEPT)
OWN = pltpu.VMEM((8, LANES), f32)


def run_prepare(skip_weight, mlp_in, mlp_out, skip_bias, field, cotangent):
    return call(
        k_prepare, "prepare",
        [shape(3, 256, 256, dtype=bf16), pltpu.HBM((C, XY, N), KEPT), pltpu.HBM((C, XY, N), KEPT)],
        [CELLS_LOW, CELLS_LOW, CELLS_KEPT, CELLS_KEPT, pltpu.SemaphoreType.DMA((2,))],
        skip_weight, mlp_in, mlp_out, skip_bias.reshape(1, C), field, cotangent, hbm_in=(4, 5), hbm_out=(1, 2),
    )


def run_middle(recv, field, cotangent, pre, dact, kron, table, offset):
    turn = pltpu.VMEM((2 * PX, PY * C, LANES), f32)
    square = pltpu.VMEM((256, 256), f32)
    return call(
        k_middle, "middle",
        [shape(PEERS * ROWS, LANES), pltpu.HBM((C, XY, N), bf16)],
        [CELLS_LOW, CELLS_LOW, CELLS_KEPT, CELLS_KEPT, pltpu.VMEM((2, 256, 256), bf16), CELLS_LOW,
         pltpu.SemaphoreType.DMA((11,)), turn, CELLS, square, square, square],
        recv, field, cotangent, pre, dact, kron, table, offset, hbm_in=(1, 2, 3, 4, 5), hbm_out=(1,),
    )


def shards(field, cotangent, spec_weight, skip_weight, skip_bias, mlp_in, mlp_out):
    table, offset = [jnp.asarray(t) for t in tables()]
    field = field.reshape(C, XY, N)
    cotangent = cotangent.reshape(C, XY, N)
    weight = spec_weight.reshape(2, C, C, ML * C)
    wa = jnp.concatenate([weight[0], weight[0]], axis=2)
    wb = jnp.concatenate([-weight[1], weight[1]], axis=2)
    turn = pltpu.VMEM((PX, PY * C, LANES), f32)
    twice = pltpu.VMEM((2 * PX, PY * C, LANES), f32)
    whole = pltpu.VMEM((4 * XY + 2 * C, PX * LANES), bf16)

    def exchange(block):
        return lax.all_to_all(block, ("px", "py"), 0, 0, tiled=True)

    def exchange_rows(block):
        return exchange(block.reshape(PEERS, 1, ROWS * LANES)).reshape(PEERS * ROWS, LANES)

    sent = call(
        k_forward, "forward", pltpu.HBM((PEERS, C, LANES), f32),
        [pltpu.VMEM((PEERS, C, LANES), f32), CELLS_LOW, whole, OWN, turn, pltpu.SemaphoreType.DMA((7 + PX,))],
        field, table, offset, hbm_in=range(3), hbm_out=(0,),
    )
    kron, pre, dact = run_prepare(
        skip_weight, mlp_in, mlp_out, skip_bias, field, cotangent
    )
    u, sent = call(
        k_mix, "mix", [shape(C, LANES), pltpu.HBM((PEERS, C, LANES), f32)],
        [pltpu.VMEM((8, C, LANES), f32), pltpu.SemaphoreType.DMA((PEERS // 8,))],
        exchange(sent), wa, wb, vmem_in=(1, 2), hbm_out=(1,),
    )
    sent, dpre = run_middle(
        exchange(sent), field, cotangent, pre, dact, kron, table, offset
    )
    sent, g = call(
        k_mix_back, "mix_back", [shape(PEERS * ROWS, LANES), shape(C, LANES)], [],
        exchange_rows(sent), wa, wb, vmem_in=(1, 2),
    )
    back = exchange_rows(sent)
    share = call(
        k_share, "share", pltpu.HBM((NB, 2 * C + 8, LANES), f32),
        [pltpu.VMEM((2 * C + 8, LANES), f32), pltpu.SemaphoreType.DMA((NB,))], back, u, g, hbm_out=(0,),
    )
    share = lax.all_to_all(share, "batch", 0, 0, tiled=True)
    grad_input = call(
        k_input, "input_grad", shape(C, XY, N, dtype=bf16),
        [CELLS_LOW, twice, CELLS, pltpu.SemaphoreType.DMA((STEPS,))],
        back, dpre, kron, table, offset, hbm_out=(0,),
    )
    spec, skip, b, inner, outer = call(
        k_shared, "shared",
        [shape(2, C, ML, 2, C), shape(C, C), shape(C), shape(C, C), shape(C, C)],
        [pltpu.VMEM((256, LANES), f32)] * 2, share,
    )
    spec = spec.transpose(0, 1, 4, 2, 3).reshape(2, C, C, 1, ML, 2)
    return (grad_input.reshape(1, C, XL, YL, N), spec, skip, b, inner, outer)


def solution(mesh):
    placed = (
        P("batch", None, "px", "py", None),
        P("batch", None, "px", "py", None),
        P(None, None, None, "py", "px", None),
        P(),
        P(),
        P(),
        P(),
    )
    return jax.shard_map(
        shards,
        mesh=mesh,
        in_specs=placed,
        out_specs=(
            P("batch", None, "px", "py", None),
            P(None, None, None, "py", "px", "batch"),
            P(),
            P(),
            P(),
            P(),
        ),
        check_vma=False,
    )
```

```python
import math

import jax
import jax.numpy as jnp
import ml_dtypes
import numpy as np
from jax import lax
from jax.experimental import pallas as pl
from jax.experimental.pallas import tpu as pltpu
from jax.sharding import PartitionSpec as P

f32 = jnp.float32
bf16 = jnp.bfloat16
C = 16
N = 128
PX, PY, NB = 4, 16, 8
XL, YL = N // PX, N // PY
XY = XL * YL
ML = C // PX
PEERS = PX * PY
STEPS = XY // 32
HALF = XY // 2
ROWS = C + 1
LANES = 128
SIGMA = 1.0 / math.sqrt(N**3)
RHO = 1.0 / math.sqrt(NB * N**3)
KEPT = f32
NT = (((1,), (1,)), ((), ()))


def tables():
    turn = lambda r, n: 2.0 * np.pi * (np.mod(r, n) / n)
    freq = np.where(np.arange(C) < C // 2, np.arange(C), np.arange(C) - C)
    depth = turn(np.arange(C)[:, None] * np.arange(N)[None, :], N)
    cos_z, sin_z = np.cos(depth), np.sin(depth)
    low = np.concatenate([cos_z, -sin_z]).astype(ml_dtypes.bfloat16)
    ax = turn(np.arange(XL)[:, None] * freq[None, :], N)
    ay = turn(np.arange(YL)[:, None] * freq[None, :], N)
    phase = ax[:, None, None, :] + ay[None, :, :, None]
    phase = phase.reshape(XY, PX, ML * C)
    co, si = np.cos(phase), np.sin(phase)
    plane = np.stack([co, -si], axis=2).reshape(XY, PX * LANES)
    plane_hi = plane.astype(ml_dtypes.bfloat16)
    plane_lo = (plane - plane_hi.astype(np.float64)).astype(ml_dtypes.bfloat16)
    ox = turn(np.arange(PX)[:, None] * XL * freq[None, :], N)
    oy = turn(np.arange(PY)[:, None] * YL * freq[None, :], N)
    off = ox[:, None, None, :] + oy[None, :, :, None]
    off = off.reshape(PEERS, PX, ML * C)
    cs = np.concatenate([np.cos(off), np.cos(off)], axis=2)
    sn = np.concatenate([np.sin(off), np.sin(off)], axis=2)
    offset = (np.concatenate([cs, sn], axis=1) * SIGMA).astype(np.float32)
    eye = np.eye(8)
    synth = np.concatenate(
        [
            np.einsum("ab,kz->akbz", eye, cos_z).reshape(8 * C, 8 * N),
            np.einsum("ab,kz->akbz", eye, -sin_z).reshape(8 * C, 8 * N),
        ]
    ).astype(ml_dtypes.bfloat16)
    low = np.pad(low.astype(np.float32), ((0, 0), (0, PX * LANES - N))).astype(ml_dtypes.bfloat16)
    table = np.concatenate([plane_hi, plane_lo, synth[:, : 4 * N], synth[:, 4 * N :], low])
    return table, offset


class Table:
    def __init__(self, ref):
        self.hi = ref.at[0:XY, :]
        self.lo = ref.at[XY : 2 * XY, :]
        self.synth = [ref.at[2 * XY : 3 * XY, :], ref.at[3 * XY : 4 * XY, :]]
        self.low = ref.at[4 * XY : 4 * XY + 2 * C, 0:N]


def dot(a, b):
    return jnp.dot(a, b, preferred_element_type=f32)


def dot_nt(a, b):
    return lax.dot_general(a, b, NT, preferred_element_type=f32)


def split(a):
    hi = a.astype(bf16)
    return hi, (a - hi.astype(f32)).astype(bf16)


def halves():
    lane = lax.broadcasted_iota(jnp.int32, (1, LANES), 1)
    return jnp.where(lane < LANES // 2, -1.0, 1.0)


def turned(v):
    return halves() * pltpu.roll(v, LANES // 2, 1)


def my_place():
    return lax.axis_index("px") * PY + lax.axis_index("py")


def forward_part(get, table, off_ref, turn_ref, put, ready=None, done=None):
    low = table.low[...]
    rows = [dot_nt(low, get(c)) for c in range(C)]
    both = jnp.concatenate([r[:C] for r in rows] + [r[C:] for r in rows], axis=0)
    x_hi, x_lo = split(both)
    if ready is not None:
        ready()
    hi = table.hi[...]
    part = dot(x_hi, hi) + dot(x_lo, hi) + dot(x_hi, table.lo[...])
    for mb in range(PX):
        pa = part[: C * C, mb * LANES : (mb + 1) * LANES]
        pb = part[C * C :, mb * LANES : (mb + 1) * LANES]
        co, si = off_ref[mb : mb + 1, :], off_ref[PX + mb : PX + mb + 1, :]
        turn_ref[mb] = (pa * co + pb * si) + turned(pb * co - pa * si)
        for k in range(C):
            put(mb * PY + k, turn_ref[mb, pl.ds(k, C, stride=C), :])
        if done is not None:
            done(mb)


def inverse_part(block, table, off_ref, turn_ref, g_ref):
    for mb in range(PX):
        v = jnp.concatenate([block(mb * PY + k) for k in range(PY)], axis=0)
        r = turned(v)
        co, si = off_ref[mb : mb + 1, :], off_ref[PX + mb : PX + mb + 1, :]
        turn_ref[mb] = v * co + r * si
        turn_ref[PX + mb] = v * si - r * co
    rows = []
    for half in range(2):
        for o in range(C):
            rows.append(
                jnp.concatenate(
                    [turn_ref[half * PX + mb, pl.ds(o, C, stride=C), :] for mb in range(PX)], axis=1
                )
            )
    v_hi, v_lo = split(jnp.concatenate(rows, axis=0))
    hi = table.hi[...]
    z = dot_nt(hi, v_hi) + dot_nt(hi, v_lo) + dot_nt(table.lo[...], v_hi)
    z = z.astype(bf16)
    for ob in range(2):
        re = z[:, ob * LANES : (ob + 1) * LANES]
        im = z[:, C * C + ob * LANES : C * C + (ob + 1) * LANES]
        both = jnp.concatenate([re, im], axis=1)
        for half in range(2):
            g = dot(both, table.synth[half][...])
            for o in range(4):
                g_ref[ob * 8 + half * 4 + o] = g[:, o * N : (o + 1) * N]


def k_forward(
    field_hbm, table_hbm, offset_hbm, out_hbm, out_ref, field_ref, table_ref, off_ref, turn_ref, sems
):
    low_rows, hi_rows, lo_rows = pl.ds(4 * XY, 2 * C), pl.ds(0, XY), pl.ds(XY, XY)
    pairs = [(table_hbm.at[low_rows], table_ref.at[low_rows])]
    for i in range(4):
        part = pl.ds(4 * i, 4)
        pairs.append((field_hbm.at[part], field_ref.at[part]))
    for part in (hi_rows, lo_rows):
        pairs.append((table_hbm.at[part], table_ref.at[part]))
    pairs.append((offset_hbm.at[my_place()], off_ref))
    copies = [pltpu.make_async_copy(a, b, sems.at[i]) for i, (a, b) in enumerate(pairs)]
    for copy in copies:
        copy.start()
    copies[0].wait()

    def get(c):
        if c % 4 == 0:
            copies[1 + c // 4].wait()
        return field_ref[c]

    def ready():
        for copy in copies[5:]:
            copy.wait()

    def put(d, value):
        out_ref[d] = value

    sent = []

    def done(mb):
        part = pl.ds(mb * PY, PY)
        sent.append(pltpu.make_async_copy(out_ref.at[part], out_hbm.at[part], sems.at[8 + mb]))
        sent[-1].start()

    forward_part(get, Table(table_ref), off_ref, turn_ref, put, ready, done)
    for copy in sent:
        copy.wait()


def spread_map(w, transpose):
    r = lax.broadcasted_iota(jnp.int32, (256, C), 0)
    l = lax.broadcasted_iota(jnp.int32, (256, C), 1)
    rep = jnp.where(r // 16 == l, 1.0, 0.0).astype(bf16)
    if transpose:
        wide = lax.dot_general(w, rep, (((0,), (1,)), ((), ())), preferred_element_type=f32)
    else:
        wide = dot_nt(w, rep)
    full = dot(rep, wide.astype(bf16))
    r = lax.broadcasted_iota(jnp.int32, (256, 256), 0)
    l = lax.broadcasted_iota(jnp.int32, (256, 256), 1)
    return jnp.where(r % 16 == l % 16, full, 0.0).astype(bf16)


def k_prepare(
    skip_ref, in_ref, outer_ref, bias_in_ref, field_hbm, cot_hbm,
    kron_ref, pre_hbm, dact_hbm, field_ref, cot_ref, pre_ref, dact_ref, sems,
):
    copies = [
        pltpu.make_async_copy(field_hbm, field_ref, sems.at[0]),
        pltpu.make_async_copy(cot_hbm, cot_ref, sems.at[1]),
    ]
    for copy in copies:
        copy.start()
    skip = spread_map(skip_ref[...], False)
    outer = spread_map(outer_ref[...], True)
    kron_ref[0] = spread_map(in_ref[...], False)
    kron_ref[1] = spread_map(in_ref[...], True)
    kron_ref[2] = spread_map(skip_ref[...], True)
    r = lax.broadcasted_iota(jnp.int32, (256, C), 0)
    l = lax.broadcasted_iota(jnp.int32, (256, C), 1)
    bias = jnp.sum(jnp.where(r // 16 == l, bias_in_ref[...], 0.0), axis=1, keepdims=True)
    for copy in copies:
        copy.wait()

    def step(p, carry):
        untile(pre_ref, p, (dot(skip, tile(field_ref, p)) + bias).astype(KEPT))
        untile(dact_ref, p, dot(outer, tile(cot_ref, p)).astype(KEPT))
        return carry

    lax.fori_loop(0, STEPS, step, 0, unroll=2)
    copies = [
        pltpu.make_async_copy(pre_ref, pre_hbm, sems.at[0]),
        pltpu.make_async_copy(dact_ref, dact_hbm, sems.at[1]),
    ]
    for copy in copies:
        copy.start()
    for copy in copies:
        copy.wait()


def k_mix(recv_ref, wa_ref, wb_ref, u_ref, out_hbm, eight_ref, sems):
    u = jnp.sum(recv_ref[...], axis=0)
    us = pltpu.roll(u, LANES // 2, 1)
    u_ref[...] = u
    v = jnp.zeros((C, LANES), f32)
    for c in range(C):
        v = v + wa_ref[c] * u[c : c + 1, :] + wb_ref[c] * us[c : c + 1, :]
    eight_ref[...] = jnp.broadcast_to(v[None], (8, C, LANES))
    copies = [
        pltpu.make_async_copy(eight_ref, out_hbm.at[pl.ds(8 * i, 8)], sems.at[i])
        for i in range(PEERS // 8)
    ]
    for copy in copies:
        copy.start()
    for copy in copies:
        copy.wait()


def gelu_parts(x):
    a = math.sqrt(2.0 / math.pi)
    b = a * 0.044715
    x2 = x * x
    h = 0.5 * jnp.tanh(x * (a + b * x2)) + 0.5
    g = x * h
    d = h + g * (1.0 - h) * (2.0 * a + (6.0 * b) * x2)
    return g, d


def tile(ref, p):
    left = ref[:, pl.ds(p * 32, 16), :].reshape(C * 16, N)
    right = ref[:, pl.ds(p * 32 + 16, 16), :].reshape(C * 16, N)
    return jnp.concatenate([left, right], axis=1)


def untile(ref, p, value):
    ref[:, pl.ds(p * 32, 16), :] = value[:, :N].reshape(C, 16, N)
    ref[:, pl.ds(p * 32 + 16, 16), :] = value[:, N:].reshape(C, 16, N)


def thirds(x):
    hi, rest = x.astype(bf16), x - x.astype(bf16).astype(f32)
    mid = rest.astype(bf16)
    return [hi, mid, (rest - mid.astype(f32)).astype(bf16)]


def picked(x, pick):
    n = x.shape[0]
    out = dot(jnp.concatenate(thirds(x), axis=0), pick)
    return out[:n] + out[n : 2 * n] + out[2 * n :]


def pack_rows(accs):
    r = lax.broadcasted_iota(jnp.int32, (256, 256), 0)
    l = lax.broadcasted_iota(jnp.int32, (256, 256), 1)
    same = r % 16 == l % 16
    kept = [jnp.where(same, a, 0.0).reshape(C, 16, 256).sum(axis=1) for a in accs]
    r = lax.broadcasted_iota(jnp.int32, (256, LANES), 0)
    l = lax.broadcasted_iota(jnp.int32, (256, LANES), 1)
    pick = jnp.where(r // 16 == l % 16, 1.0, 0.0).astype(bf16)
    spread = picked(jnp.concatenate(kept, axis=0), pick)
    r = lax.broadcasted_iota(jnp.int32, (len(accs) * C, LANES), 0)
    l = lax.broadcasted_iota(jnp.int32, (len(accs) * C, LANES), 1)
    return jnp.where(r % 8 == l // 16, spread, 0.0)


def k_middle(
    recv_ref, field_hbm, cot_hbm, pre_hbm, dact_hbm, kron_hbm, table_ref, offset_ref,
    out_ref, dpre_hbm,
    field_ref, cot_ref, pre_ref, dact_ref, kron_ref, dpre_ref, sems, turn_ref, g_ref, skip_acc, in_acc, out_acc,
):
    pairs = [(kron_hbm.at[0:2], kron_ref)]
    for i in range(2):
        part = pl.ds(i * HALF, HALF)
        for a, b in ((pre_hbm, pre_ref), (dact_hbm, dact_ref), (field_hbm, field_ref), (cot_hbm, cot_ref)):
            pairs.append((a.at[:, part], b.at[:, part]))
    copies = [pltpu.make_async_copy(a, b, sems.at[i]) for i, (a, b) in enumerate(pairs)]
    for copy in copies:
        copy.start()
    off_ref = offset_ref.at[my_place()]
    table = Table(table_ref)
    inverse_part(lambda d: recv_ref[d], table, off_ref, turn_ref, g_ref)

    kept, sums = [], []

    def step(p):
        f = tile(field_ref, p)
        cot = tile(cot_ref, p)
        pre = tile(g_ref, p) + tile(pre_ref, p)
        hid, d_hid = gelu_parts(pre)
        hid = hid.astype(bf16)
        act, d_act = gelu_parts(dot(kron_ref[0], hid))
        act = act.astype(bf16)
        d_inner = (tile(dact_ref, p) * d_act).astype(bf16)
        dpre = dot(kron_ref[1], d_inner) * d_hid
        dpre = dpre.astype(bf16)
        untile(dpre_ref, p, dpre)
        kept.append((dpre, f, d_inner, hid, cot, act))
        if p % 2:
            wide = lambda i: jnp.concatenate([k[i] for k in kept[-2:]], axis=1)
            for i, acc in enumerate((skip_acc, in_acc, out_acc)):
                pair = dot_nt(wide(2 * i), wide(2 * i + 1))
                acc[...] = pair if p == 1 else acc[...] + pair
        sums.append(dpre.astype(f32).reshape(C, 16, 256).sum(axis=1))

    copies[0].wait()
    left = []
    for p in range(STEPS):
        if p % (STEPS // 2) == 0:
            first = 1 + 4 * (p // (STEPS // 2))
            for copy in copies[first : first + 4]:
                copy.wait()
        step(p)
        if p % (STEPS // 2) == STEPS // 2 - 1:
            part = pl.ds((p // (STEPS // 2)) * HALF, HALF)
            left.append(pltpu.make_async_copy(dpre_ref.at[:, part], dpre_hbm.at[:, part], sems.at[9 + len(left)]))
            left[-1].start()
    bias = sum(sums)
    total = jnp.sum(bias, axis=1, keepdims=True)
    r = lax.broadcasted_iota(jnp.int32, (C, LANES), 0)
    l = lax.broadcasted_iota(jnp.int32, (C, LANES), 1)
    bias_row = jnp.sum(jnp.where(r == l, total, 0.0), axis=0, keepdims=True)
    small = jnp.concatenate(
        [pack_rows([skip_acc[...], in_acc[...], out_acc[...]]),
         bias_row, jnp.zeros((C - 1, LANES), f32)], axis=0
    )

    def put(d, value):
        out_ref[d * ROWS : (d + 1) * ROWS, :] = jnp.concatenate([value, small[d : d + 1]], axis=0)

    forward_part(lambda c: dpre_ref[c], table, off_ref, turn_ref, put)
    for copy in left:
        copy.wait()


def k_mix_back(recv_ref, wa_ref, wb_ref, out_ref, g_ref):
    slabs = recv_ref[...].reshape(8, 8 * ROWS, LANES).sum(axis=0)
    got = slabs[:ROWS]
    for i in range(1, 8):
        got = got + slabs[i * ROWS : (i + 1) * ROWS]
    g = got[:C]
    g_ref[...] = g
    gs = pltpu.roll(g, LANES // 2, 1)
    rows = []
    for c in range(C):
        rows.append(jnp.sum(wa_ref[c] * g - wb_ref[c] * gs, axis=0, keepdims=True))
    block = jnp.concatenate(rows + [got[C:]], axis=0)
    slab = jnp.concatenate([block] * 8, axis=0)
    for i in range(8):
        out_ref[i * 8 * ROWS : (i + 1) * 8 * ROWS, :] = slab


def k_share(back_ref, u_ref, g_ref, share_hbm, block_ref, sems):
    small = back_ref[pl.ds(C, PEERS, stride=ROWS), :].reshape(8, 8, LANES).sum(axis=1)
    block_ref[...] = jnp.concatenate([u_ref[...], g_ref[...], small], axis=0)
    copies = [pltpu.make_async_copy(block_ref, share_hbm.at[i], sems.at[i]) for i in range(NB)]
    for copy in copies:
        copy.start()
    for copy in copies:
        copy.wait()


def k_input(
    recv_ref, dpre_ref, kron_ref, table_ref, offset_ref, out_hbm,
    out_ref, turn_ref, g_ref, sems,
):
    steps = XY // 32
    off_ref = offset_ref.at[my_place()]
    inverse_part(
        lambda d: recv_ref[d * ROWS : d * ROWS + C, :], Table(table_ref), off_ref, turn_ref, g_ref
    )
    copies = []
    for p in range(steps):
        untile(out_ref, p, (dot(kron_ref[2], tile(dpre_ref, p)) + tile(g_ref, p)).astype(bf16))
        part = pl.ds(p * 32, 32)
        copies.append(pltpu.make_async_copy(out_ref.at[:, part], out_hbm.at[:, part], sems.at[p]))
        copies[-1].start()
    for copy in copies:
        copy.wait()


def k_shared(recv_ref, spec_ref, skip_ref, bias_ref, in_ref, outer_ref, pa_ref, pb_ref):
    gs = [recv_ref[s, C : 2 * C, :] for s in range(NB)]
    turns = [pltpu.roll(g, LANES // 2, 1) for g in gs]
    for c in range(C):
        us = [recv_ref[s, c : c + 1, :] for s in range(NB)]
        pa_ref[c * C : (c + 1) * C, :] = sum(u * g for u, g in zip(us, gs))
        pb_ref[c * C : (c + 1) * C, :] = sum(u * g for u, g in zip(us, turns))
    b = lax.axis_index("batch")
    r = lax.broadcasted_iota(jnp.int32, (8, LANES), 0)
    l = lax.broadcasted_iota(jnp.int32, (8, LANES), 1)
    mine = ((l % 64) // C == r // 2) & (l % C == 2 * b + r % 2)
    sel_a = jnp.where(mine, 1.0, 0.0)
    sel_b = jnp.where(l < 64, sel_a, -sel_a)
    for i, (sel, ref) in enumerate(((sel_a, pa_ref), (sel_b, pb_ref))):
        part = sum(dot_nt(sel.astype(bf16), third) for third in thirds(ref[...]))
        for c in range(C):
            for m in range(ML):
                spec_ref[i, c, m] = part[2 * m : 2 * m + 2, c * C : (c + 1) * C]
    small = jnp.sum(recv_ref[:, 2 * C :, :], axis=0) * RHO
    r = lax.broadcasted_iota(jnp.int32, (3 * C, LANES), 0)
    l = lax.broadcasted_iota(jnp.int32, (3 * C, LANES), 1)
    pr = lax.broadcasted_iota(jnp.int32, (LANES, C), 0)
    pc = lax.broadcasted_iota(jnp.int32, (LANES, C), 1)
    pick = jnp.where(pr % C == pc, 1.0, 0.0).astype(bf16)
    rows = jnp.concatenate([jnp.broadcast_to(small[i : i + 1], (8, LANES)) for i in range(6)], axis=0)
    maps = picked(jnp.where(l // C == r % 8, rows, 0.0), pick)
    for i, ref in enumerate((skip_ref, in_ref, outer_ref)):
        ref[...] = maps[i * C : (i + 1) * C]
    bias_ref[...] = small[6, :C]


def call(body, name, outs, scratch, *args, hbm_in=(), vmem_in=(), hbm_out=()):
    vm = pl.BlockSpec(memory_space=pltpu.VMEM)
    hbm = pl.BlockSpec(memory_space=pltpu.HBM)
    many = isinstance(outs, (list, tuple))
    out_specs = [hbm if i in hbm_out else vm for i in range(len(outs) if many else 1)]
    args = [
        pltpu.with_memory_space_constraint(a, pltpu.HBM) if i in hbm_in
        else pltpu.with_memory_space_constraint(a, pltpu.VMEM) if i in vmem_in
        else a
        for i, a in enumerate(args)
    ]
    return pl.pallas_call(
        body,
        out_shape=outs,
        in_specs=[hbm if i in hbm_in else vm for i in range(len(args))],
        out_specs=out_specs if many else out_specs[0],
        scratch_shapes=scratch,
        compiler_params=pltpu.CompilerParams(vmem_limit_bytes=32 * 2**20),
        name=name,
    )(*args)


def shape(*dims, dtype=f32):
    return jax.ShapeDtypeStruct(dims, dtype)


CELLS = pltpu.VMEM((C, XY, N), f32)
CELLS_LOW = pltpu.VMEM((C, XY, N), bf16)
CELLS_KEPT = pltpu.VMEM((C, XY, N), KEPT)
OWN = pltpu.VMEM((8, LANES), f32)


def run_prepare(skip_weight, mlp_in, mlp_out, skip_bias, field, cotangent):
    return call(
        k_prepare, "prepare",
        [shape(3, 256, 256, dtype=bf16), pltpu.HBM((C, XY, N), KEPT), pltpu.HBM((C, XY, N), KEPT)],
        [CELLS_LOW, CELLS_LOW, CELLS_KEPT, CELLS_KEPT, pltpu.SemaphoreType.DMA((2,))],
        skip_weight, mlp_in, mlp_out, skip_bias.reshape(1, C), field, cotangent, hbm_in=(4, 5), hbm_out=(1, 2),
    )


def run_middle(recv, field, cotangent, pre, dact, kron, table, offset):
    turn = pltpu.VMEM((2 * PX, PY * C, LANES), f32)
    square = pltpu.VMEM((256, 256), f32)
    return call(
        k_middle, "middle",
        [shape(PEERS * ROWS, LANES), pltpu.HBM((C, XY, N), bf16)],
        [CELLS_LOW, CELLS_LOW, CELLS_KEPT, CELLS_KEPT, pltpu.VMEM((2, 256, 256), bf16), CELLS_LOW,
         pltpu.SemaphoreType.DMA((11,)), turn, CELLS, square, square, square],
        recv, field, cotangent, pre, dact, kron, table, offset, hbm_in=(1, 2, 3, 4, 5), hbm_out=(1,),
    )


def shards(field, cotangent, spec_weight, skip_weight, skip_bias, mlp_in, mlp_out):
    table, offset = [jnp.asarray(t) for t in tables()]
    field = field.reshape(C, XY, N)
    cotangent = cotangent.reshape(C, XY, N)
    weight = spec_weight.reshape(2, C, C, ML * C)
    wa = jnp.concatenate([weight[0], weight[0]], axis=2)
    wb = jnp.concatenate([-weight[1], weight[1]], axis=2)
    turn = pltpu.VMEM((PX, PY * C, LANES), f32)
    twice = pltpu.VMEM((2 * PX, PY * C, LANES), f32)
    whole = pltpu.VMEM((4 * XY + 2 * C, PX * LANES), bf16)

    def exchange(block):
        return lax.all_to_all(block, ("px", "py"), 0, 0, tiled=True)

    def exchange_rows(block):
        return exchange(block.reshape(PEERS, 1, ROWS * LANES)).reshape(PEERS * ROWS, LANES)

    sent = call(
        k_forward, "forward", pltpu.HBM((PEERS, C, LANES), f32),
        [pltpu.VMEM((PEERS, C, LANES), f32), CELLS_LOW, whole, OWN, turn, pltpu.SemaphoreType.DMA((8 + PX,))],
        field, table, offset, hbm_in=range(3), hbm_out=(0,),
    )
    kron, pre, dact = run_prepare(
        skip_weight, mlp_in, mlp_out, skip_bias, field, cotangent
    )
    u, sent = call(
        k_mix, "mix", [shape(C, LANES), pltpu.HBM((PEERS, C, LANES), f32)],
        [pltpu.VMEM((8, C, LANES), f32), pltpu.SemaphoreType.DMA((PEERS // 8,))],
        exchange(sent), wa, wb, vmem_in=(1, 2), hbm_out=(1,),
    )
    sent, dpre = run_middle(
        exchange(sent), field, cotangent, pre, dact, kron, table, offset
    )
    sent, g = call(
        k_mix_back, "mix_back", [shape(PEERS * ROWS, LANES), shape(C, LANES)], [],
        exchange_rows(sent), wa, wb, vmem_in=(1, 2),
    )
    back = exchange_rows(sent)
    share = call(
        k_share, "share", pltpu.HBM((NB, 2 * C + 8, LANES), f32),
        [pltpu.VMEM((2 * C + 8, LANES), f32), pltpu.SemaphoreType.DMA((NB,))], back, u, g, hbm_out=(0,),
    )
    share = lax.all_to_all(share, "batch", 0, 0, tiled=True)
    grad_input = call(
        k_input, "input_grad", shape(C, XY, N, dtype=bf16),
        [CELLS_LOW, twice, CELLS, pltpu.SemaphoreType.DMA((STEPS,))],
        back, dpre, kron, table, offset, hbm_out=(0,),
    )
    spec, skip, b, inner, outer = call(
        k_shared, "shared",
        [shape(2, C, ML, 2, C), shape(C, C), shape(C), shape(C, C), shape(C, C)],
        [pltpu.VMEM((256, LANES), f32)] * 2, share,
    )
    spec = spec.transpose(0, 1, 4, 2, 3).reshape(2, C, C, 1, ML, 2)
    return (grad_input.reshape(1, C, XL, YL, N), spec, skip, b, inner, outer)


def solution(mesh):
    placed = (
        P("batch", None, "px", "py", None),
        P("batch", None, "px", "py", None),
        P(None, None, None, "py", "px", None),
        P(),
        P(),
        P(),
        P(),
    )
    return jax.shard_map(
        shards,
        mesh=mesh,
        in_specs=placed,
        out_specs=(
            P("batch", None, "px", "py", None),
            P(None, None, None, "py", "px", "batch"),
            P(),
            P(),
            P(),
            P(),
        ),
        check_vma=False,
    )
```
